256 devices in a mesh: dp: 4 (over x), seq: 64 (over y, z, core).
Axes of the slice: x: 4, y: 4, z: 8, core: 2. Of those that a mesh axis runs over, the one named last changes fastest.
Arguments:
- queries: float32 [4, 8192, 768], P('dp', 'seq'), may hold values from -6 to 6
- keys: float32 [4, 8192, 768], P('dp', 'seq'), may hold values from -6 to 6
- values: float32 [4, 8192, 768], P('dp', 'seq'), may hold values from -6 to 6
- out_grad: float32 [4, 8192, 768], P('dp', 'seq'), may hold values from -16 to 16
- out_weight: float32 [768, 768], P(('dp', 'seq')), may hold values from -0.21875 to 0.21875
- valid_tiles: int32 [4], P('dp'), may hold values from 2048 to 8192, as said below
- head_offsets: int32 [12], replicated, may hold values from 0 to 63
Outputs:
- query_grad: float32 [4, 8192, 768], P('dp', 'seq')
- key_grad: float32 [4, 8192, 768], P('dp', 'seq')
- value_grad: float32 [4, 8192, 768], P('dp', 'seq')
- weight_grad: float32 [768, 768], P(('dp', 'seq'))
The draws below stay inside these ranges and needn't reach their ends.
Inputs may be any that keep to these rules, and one draw needn't show every extreme that they name: The first valid_tiles[s] tiles of slide s are real, the rest padding.
All inputs are finite; a program needn't handle non-finite values.
Results may differ from the reference program's by a relative error of at most 0.0003.
Values sent between devices are 32-bit elements; how exact they have to be, the bound alone decides.
A program may use at most 128 MiB of HBM per device.

```python
import jax
import jax.numpy as jnp
from jax import lax

D = 768
HEADS = 12
HEAD_DIM = 64
SHORT_SEG = 512
SLIDES = 4
SPACING = 64
SEQ_LEN = 8192


def draw_queries(key, part):
    key = jax.random.fold_in(key, 11)
    return jax.random.truncated_normal(key, -4.0, 4.0, (SLIDES, SEQ_LEN, D), jnp.float32)


def draw_keys(key, part):
    key = jax.random.fold_in(key, 13)
    return jax.random.truncated_normal(key, -4.0, 4.0, (SLIDES, SEQ_LEN, D), jnp.float32)


def draw_valid_tiles(key, part):
    key = jax.random.fold_in(key, 23)
    lengths = jax.random.randint(key, (SLIDES,), SEQ_LEN // 4, SEQ_LEN + 1)
    full_slide = jax.random.randint(jax.random.fold_in(key, 1), (), 0, SLIDES)
    short_slide = (full_slide + 1 + jax.random.randint(jax.random.fold_in(key, 2), (), 0, SLIDES - 1)) % SLIDES
    slide_ids = jnp.arange(SLIDES)
    lengths = jnp.where(slide_ids == full_slide, SEQ_LEN, lengths)
    lengths = jnp.where(slide_ids == short_slide, SEQ_LEN // 4, lengths)
    return lengths.astype(jnp.int32)


def with_ends(entries, key, least, largest):
    index_at = [jax.random.randint(jax.random.fold_in(key, axis), (), 0, length) for axis, length in enumerate(entries.shape)]
    widest = entries.shape.index(max(entries.shape))
    beside = index_at[:widest] + [(index_at[widest] + 1) % entries.shape[widest]] + index_at[widest + 1:]
    return entries.at[tuple(index_at)].set(least).at[tuple(beside)].set(largest)


def spiked(array, stream_key, source, target, parts, factor):
    def block_of(axis_at):
        return (jnp.arange(array.shape[axis_at]) // (array.shape[axis_at] // parts)).reshape((-1,) + (1,) * (array.ndim - 1 - axis_at))

    near = jax.random.permutation(stream_key, parts)[block_of(target)]
    other_side = (block_of(target) + parts // 2) % parts
    return jnp.where((block_of(source) == near) | (block_of(source) == other_side), factor * array, array)


def shard_levels(rng, extent, split, least, top_value):
    gain, own = 1.0, jax.random.fold_in(rng, 6)
    for dim, parts in split:
        draws = jnp.exp(jax.random.uniform(jax.random.fold_in(own, dim), (parts,), jnp.float32, least / len(split), top_value / len(split)))
        gain = gain * jnp.repeat(draws, extent[dim] // parts).reshape([-1 if axis == dim else 1 for axis in range(len(extent))])
    return gain


def centred(key, shape, width, bound, split=(), held_as=jnp.bfloat16):
    result = width * jax.random.normal(key, shape, jnp.float32)
    if split:
        result = result * shard_levels(key, shape, split, -0.22, 0.18)
    return jnp.clip(result, -bound, bound).astype(held_as)


def noise_with(stream_key, shape, deviation, bound, cuts, heavy, kind=jnp.bfloat16):
    result = deviation * jax.random.normal(stream_key, shape, jnp.float32)
    if cuts:
        result = result * shard_levels(stream_key, shape, cuts, -0.22, 0.18)
    return jnp.clip(spiked(result, jax.random.fold_in(stream_key, 3), *heavy), -bound, bound).astype(kind)


def setup_inputs(seed: int = 0) -> dict:
    key_list = jax.random.split(jax.random.key(seed), 8)
    return {
        "queries": draw_queries(jax.random.fold_in(key_list[7], 71), 0),
        "keys": draw_keys(jax.random.fold_in(key_list[7], 71), 0),
        "values": centred(key_list[2], (SLIDES, SEQ_LEN, D), 1.0, 6.0, ((0, 4), (1, 64)), jnp.float32),
        "out_grad": noise_with(key_list[3], (SLIDES, SEQ_LEN, D), 1.0, 16.0, ((0, 4), (1, 64)), (1, 2, 64, 4.0), jnp.float32),
        "out_weight": centred(key_list[4], (D, D), D ** -0.5, 0.21875, ((0, 256),), jnp.float32),
        "valid_tiles": draw_valid_tiles(jax.random.fold_in(key_list[7], 71), 0),
        "head_offsets": with_ends(jax.random.randint(key_list[6], (HEADS,), 0, SPACING), jax.random.fold_in(key_list[6], 1), 0, SPACING - 1).astype(jnp.int32),
    }


PRECISE = lax.Precision.HIGHEST
MASKED = -1e+30

def contract(form, left, right):
    return jnp.einsum(form, left, right, precision=PRECISE)

def attend(queries, keys, values, valid_count, head_offsets):
    blocks = SEQ_LEN // SHORT_SEG
    groups = SEQ_LEN // SPACING
    score_scale_factor = HEAD_DIM ** (-0.5)
    query_blocks = queries.reshape(blocks, SHORT_SEG, HEADS, HEAD_DIM)
    key_blocks = keys.reshape(blocks, SHORT_SEG, HEADS, HEAD_DIM)
    value_blocks = values.reshape(blocks, SHORT_SEG, HEADS, HEAD_DIM)
    positions = jnp.arange(SEQ_LEN, dtype=jnp.int32)
    key_live = (positions < valid_count).reshape(blocks, SHORT_SEG)
    diagonal_keep = jnp.eye(SHORT_SEG, dtype=bool)[None]

    def block_scores(query_block, key_block, live_block):
        keep = live_block[None, None, :] | diagonal_keep
        return jnp.where(keep, contract('ihe,jhe->hij', query_block, key_block) * score_scale_factor, MASKED)

    def block_top(inputs):
        query_block, key_block, live_block = inputs
        return lax.optimization_barrier(jnp.max(block_scores(query_block, key_block, live_block), axis=2))
    local_maximum = lax.map(block_top, (lax.stop_gradient(query_blocks), lax.stop_gradient(key_blocks), key_live))
    local_maximum = local_maximum.transpose(1, 0, 2).reshape(HEADS, SEQ_LEN)
    picker = (jnp.arange(SPACING, dtype=jnp.int32)[None, :] == head_offsets[:, None]).astype(queries.dtype)

    def select_rows(source):
        return contract('grhe,hr->hge', source.reshape(groups, SPACING, HEADS, HEAD_DIM), picker)
    query_far = select_rows(queries)
    key_far = select_rows(keys)
    value_far = select_rows(values)
    far_pos = jnp.arange(groups, dtype=jnp.int32)[None, :] * SPACING + head_offsets[:, None]
    distant_score_rows = jnp.where((far_pos < valid_count)[:, None, :], contract('hge,hke->hgk', query_far, key_far) * score_scale_factor, MASKED)
    chosen = (positions % SPACING)[None, :] == head_offsets[:, None]
    far_top = lax.optimization_barrier(jnp.max(distant_score_rows, axis=2))
    spread_top = (far_top[:, :, None] * picker[:, None, :]).reshape(HEADS, SEQ_LEN)
    row_top = lax.stop_gradient(jnp.where(chosen, jnp.maximum(local_maximum, spread_top), local_maximum))
    block_row_top = row_top.reshape(HEADS, blocks, SHORT_SEG).transpose(1, 0, 2)

    def block_sums(inputs):
        query_block, key_block, value_block, live_block, top_block = inputs
        weight = jnp.exp(block_scores(query_block, key_block, live_block) - top_block[:, :, None])
        return (lax.optimization_barrier(jnp.sum(weight, axis=2)), contract('hij,jhe->ihe', weight, value_block))
    near_total_blocks, near_part = lax.map(block_sums, (query_blocks, key_blocks, value_blocks, key_live, block_row_top))
    local_total = near_total_blocks.transpose(1, 0, 2).reshape(HEADS, SEQ_LEN)
    near_part = near_part.reshape(SEQ_LEN, HEADS, HEAD_DIM)
    far_row_top = contract('hgr,hr->hg', row_top.reshape(HEADS, groups, SPACING), picker)
    distant_weight = jnp.exp(distant_score_rows - far_row_top[:, :, None])
    far_total = lax.optimization_barrier(jnp.sum(distant_weight, axis=2))
    row_total = local_total + (far_total[:, :, None] * picker[:, None, :]).reshape(HEADS, SEQ_LEN)
    far_part = contract('hgk,hke->hge', distant_weight, value_far)
    far_rows = contract('hge,hr->grhe', far_part, picker).reshape(SEQ_LEN, HEADS, HEAD_DIM)
    mixed_rows = (near_part + far_rows) / row_total.T[:, :, None]
    return mixed_rows.reshape(SEQ_LEN, D)

def reference(queries, keys, values, out_grad, out_weight, valid_tiles, head_offsets):
    positions = jnp.arange(SEQ_LEN, dtype=jnp.int32)

    def one_slide(inputs):
        slide_query, slide_key, slide_value, slide_grad, valid_count = inputs

        def layer_out(query_in, key_in, value_in, weight_in):
            mixed_rows = attend(query_in, key_in, value_in, valid_count, head_offsets)
            return jnp.dot(mixed_rows, weight_in.T, precision=PRECISE, preferred_element_type=jnp.float32)
        cotangent = jnp.where((positions < valid_count)[:, None], slide_grad, 0.0)
        unused_out, pull_back = jax.vjp(layer_out, slide_query, slide_key, slide_value, out_weight)
        return pull_back(cotangent)
    query_grad, key_grad, value_grad, weight_parts = lax.map(one_slide, (queries, keys, values, out_grad, valid_tiles))
    weight_grad = lax.optimization_barrier(jnp.sum(weight_parts, axis=0)) * SEQ_LEN ** (-0.5)
    return (query_grad, key_grad, value_grad, weight_grad)
```

```python
import jax
import jax.numpy as jnp
from jax import lax
from jax.experimental import pallas as pl
from jax.experimental.pallas import tpu as pltpu

F32 = jnp.float32
BF16 = jnp.bfloat16
MASKED = -1e30
MESH = pl.DeviceIdType.MESH

X, Y, Z = 4, 4, 8
ROWS = 128
SEATS = 4
SEG = ROWS * SEATS
SPACING = 64
SEGMENTS = 16
FAR = 128
WIDTH = 768
HEADS_HERE = 3
KEYS = SEG + FAR
G_CHUNKS = 2
SENDS = 96


def dot(left, right):
    return lax.dot_general(left, right, (((1,), (0,)), ((), ())), preferred_element_type=F32)


def dot_nt(left, right):
    return lax.dot_general(left, right, (((1,), (1,)), ((), ())), preferred_element_type=F32)


def flip(block):
    return pltpu.roll(block, 64, 1)


def low_lanes(block):
    return lax.broadcasted_iota(jnp.int32, block.shape, 1) < 64


def split(block):
    high = block.astype(BF16).astype(F32)
    return high, block - high


def pair(block, upper):
    high, low = split(block)
    if upper:
        return jnp.where(low_lanes(block), flip(high), low)
    return jnp.where(low_lanes(block), high, flip(low))


def twice(block, upper):
    if upper:
        return jnp.where(low_lanes(block), flip(block), block)
    return jnp.where(low_lanes(block), block, flip(block))


def unfold(packed):
    return jnp.concatenate([packed, flip(packed)], axis=0)


def fold_halves(block):
    return block + flip(block)


def kernel(
    q_in, k_in, v_in, g_in, w_in, valid_ref, offset_ref,
    dq_out, dk_out, dv_out, wg_out,
    q_own, k_own, v_own, q_send, k_send, v_send, q_seg, k_seg, v_seg, g_seg,
    w_seg, w_ring, w_all, w_hi, w_lo, far,
    q4, k4, v4, kt, vt, do4, do_t, attn_t, prob, prob_hi, prob_lo, ds_hi, ds_lo, g_hi, g_lo,
    far_part, far_y, far_sum, far_z, extra,
    wg_x, wg_xr, wg_y, wg_yr, wg_z, wg_zr, wg_q, wg_qr,
    dq_t, full_send, half_send, full_got, half_got,
    send_sem, recv_sem, local_sem,
):
    x = lax.axis_index("dp")
    s = lax.axis_index("seq")
    y = lax.div(s, 16)
    z = lax.rem(lax.div(s, 2), 8)
    c = lax.rem(s, 2)
    hz = lax.rem(z, 2)
    zz = lax.div(z, 2)
    t = lax.rem(s, 4)
    seg = lax.div(s, 4)
    xy = x * 4 + y

    def seat_of(d):
        core = c if d % 2 == 0 else 1 - c
        half = hz if d < 2 else 1 - hz
        return half * 2 + core

    def seg_peer(d):
        return (x, (y * 8 + zz * 2) * 2 + seat_of(d))

    def z_peer(j):
        return (x, (y * 8 + lax.rem(z + 2 * j, 8)) * 2 + c)

    def y_peer(j):
        return (x, (lax.rem(y + j, 4) * 8 + z) * 2 + c)

    def x_peer(j):
        return (lax.rem(x + j, 4), s)

    pushed = []

    def push(src, dst, device):
        i = len(pushed)
        copy = pltpu.make_async_remote_copy(
            src_ref=src, dst_ref=dst, send_sem=send_sem.at[i], recv_sem=recv_sem.at[i],
            device_id=device, device_id_type=MESH,
        )
        copy.start()
        pushed.append(copy)
        return copy

    def arrive(copies):
        for copy in copies:
            copy.wait_recv()

    loads = []
    for src, dst in (
        (w_in, w_seg.at[t]), (k_in, k_own), (v_in, v_own), (q_in, q_own), (g_in, g_seg.at[t]),
    ):
        copy = pltpu.make_async_copy(src, dst, local_sem.at[len(loads)])
        copy.start()
        loads.append(copy)

    barrier = pltpu.get_barrier_semaphore()
    for device in (
        [seg_peer(d) for d in (1, 2, 3)]
        + [z_peer(j) for j in (1, 2, 3)]
        + [y_peer(j) for j in (1, 2, 3)]
        + [x_peer(j) for j in (1, 2, 3)]
    ):
        pl.semaphore_signal(barrier, inc=1, device_id=device, device_id_type=MESH)
    pl.semaphore_wait(barrier, 12)

    loads[0].wait()
    w_moves = [push(w_seg.at[t], w_seg.at[t], seg_peer(d)) for d in (2, 3, 1)]

    def scatter_heads(own, send, seg_ref):
        for tt in range(SEATS):
            tile = 3 * (tt // 2) + 2 * (tt % 2)
            send[tt, 0:128, :] = own[:, tile * 128:(tile + 1) * 128]
            middle = 3 * (tt // 2) + 1
            top = own[0:64, middle * 128:(middle + 1) * 128]
            bottom = own[64:128, middle * 128:(middle + 1) * 128]
            if tt % 2 == 0:
                send[tt, 128:192, :] = jnp.where(low_lanes(top), top, flip(bottom))
            else:
                send[tt, 128:192, :] = jnp.where(low_lanes(top), flip(top), bottom)
        moves = [push(send.at[seat_of(d)], seg_ref.at[t], seg_peer(d)) for d in (2, 3, 1)]
        seg_ref[t] = send[t]
        return moves

    loads[1].wait()
    k_moves = scatter_heads(k_own, k_send, k_seg)
    loads[2].wait()
    v_moves = scatter_heads(v_own, v_send, v_seg)
    loads[3].wait()
    q_moves = scatter_heads(q_own, q_send, q_seg)
    loads[4].wait()
    g_rows = ROWS // G_CHUNKS
    g_across, g_beside = [], []
    for n in range(G_CHUNKS):
        part = g_seg.at[t, pl.ds(n * g_rows, g_rows)]
        g_across.append(push(part, part, seg_peer(2)))
    for n in range(G_CHUNKS):
        part = g_seg.at[t, pl.ds(n * g_rows, g_rows)]
        g_beside.append(push(part, part, seg_peer(1)))

    arrive(w_moves)
    full_tile = pl.multiple_of((3 * hz + 2 * c) * 128, 128)
    middle_tile = pl.multiple_of((3 * hz + 1) * 128, 128)
    for tt in range(SEATS):
        w_ring[zz, 3 * tt:3 * tt + 3, 0:128] = w_seg[tt, :, pl.ds(full_tile, 128)]
        middle = w_seg[tt, :, pl.ds(middle_tile, 128)]
        w_ring[zz, 3 * tt:3 * tt + 3, 128:256] = jnp.where(c == 1, flip(middle), middle)
    arrive([push(w_ring.at[zz], w_ring.at[zz], z_peer(j)) for j in (1, 2, 3)])
    for j in range(4):
        w_all[xy, 12 * j:12 * j + 12, :] = w_ring[j]
    arrive([push(w_all.at[xy], w_all.at[xy], y_peer(j)) for j in (1, 2, 3)])
    wx_moves = [
        push(w_all.at[pl.ds(x * 4, 4)], w_all.at[pl.ds(x * 4, 4)], x_peer(j)) for j in (1, 2, 3)
    ]

    arrive(k_moves)
    arrive(v_moves)
    first_head = 6 * hz + 4 * c
    heads = [first_head, first_head + 1, 6 * hz + 2 + c]
    offsets = [offset_ref[head] for head in heads]

    def long_rows(seg_ref, h):
        rows = []
        for r in range(8):
            if h < 2:
                rows.append(seg_ref[r // 2, pl.ds((r % 2) * 64 + offsets[h], 1), :])
            else:
                row = seg_ref[r // 2, pl.ds(128 + offsets[h], 1), :]
                rows.append(row if r % 2 == 0 else flip(row))
        return jnp.concatenate(rows, axis=0)

    for h in range(HEADS_HERE):
        key_rows, value_rows = long_rows(k_seg, h), long_rows(v_seg, h)
        low = low_lanes(key_rows)
        if h == 1:
            block = jnp.where(low, flip(key_rows), value_rows)
        else:
            block = jnp.where(low, key_rows, flip(value_rows))
        far[seg, 8 * h:8 * h + 8, :] = block
    far_moves = [push(far.at[seg], far.at[seg], z_peer(j)) for j in (1, 2, 3)]

    def head_blocks(seg_ref, tt):
        full = seg_ref[tt, 0:128, :]
        return ((0, full, False), (1, full, True), (2, unfold(seg_ref[tt, 128:192, :]), False))

    def as_keys(h, rows, block, upper, four, transposed):
        high, low = split(block)
        four[h, rows, 0:128] = twice(high, upper).astype(BF16)
        four[h, rows, 128:256] = twice(low, upper).astype(BF16)
        transposed[h, :, rows] = pair(block, upper).T.astype(BF16)

    for tt in range(SEATS):
        rows = slice(tt * 128, (tt + 1) * 128)
        for h, block, upper in head_blocks(k_seg, tt):
            as_keys(h, rows, block, upper, k4, kt)
        for h, block, upper in head_blocks(v_seg, tt):
            as_keys(h, rows, block, upper, v4, vt)

    arrive(far_moves)
    far_moves = [
        push(far.at[pl.ds(y * 4, 4)], far.at[pl.ds(y * 4, 4)], y_peer(j)) for j in (1, 2, 3)
    ]

    arrive(q_moves)
    for tt in range(SEATS):
        rows = slice(tt * 128, (tt + 1) * 128)
        for h, block, upper in head_blocks(q_seg, tt):
            both = pair(block * 0.125, upper).astype(BF16)
            q4[h, rows, 0:128] = both
            q4[h, rows, 128:256] = both

    arrive(far_moves)
    for h in range(HEADS_HERE):
        block = far[:, 8 * h:8 * h + 8, :].reshape(FAR, 128)
        as_keys(h, slice(SEG, KEYS), block, False, k4, kt)
        as_keys(h, slice(SEG, KEYS), block, True, v4, vt)

    valid = valid_ref[0]
    key_row = lax.broadcasted_iota(jnp.int32, (128, 256), 0)
    query_lane = lax.broadcasted_iota(jnp.int32, (128, 256), 1)

    def forward(h, carry):
        offset = offset_ref[jnp.where(h == 2, heads[2], first_head + h)]
        for qb in range(2):
            lanes = slice(qb * 256, (qb + 1) * 256)
            queries = q4[h, lanes, :]
            top = None
            for kb in range(5):
                rows = slice(kb * 128, (kb + 1) * 128)
                scores = dot_nt(k4[h, rows, :], queries)
                if kb < 4:
                    keep = (seg * SEG + kb * 128 + key_row < valid) | (
                        kb * 128 + key_row == qb * 256 + query_lane
                    )
                else:
                    keep = (key_row * SPACING + offset < valid) & (
                        lax.rem(query_lane, SPACING) == offset
                    )
                scores = jnp.where(keep, scores, MASKED)
                prob[h, rows, lanes] = scores
                here = jnp.max(scores, axis=0, keepdims=True)
                top = here if top is None else jnp.maximum(top, here)
            total = None
            for kb in range(5):
                rows = slice(kb * 128, (kb + 1) * 128)
                weight = jnp.exp(prob[h, rows, lanes] - top)
                prob[h, rows, lanes] = weight
                here = jnp.sum(weight, axis=0, keepdims=True)
                total = here if total is None else total + here
            scale = 1.0 / total
            for kb in range(5):
                rows = slice(kb * 128, (kb + 1) * 128)
                p = prob[h, rows, lanes] * scale
                prob[h, rows, lanes] = p
                high = p.astype(BF16)
                prob_hi[h, rows, lanes] = high
                prob_lo[h, rows, lanes] = (p - high.astype(F32)).astype(BF16)
            out = dot(vt[h], prob_hi[h, :, lanes]) + dot(vt[h], prob_lo[h, :, lanes])
            attn_t[h, :, lanes] = out[0:64] + out[64:128]
        return carry

    lax.fori_loop(0, HEADS_HERE, forward, 0)

    arrive(wx_moves)
    w_cols = w_all[...].reshape(WIDTH, 256)
    high = w_cols.astype(BF16)
    w_hi[...] = high
    w_lo[...] = (w_cols - high.astype(F32)).astype(BF16)
    forwarded = []
    for n in range(G_CHUNKS):
        g_across[n].wait_recv()
        part = g_seg.at[seat_of(2), pl.ds(n * g_rows, g_rows)]
        forwarded.append(push(part, part, seg_peer(1)))
    arrive(g_beside)
    arrive(forwarded)
    tile_row = lax.broadcasted_iota(jnp.int32, (ROWS, WIDTH), 0)
    for tt in range(SEATS):
        rows = slice(tt * 128, (tt + 1) * 128)
        grad = jnp.where(seg * SEG + tt * 128 + tile_row < valid, g_seg[tt], 0.0)
        high = grad.astype(BF16)
        low = (grad - high.astype(F32)).astype(BF16)
        g_hi[rows, :] = high
        g_lo[rows, :] = low
        out = dot(high, w_hi[...]) + dot(low, w_hi[...]) + dot(high, w_lo[...])
        full, middle = out[:, 0:128], out[:, 128:256]
        for h, block, upper in ((0, full, False), (1, full, True), (2, middle, False)):
            both = pair(block, upper).astype(BF16)
            do4[h, rows, 0:128] = both
            do4[h, rows, 128:256] = both
        turned = full.T
        do_t[0, :, rows] = turned[0:64]
        do_t[1, :, rows] = turned[64:128]
        do_t[2, :, rows] = middle.T[0:64]

    for h in range(HEADS_HERE):
        if h == 1:
            continue
        attn = attn_t[0:2].reshape(128, SEG) if h == 0 else attn_t[2]
        high = attn.astype(BF16)
        low = (attn - high.astype(F32)).astype(BF16)
        turned = dot(high, g_hi[...]) + dot(low, g_hi[...]) + dot(high, g_lo[...])
        if h == 2:
            turned = jnp.concatenate([turned, turned], axis=0)
        lanes = slice(0, 128) if h == 0 else slice(128, 256)
        for xx in range(X):
            wg_x[xx, :, lanes] = turned[:, xx * 192:(xx + 1) * 192].T
    wg_moves = [
        push(wg_x.at[lax.rem(x + j, 4)], wg_xr.at[j - 1], x_peer(j)) for j in (1, 2, 3)
    ]

    def score_grad(h, kb):
        rows = slice(kb * 128, (kb + 1) * 128)
        delta = jnp.sum(attn_t[h] * do_t[h], axis=0, keepdims=True)
        d_prob = dot_nt(v4[h, rows, :], do4[h])
        ds = prob[h, rows, :] * (d_prob - delta)
        high = ds.astype(BF16)
        ds_hi[h, rows, :] = high
        ds_lo[h, rows, :] = (ds - high.astype(F32)).astype(BF16)

    def key_value_grad(h, rows):
        queries, grads = q4[h, :, 0:128], do4[h, :, 0:128]
        d_key = dot(ds_hi[h, rows, :], queries) + dot(ds_lo[h, rows, :], queries)
        d_value = dot(prob_hi[h, rows, :], grads) + dot(prob_lo[h, rows, :], grads)
        return fold_halves(d_key), fold_halves(d_value)

    for h in range(HEADS_HERE):
        score_grad(h, 4)
        d_key, d_value = key_value_grad(h, slice(SEG, KEYS))
        block = jnp.where(low_lanes(d_key), d_key, d_value)
        far_part[:, 8 * h:8 * h + 8, :] = block.reshape(SEGMENTS, 8, 128)
    far_moves = [
        push(far_part.at[pl.ds(lax.rem(y + j, 4) * 4, 4)], far_y.at[j - 1], y_peer(j))
        for j in (1, 2, 3)
    ]

    def near(h):
        for kb in range(4):
            score_grad(h, kb)
        turned = dot(kt[h], ds_hi[h]) + dot(kt[h], ds_lo[h])
        dq_t[h] = (turned[0:64] + turned[64:128]) * 0.125
        return key_value_grad(h, slice(0, SEG))

    d_key, d_value = near(2)
    for tt in range(SEATS):
        block = dq_t[2, :, tt * 128:(tt + 1) * 128]
        block = jnp.concatenate([block, block], axis=0).T
        low = low_lanes(block[0:64])
        half_send[0, tt] = jnp.where(low, block[0:64], block[64:128])
        for n, part in ((1, d_key), (2, d_value)):
            top, bottom = part[tt * 128:tt * 128 + 64], part[tt * 128 + 64:tt * 128 + 128]
            half_send[n, tt] = jnp.where(low, top, bottom)
    out_moves = [
        push(half_send.at[:, seat_of(d)], half_got.at[:, t], seg_peer(d)) for d in (2, 3, 1)
    ]
    for n in range(3):
        half_got[n, t] = half_send[n, t]

    arrive(far_moves)
    far_sum[...] = far_part[pl.ds(y * 4, 4)] + far_y[0] + far_y[1] + far_y[2]
    far_moves = [push(far_sum.at[lax.rem(zz + j, 4)], far_z.at[j - 1], z_peer(j)) for j in (1, 2, 3)]

    low_key, low_value = near(0)
    high_key, high_value = near(1)
    lane_low = low_lanes(low_key)
    d_key = jnp.where(lane_low, low_key, high_key)
    d_value = jnp.where(lane_low, low_value, high_value)
    for tt in range(SEATS):
        rows = slice(tt * 128, (tt + 1) * 128)
        full_send[0, tt] = dq_t[0:2, :, rows].reshape(128, 128).T
        full_send[1, tt] = d_key[rows]
        full_send[2, tt] = d_value[rows]
    out_moves += [
        push(full_send.at[:, seat_of(d)], full_got.at[:, t], seg_peer(d)) for d in (2, 3, 1)
    ]
    for n in range(3):
        full_got[n, t] = full_send[n, t]

    arrive(far_moves)
    extra[t] = far_sum[zz] + far_z[0] + far_z[1] + far_z[2]
    extra_moves = [push(extra.at[t], extra.at[t], seg_peer(d)) for d in (2, 3, 1)]

    arrive(wg_moves)
    wg_sum = wg_x[x] + wg_xr[0] + wg_xr[1] + wg_xr[2]
    for yy in range(Y):
        wg_y[yy] = wg_sum[yy * 48:(yy + 1) * 48]
    arrive([push(wg_y.at[lax.rem(y + j, 4)], wg_yr.at[j - 1], y_peer(j)) for j in (1, 2, 3)])
    wg_sum = wg_y[y] + wg_yr[0] + wg_yr[1] + wg_yr[2]
    for j in range(4):
        wg_z[j] = wg_sum[j * 12:(j + 1) * 12]
    arrive([push(wg_z.at[lax.rem(zz + j, 4)], wg_zr.at[j - 1], z_peer(j)) for j in (1, 2, 3)])
    wg_sum = (wg_z[zz] + wg_zr[0] + wg_zr[1] + wg_zr[2]) * (8192.0 ** -0.5)
    for tt in range(SEATS):
        wg_q[tt] = wg_sum[tt * 3:(tt + 1) * 3]
    wg_moves = [push(wg_q.at[seat_of(d)], wg_qr.at[t], seg_peer(d)) for d in (2, 3, 1)]
    wg_qr[t] = wg_q[t]

    arrive(extra_moves)
    arrive(out_moves)
    row64 = lax.broadcasted_iota(jnp.int32, (64, 128), 0)
    low64 = lax.broadcasted_iota(jnp.int32, (64, 128), 1) < 64
    outs = (dq_out, dk_out, dv_out)

    def with_extra(n, r, tt, h, upper, block):
        if n == 0:
            return block
        head = 6 * (tt // 2) + (4 * (tt % 2) + h if h < 2 else 2 + tt % 2)
        row = extra[tt, pl.ds(8 * h + 2 * t + r, 1), :]
        if (n == 2) != upper:
            row = flip(row)
        keep = (row64 == offset_ref[head]) & (low64 != upper)
        return block + jnp.where(keep, jnp.broadcast_to(row, (64, 128)), 0.0)

    for n in range(3):
        for tt in range(SEATS):
            tile = 3 * (tt // 2) + 2 * (tt % 2)
            for r in range(2):
                block = full_got[n, tt, r * 64:(r + 1) * 64, :]
                block = with_extra(n, r, tt, 0, False, block)
                block = with_extra(n, r, tt, 1, True, block)
                outs[n][r * 64:(r + 1) * 64, tile * 128:(tile + 1) * 128] = block
        for half in range(2):
            tile = 3 * half + 1
            even, odd = half_got[n, 2 * half], half_got[n, 2 * half + 1]
            for r in range(2):
                if r == 0:
                    block = jnp.where(low64, even, flip(odd))
                else:
                    block = jnp.where(low64, flip(even), odd)
                block = with_extra(n, r, 2 * half, 2, False, block)
                block = with_extra(n, r, 2 * half + 1, 2, True, block)
                outs[n][r * 64:(r + 1) * 64, tile * 128:(tile + 1) * 128] = block

    arrive(wg_moves)
    for tt in range(SEATS):
        tile = 3 * (tt // 2) + 2 * (tt % 2)
        wg_out[:, tile * 128:(tile + 1) * 128] = wg_qr[tt, :, 0:128]
    for half in range(2):
        tile = 3 * half + 1
        even, odd = wg_qr[2 * half, :, 128:256], wg_qr[2 * half + 1, :, 128:256]
        wg_out[:, tile * 128:(tile + 1) * 128] = jnp.where(low_lanes(even), even, odd)

    for copy in pushed:
        copy.wait_send()


def on_device(queries, keys, values, out_grad, out_weight, valid_tiles, head_offsets):
    def block(*shape):
        return pltpu.VMEM(shape, F32)

    def half(*shape):
        return pltpu.VMEM(shape, BF16)

    scratch = [
        block(ROWS, WIDTH), block(ROWS, WIDTH), block(ROWS, WIDTH),
        block(4, 192, 128), block(4, 192, 128), block(4, 192, 128),
        block(4, 192, 128), block(4, 192, 128), block(4, 192, 128),
        block(4, ROWS, WIDTH),
        block(4, 3, WIDTH), block(4, 12, 256), block(16, 48, 256),
        half(WIDTH, 256), half(WIDTH, 256),
        block(SEGMENTS, 24, 128),
        half(3, SEG, 256), half(3, KEYS, 256), half(3, KEYS, 256),
        half(3, 128, KEYS), half(3, 128, KEYS),
        half(3, SEG, 256), block(3, 64, SEG), block(3, 64, SEG),
        block(3, KEYS, SEG), half(3, KEYS, SEG), half(3, KEYS, SEG),
        half(3, KEYS, SEG), half(3, KEYS, SEG),
        half(SEG, WIDTH), half(SEG, WIDTH),
        block(SEGMENTS, 24, 128), block(3, 4, 24, 128), block(4, 24, 128), block(3, 24, 128),
        block(4, 24, 128),
        block(4, 192, 256), block(3, 192, 256), block(4, 48, 256), block(3, 48, 256),
        block(4, 12, 256), block(3, 12, 256), block(4, 3, 256), block(4, 3, 256),
        block(3, 64, SEG),
        block(3, 4, 128, 128), block(3, 4, 64, 128), block(3, 4, 128, 128), block(3, 4, 64, 128),
        pltpu.SemaphoreType.DMA((SENDS,)), pltpu.SemaphoreType.DMA((SENDS,)),
        pltpu.SemaphoreType.DMA((5,)),
    ]
    whole = pl.BlockSpec(memory_space=pl.ANY)
    scalars = pl.BlockSpec(memory_space=pltpu.SMEM)
    vmem = pl.BlockSpec(memory_space=pltpu.VMEM)
    rows = jax.ShapeDtypeStruct((ROWS, WIDTH), F32)
    d_query, d_key, d_value, d_weight = pl.pallas_call(
        kernel,
        out_shape=(rows, rows, rows, jax.ShapeDtypeStruct((3, WIDTH), F32)),
        in_specs=[whole] * 5 + [scalars] * 2,
        out_specs=(vmem,) * 4,
        scratch_shapes=scratch,
        compiler_params=pltpu.CompilerParams(
            collective_id=0, has_side_effects=True, vmem_limit_bytes=52 * 1024 * 1024
        ),
        cost_estimate=pl.CostEstimate(
            flops=4_000_000_000, bytes_accessed=4_000_000, transcendentals=1_000_000
        ),
        name="dilated_backward",
    )(queries[0], keys[0], values[0], out_grad[0], out_weight, valid_tiles, head_offsets)
    return d_query[None], d_key[None], d_value[None], d_weight


def solution(mesh):
    from jax.sharding import PartitionSpec as P

    tiles = P("dp", "seq", None)
    weight = P(("dp", "seq"), None)
    return jax.shard_map(
        on_device,
        mesh=mesh,
        in_specs=(tiles, tiles, tiles, tiles, weight, P("dp"), P()),
        out_specs=(tiles, tiles, tiles, weight),
        check_vma=False,
    )
```

```python
import jax
import jax.numpy as jnp
from jax import lax
from jax.experimental import pallas as pl
from jax.experimental.pallas import tpu as pltpu

F32 = jnp.float32
BF16 = jnp.bfloat16
MASKED = -1e30
MESH = pl.DeviceIdType.MESH

X = 4
ROWS = 128
SEATS = 4
SEG = ROWS * SEATS
SPACING = 64
FAR = 128
WIDTH = 768
HEADS_HERE = 3
KEYS = SEG + FAR
G_CHUNKS = 4
G_EARLY = 2
FAR_FIRST = (8, 7, 9, 6, 10, 5, 11, 4, 12, 3, 13, 2, 14, 1, 15)
SENDS = 128


def dot(left, right):
    return lax.dot_general(left, right, (((1,), (0,)), ((), ())), preferred_element_type=F32)


def dot_nt(left, right):
    return lax.dot_general(left, right, (((1,), (1,)), ((), ())), preferred_element_type=F32)


def flip(block):
    return pltpu.roll(block, 64, 1)


def low_lanes(block):
    return lax.broadcasted_iota(jnp.int32, block.shape, 1) < 64


def split(block):
    high = block.astype(BF16).astype(F32)
    return high, block - high


def pair(block, upper):
    high, low = split(block)
    if upper:
        return jnp.where(low_lanes(block), flip(high), low)
    return jnp.where(low_lanes(block), high, flip(low))


def twice(block, upper):
    if upper:
        return jnp.where(low_lanes(block), flip(block), block)
    return jnp.where(low_lanes(block), block, flip(block))


def unfold(packed):
    return jnp.concatenate([packed, flip(packed)], axis=0)


def fold_halves(block):
    return block + flip(block)


def lanes_of(tile):
    return slice(tile * 128, (tile + 1) * 128)


def full_tile(seat):
    return 3 * (seat // 2) + 2 * (seat % 2)


def middle_tile(seat):
    return 3 * (seat // 2) + 1


def head_of(seat, h):
    return 6 * (seat // 2) + (2 + seat % 2 if h == 2 else 4 * (seat % 2) + h)


def kernel(
    q_in, k_in, v_in, g_in, w_in, valid_ref, offset_ref,
    full_got, half_got, last_got,
    q_own, k_own, v_own, w_own, half_in, half_seg, full_in, full_seg, g_seg,
    note, note_got, w_full, w_mid, w_hi, w_lo, far,
    q4, k4, v4, kt, vt, do4, do_t, attn_t, prob, prob_hi, prob_lo, ds_hi, ds_lo, g_hi, g_lo,
    far_part, far_got,
    wg_full, wg_full_1, wg_full_sum, wg_full_2, wg_mid, wg_mid_y, wg_mid_sum, wg_mid_x,
    last, dq_t, full_send, half_send,
    send_sem, recv_sem, local_sem,
):
    x = lax.axis_index("dp")
    s = lax.axis_index("seq")
    y = lax.div(s, 16)
    m = lax.rem(s, 16)
    z = lax.div(m, 2)
    c = lax.rem(s, 2)
    hz = lax.rem(z, 2)
    zz = lax.div(z, 2)
    t = lax.rem(s, 4)
    seg = lax.div(s, 4)

    def seat_of(d):
        core = c if d % 2 == 0 else 1 - c
        half = hz if d < 2 else 1 - hz
        return half * 2 + core

    def seg_peer(d):
        return (x, seg * 4 + seat_of(d))

    def ring_place(j):
        return lax.rem(m + j, 16)

    def ring_peer(j):
        return (x, y * 16 + ring_place(j))

    def y_place(j):
        return lax.rem(y + j, 4)

    def y_peer(j):
        return (x, y_place(j) * 16 + m)

    def x_place(j):
        return lax.rem(x + j, 4)

    def x_peer(j):
        return (x_place(j), s)

    pushed = []

    def push(src, dst, device):
        i = len(pushed)
        copy = pltpu.make_async_remote_copy(
            src_ref=src, dst_ref=dst, send_sem=send_sem.at[i], recv_sem=recv_sem.at[i],
            device_id=device, device_id_type=MESH,
        )
        copy.start()
        pushed.append(copy)
        return copy

    def arrive(copies):
        for copy in copies:
            copy.wait_recv()

    barrier = pltpu.get_barrier_semaphore()
    for device in (
        [ring_peer(j) for j in range(1, 16)]
        + [y_peer(j) for j in (1, 2, 3)]
        + [x_peer(j) for j in (1, 2, 3)]
    ):
        pl.semaphore_signal(barrier, inc=1, device_id=device, device_id_type=MESH)

    loads = []
    for src, dst in (
        (g_in, g_seg.at[t]), (k_in, k_own), (v_in, v_own), (w_in, w_own), (q_in, q_own),
    ):
        copy = pltpu.make_async_copy(src, dst, local_sem.at[len(loads)])
        copy.start()
        loads.append(copy)

    owns = (q_own, k_own, v_own)

    def deal(n):
        for tt in range(SEATS):
            full_in[tt, n] = owns[n][:, lanes_of(full_tile(tt))]
            top = owns[n][0:64, lanes_of(middle_tile(tt))]
            bottom = owns[n][64:128, lanes_of(middle_tile(tt))]
            if tt % 2 == 0:
                half_in[tt, n] = jnp.where(low_lanes(top), top, flip(bottom))
            else:
                half_in[tt, n] = jnp.where(low_lanes(top), flip(top), bottom)

    g_rows = ROWS // G_CHUNKS

    def g_part(seat, n):
        return g_seg.at[seat, pl.ds(n * g_rows, g_rows)]

    loads[0].wait()
    pl.semaphore_wait(barrier, 21)
    g_across = [push(g_part(t, n), g_part(t, n), seg_peer(2)) for n in range(G_EARLY)]

    loads[1].wait()
    deal(1)
    loads[2].wait()
    deal(2)

    def long_rows(tt, h, n):
        offset = offset_ref[head_of(tt, h)]
        if h == 2:
            row = half_in[tt, n, pl.ds(offset, 1), :]
            return jnp.concatenate([row, flip(row)], axis=0)
        return jnp.concatenate(
            [full_in[tt, n, pl.ds(r * 64 + offset, 1), :] for r in range(2)], axis=0
        )

    loads[3].wait()
    for tt in range(SEATS):
        note[tt, 0:3, :] = w_own[:, lanes_of(full_tile(tt))]
        note[tt, 3:6, :] = w_own[:, lanes_of(middle_tile(tt))]
        for h in range(HEADS_HERE):
            key_rows, value_rows = long_rows(tt, h, 1), long_rows(tt, h, 2)
            low = low_lanes(key_rows)
            if h == 1:
                rows = jnp.where(low, flip(key_rows), value_rows)
            else:
                rows = jnp.where(low, key_rows, flip(value_rows))
            note[tt, 6 + 2 * h:8 + 2 * h, :] = rows

    notes = [
        push(note.at[lax.rem(ring_place(j), 4)], note_got.at[m], ring_peer(j)) for j in FAR_FIRST
    ]
    g_across += [
        push(g_part(t, n), g_part(t, n), seg_peer(2)) for n in range(G_EARLY, G_CHUNKS)
    ]
    g_beside = [push(g_seg.at[t], g_seg.at[t], seg_peer(1))]
    note_got[m] = note[t]

    loads[4].wait()
    deal(0)
    half_seg[t] = half_in[t]
    full_seg[t] = full_in[t]

    arrive(notes)
    for mm in range(16):
        w_full[x, y, 3 * mm:3 * mm + 3, :] = note_got[mm, 0:3, :]
        w_mid[x, y, 3 * mm:3 * mm + 3, :] = note_got[mm, 3:6, :]
        for h in range(HEADS_HERE):
            far[y, h, 2 * mm:2 * mm + 2, :] = note_got[mm, 6 + 2 * h:8 + 2 * h, :]
    w_moves = [push(w_full.at[x, y], w_full.at[x, y], y_peer(j)) for j in (1, 3, 2)]
    w_moves += [push(w_mid.at[x, y], w_mid.at[x, y], x_peer(j)) for j in (1, 3, 2)]
    far_moves = [push(far.at[y], far.at[y], y_peer(j)) for j in (1, 3, 2)]
    half_moves = [push(half_in.at[seat_of(d)], half_seg.at[t], seg_peer(d)) for d in (2, 3, 1)]
    arrive(w_moves)
    w_moves = [push(w_full.at[x], w_full.at[x], x_peer(j)) for j in (1, 3, 2)]
    w_moves += [push(w_mid.at[:, y], w_mid.at[:, y], y_peer(j)) for j in (1, 3, 2)]
    arrive(far_moves)

    def as_keys(h, rows, block, upper, four, transposed):
        high, low = split(block)
        four[h, rows, 0:128] = twice(high, upper).astype(BF16)
        four[h, rows, 128:256] = twice(low, upper).astype(BF16)
        transposed[h, :, rows] = pair(block, upper).T.astype(BF16)

    for h in range(HEADS_HERE):
        block = far[:, h].reshape(FAR, 128)
        as_keys(h, slice(SEG, KEYS), block, False, k4, kt)
        as_keys(h, slice(SEG, KEYS), block, True, v4, vt)

    valid = valid_ref[0]
    tile_row = lax.broadcasted_iota(jnp.int32, (ROWS, WIDTH), 0)

    def take_grad(seat):
        rows = pl.ds(pl.multiple_of(seat * ROWS, ROWS), ROWS)
        grad = jnp.where(seg * SEG + seat * ROWS + tile_row < valid, g_seg[seat], 0.0)
        high = grad.astype(BF16)
        g_hi[rows, :] = high
        g_lo[rows, :] = (grad - high.astype(F32)).astype(BF16)

    take_grad(t)
    arrive(g_beside)
    take_grad(seat_of(1))
    g_forwarded = []
    for n in range(G_CHUNKS):
        g_across[n].wait_recv()
        g_forwarded.append(push(g_part(seat_of(2), n), g_part(seat_of(2), n), seg_peer(1)))
    full_moves = [
        push(full_in.at[seat_of(d), pl.ds(0, 2)], full_seg.at[t, pl.ds(0, 2)], seg_peer(d))
        for d in (2, 3, 1)
    ]
    full_value_moves = [
        push(full_in.at[seat_of(d), 2], full_seg.at[t, 2], seg_peer(d)) for d in (2, 3, 1)
    ]
    take_grad(seat_of(2))

    arrive(w_moves)
    for tile, ref in ((0, w_full), (1, w_mid)):
        columns = ref[...].reshape(WIDTH, 128)
        if tile == 1:
            columns = jnp.where(c == 1, flip(columns), columns)
        high = columns.astype(BF16)
        w_hi[:, lanes_of(tile)] = high
        w_lo[:, lanes_of(tile)] = (columns - high.astype(F32)).astype(BF16)

    arrive(g_forwarded)
    take_grad(seat_of(3))
    for tt in range(SEATS):
        rows = slice(tt * 128, (tt + 1) * 128)
        high, low = g_hi[rows, :], g_lo[rows, :]
        out = dot(high, w_hi[...]) + dot(low, w_hi[...]) + dot(high, w_lo[...])
        full, middle = out[:, 0:128], out[:, 128:256]
        for h, block, upper in ((0, full, False), (1, full, True), (2, middle, False)):
            both = pair(block, upper).astype(BF16)
            do4[h, rows, 0:128] = both
            do4[h, rows, 128:256] = both
        turned = full.T
        do_t[0, :, rows] = turned[0:64]
        do_t[1, :, rows] = turned[64:128]
        do_t[2, :, rows] = middle.T[0:64]

    def as_queries(h, rows, block, upper):
        both = pair(block * 0.125, upper).astype(BF16)
        q4[h, rows, 0:128] = both
        q4[h, rows, 128:256] = both

    key_row = lax.broadcasted_iota(jnp.int32, (128, 256), 0)
    query_lane = lax.broadcasted_iota(jnp.int32, (128, 256), 1)

    def weights(h):
        head = 6 * hz + jnp.where(h == 2, 2 + c, 4 * c + h)
        offset = offset_ref[head]
        for qb in range(2):
            lanes = slice(qb * 256, (qb + 1) * 256)
            queries = q4[h, lanes, :]
            top = None
            for kb in range(5):
                rows = slice(kb * 128, (kb + 1) * 128)
                scores = dot_nt(k4[h, rows, :], queries)
                if kb < 4:
                    keep = (seg * SEG + kb * 128 + key_row < valid) | (
                        kb * 128 + key_row == qb * 256 + query_lane
                    )
                else:
                    keep = (key_row * SPACING + offset < valid) & (
                        lax.rem(query_lane, SPACING) == offset
                    )
                scores = jnp.where(keep, scores, MASKED)
                prob[h, rows, lanes] = scores
                here = jnp.max(scores, axis=0, keepdims=True)
                top = here if top is None else jnp.maximum(top, here)
            total = None
            for kb in range(5):
                rows = slice(kb * 128, (kb + 1) * 128)
                weight = jnp.exp(prob[h, rows, lanes] - top)
                prob[h, rows, lanes] = weight
                here = jnp.sum(weight, axis=0, keepdims=True)
                total = here if total is None else total + here
            scale = 1.0 / total
            for kb in range(5):
                rows = slice(kb * 128, (kb + 1) * 128)
                p = prob[h, rows, lanes] * scale
                prob[h, rows, lanes] = p
                high = p.astype(BF16)
                prob_hi[h, rows, lanes] = high
                prob_lo[h, rows, lanes] = (p - high.astype(F32)).astype(BF16)

    def attention(h):
        for qb in range(2):
            lanes = slice(qb * 256, (qb + 1) * 256)
            out = dot(vt[h], prob_hi[h, :, lanes]) + dot(vt[h], prob_lo[h, :, lanes])
            attn_t[h, :, lanes] = out[0:64] + out[64:128]

    def value_grad(h):
        grads = do4[h, :, 0:128]
        return fold_halves(dot(prob_hi[h], grads) + dot(prob_lo[h], grads))

    def key_grad(h):
        queries = q4[h, :, 0:128]
        return fold_halves(dot(ds_hi[h], queries) + dot(ds_lo[h], queries))

    def score_grad(h):
        for qb in range(2):
            lanes = slice(qb * 256, (qb + 1) * 256)
            delta = jnp.sum(attn_t[h, :, lanes] * do_t[h, :, lanes], axis=0, keepdims=True)
            for kb in range(5):
                rows = slice(kb * 128, (kb + 1) * 128)
                d_prob = dot_nt(v4[h, rows, :], do4[h, lanes, :])
                ds = prob[h, rows, lanes] * (d_prob - delta)
                high = ds.astype(BF16)
                ds_hi[h, rows, lanes] = high
                ds_lo[h, rows, lanes] = (ds - high.astype(F32)).astype(BF16)

    def query_grad(h):
        turned = dot(kt[h], ds_hi[h]) + dot(kt[h], ds_lo[h])
        dq_t[h] = (turned[0:64] + turned[64:128]) * 0.125

    def weight_grad(attn):
        high = attn.astype(BF16)
        low = (attn - high.astype(F32)).astype(BF16)
        return dot(high, g_hi[...]) + dot(low, g_hi[...]) + dot(high, g_lo[...])

    def far_grad(h, d_key, d_value):
        d_key, d_value = d_key[SEG:KEYS], d_value[SEG:KEYS]
        block = jnp.where(low_lanes(d_key), d_key, d_value)
        far_part[:, h] = block.reshape(4, 32, 128)

    arrive(half_moves)
    for tt in range(SEATS):
        rows = slice(tt * 128, (tt + 1) * 128)
        as_queries(2, rows, unfold(half_seg[tt, 0]), False)
        as_keys(2, rows, unfold(half_seg[tt, 1]), False, k4, kt)
        as_keys(2, rows, unfold(half_seg[tt, 2]), False, v4, vt)
    weights(2)
    attention(2)
    turned = weight_grad(attn_t[2])
    turned = jnp.concatenate([turned, turned], axis=0)
    for xx in range(X):
        wg_mid[xx] = turned[:, xx * 192:(xx + 1) * 192].T.reshape(4, 48, 128)
    mid_moves = [push(wg_mid.at[:, y_place(j)], wg_mid_y.at[j - 1], y_peer(j)) for j in (1, 2, 3)]
    d_value = value_grad(2)
    score_grad(2)
    d_key = key_grad(2)
    query_grad(2)
    far_grad(2, d_key, d_value)
    for tt in range(SEATS):
        block = dq_t[2, :, tt * 128:(tt + 1) * 128]
        block = jnp.concatenate([block, block], axis=0).T
        low = low_lanes(block[0:64])
        half_send[tt, 0] = jnp.where(low, block[0:64], block[64:128])
        for n, part in ((1, d_key), (2, d_value)):
            top, bottom = part[tt * 128:tt * 128 + 64], part[tt * 128 + 64:tt * 128 + 128]
            half_send[tt, n] = jnp.where(low, top, bottom)
    half_out = [push(half_send.at[seat_of(d)], half_got.at[t], seg_peer(d)) for d in (2, 3, 1)]
    own_out = [pltpu.make_async_copy(half_send.at[t], half_got.at[t], local_sem.at[5])]
    own_out[0].start()
    far_moves = [
        push(far_part.at[y_place(j), pl.ds(2, 1)], far_got.at[j - 1, pl.ds(2, 1)], y_peer(j))
        for j in (1, 2, 3)
    ]
    arrive(mid_moves)
    wg_mid_sum[...] = wg_mid[:, y] + wg_mid_y[0] + wg_mid_y[1] + wg_mid_y[2]
    mid_moves = [push(wg_mid_sum.at[x_place(j)], wg_mid_x.at[j - 1], x_peer(j)) for j in (1, 2, 3)]

    arrive(full_moves)
    for tt in range(SEATS):
        rows = slice(tt * 128, (tt + 1) * 128)
        for h in range(2):
            as_queries(h, rows, full_seg[tt, 0], h == 1)
            as_keys(h, rows, full_seg[tt, 1], h == 1, k4, kt)
    weights(0)
    arrive(full_value_moves)
    for tt in range(SEATS):
        rows = slice(tt * 128, (tt + 1) * 128)
        for h in range(2):
            as_keys(h, rows, full_seg[tt, 2], h == 1, v4, vt)
    weights(1)
    attention(0)
    attention(1)
    turned = weight_grad(attn_t[0:2].reshape(128, SEG))
    for xx in range(X):
        block = turned[:, xx * 192:(xx + 1) * 192].T
        for yy in range(4):
            for n in range(2):
                wg_full[n, xx, yy] = block[yy * 48 + n * 24:yy * 48 + n * 24 + 24]
    wg_moves = [
        push(wg_full.at[0, x_place(j)], wg_full_1.at[0, j - 1], x_peer(j)) for j in (2, 1, 3)
    ] + [
        push(wg_full.at[1, :, y_place(j)], wg_full_1.at[1, j - 1], y_peer(j)) for j in (2, 1, 3)
    ]

    def send_full(n):
        moves = [push(full_send.at[seat_of(d), n], full_got.at[t, n], seg_peer(d)) for d in (2, 3, 1)]
        own_out.append(
            pltpu.make_async_copy(full_send.at[t, n], full_got.at[t, n], local_sem.at[6 + n])
        )
        own_out[-1].start()
        return moves

    def both_heads(low, high, n):
        block = jnp.where(low_lanes(low), low, high)
        for tt in range(SEATS):
            full_send[tt, n] = block[tt * 128:(tt + 1) * 128]
        return send_full(n)

    values_0, values_1 = value_grad(0), value_grad(1)
    full_out = both_heads(values_0, values_1, 2)
    score_grad(0)
    score_grad(1)
    keys_0, keys_1 = key_grad(0), key_grad(1)
    full_out += both_heads(keys_0, keys_1, 1)
    far_grad(0, keys_0, values_0)
    far_grad(1, keys_1, values_1)
    far_moves += [
        push(far_part.at[y_place(j), pl.ds(0, 2)], far_got.at[j - 1, pl.ds(0, 2)], y_peer(j))
        for j in (1, 2, 3)
    ]
    query_grad(0)
    query_grad(1)
    for tt in range(SEATS):
        full_send[tt, 0] = dq_t[0:2, :, tt * 128:(tt + 1) * 128].reshape(128, 128).T
    full_out += send_full(0)

    arrive(wg_moves)
    wg_full_sum[0] = wg_full[0, x] + wg_full_1[0, 0] + wg_full_1[0, 1] + wg_full_1[0, 2]
    wg_full_sum[1] = wg_full[1, :, y] + wg_full_1[1, 0] + wg_full_1[1, 1] + wg_full_1[1, 2]
    wg_moves = [
        push(wg_full_sum.at[0, y_place(j)], wg_full_2.at[0, j - 1], y_peer(j)) for j in (2, 1, 3)
    ] + [
        push(wg_full_sum.at[1, x_place(j)], wg_full_2.at[1, j - 1], x_peer(j)) for j in (2, 1, 3)
    ]
    arrive(mid_moves)
    mid_rows = wg_mid_sum[x] + wg_mid_x[0] + wg_mid_x[1] + wg_mid_x[2]
    for mm in range(16):
        last[mm, 3:6, :] = mid_rows[3 * mm:3 * mm + 3]
    arrive(far_moves)
    for h in range(HEADS_HERE):
        rows = far_part[y, h] + far_got[0, h] + far_got[1, h] + far_got[2, h]
        for mm in range(16):
            last[mm, 6 + 2 * h:8 + 2 * h, :] = rows[2 * mm:2 * mm + 2]
    arrive(wg_moves)
    rows_0 = wg_full_sum[0, y] + wg_full_2[0, 0] + wg_full_2[0, 1] + wg_full_2[0, 2]
    rows_1 = wg_full_sum[1, x] + wg_full_2[1, 0] + wg_full_2[1, 1] + wg_full_2[1, 2]
    for mm in range(16):
        rows = rows_0 if mm < 8 else rows_1
        last[mm, 0:3, :] = rows[3 * (mm % 8):3 * (mm % 8) + 3]
    last_moves = [
        push(last.at[ring_place(j)], last_got.at[m], ring_peer(j)) for j in FAR_FIRST
    ]
    own_out.append(pltpu.make_async_copy(last.at[m], last_got.at[m], local_sem.at[9]))
    own_out[-1].start()

    arrive(half_out)
    arrive(full_out)
    arrive(last_moves)
    for copy in own_out:
        copy.wait()
    for copy in pushed:
        copy.wait_send()


def put_together(
    full_in, half_in, last_in, offset_ref, dq_out, dk_out, dv_out, wg_out,
    full_got, half_got, last_got, dq_own, dk_own, dv_own, wg_own, in_sem, out_sem,
):
    loads = []
    for n in range(3):
        for src, dst in ((full_in, full_got), (half_in, half_got)):
            loads.append(
                pltpu.make_async_copy(src.at[:, n], dst.at[:, n], in_sem.at[len(loads)])
            )
    loads.append(pltpu.make_async_copy(last_in, last_got, in_sem.at[6]))
    for copy in loads:
        copy.start()
    stores = [
        pltpu.make_async_copy(src, dst, out_sem.at[n])
        for n, (src, dst) in enumerate(
            ((dq_own, dq_out), (dk_own, dk_out), (dv_own, dv_out), (wg_own, wg_out))
        )
    ]
    row64 = lax.broadcasted_iota(jnp.int32, (64, 128), 0)
    low64 = lax.broadcasted_iota(jnp.int32, (64, 128), 1) < 64
    outs = (dq_own, dk_own, dv_own)
    notes = []

    def with_extra(n, r, tt, h, upper, block):
        if n == 0:
            return block
        row = notes[tt][6 + 2 * h + r:7 + 2 * h + r]
        if (n == 2) != upper:
            row = flip(row)
        keep = (row64 == offset_ref[head_of(tt, h)]) & (low64 != upper)
        return block + jnp.where(keep, jnp.broadcast_to(row, (64, 128)), 0.0)

    for n in range(3):
        loads[2 * n].wait()
        loads[2 * n + 1].wait()
        if n == 1:
            loads[6].wait()
            notes += [
                last_got[tt] + last_got[4 + tt] + last_got[8 + tt] + last_got[12 + tt]
                for tt in range(SEATS)
            ]
        for half in range(2):
            even, odd = half_got[2 * half, n], half_got[2 * half + 1, n]
            for r in range(2):
                if r == 0:
                    block = jnp.where(low64, even, flip(odd))
                else:
                    block = jnp.where(low64, flip(even), odd)
                block = with_extra(n, r, 2 * half, 2, False, block)
                block = with_extra(n, r, 2 * half + 1, 2, True, block)
                outs[n][r * 64:(r + 1) * 64, lanes_of(3 * half + 1)] = block
        for tt in range(SEATS):
            for r in range(2):
                block = full_got[tt, n, r * 64:(r + 1) * 64, :]
                block = with_extra(n, r, tt, 0, False, block)
                block = with_extra(n, r, tt, 1, True, block)
                outs[n][r * 64:(r + 1) * 64, lanes_of(full_tile(tt))] = block
        stores[n].start()

    scale = 8192.0 ** -0.5
    for tt in range(SEATS):
        wg_own[:, lanes_of(full_tile(tt))] = notes[tt][0:3] * scale
    for half in range(2):
        even, odd = notes[2 * half][3:6], notes[2 * half + 1][3:6]
        wg_own[:, lanes_of(3 * half + 1)] = jnp.where(low_lanes(even), even, odd) * scale
    stores[3].start()
    for copy in stores:
        copy.wait()


def on_device(queries, keys, values, out_grad, out_weight, valid_tiles, head_offsets):
    def block(*shape):
        return pltpu.VMEM(shape, F32)

    def half(*shape):
        return pltpu.VMEM(shape, BF16)

    scratch = [
        block(ROWS, WIDTH), block(ROWS, WIDTH), block(ROWS, WIDTH), block(3, WIDTH),
        block(4, 3, 64, 128), block(4, 3, 64, 128), block(4, 3, 128, 128), block(4, 3, 128, 128),
        block(4, ROWS, WIDTH),
        block(4, 12, 128), block(16, 12, 128),
        block(4, 4, 48, 128), block(4, 4, 48, 128), half(WIDTH, 256), half(WIDTH, 256),
        block(4, 3, 32, 128),
        half(3, SEG, 256), half(3, KEYS, 256), half(3, KEYS, 256),
        half(3, 128, KEYS), half(3, 128, KEYS),
        half(3, SEG, 256), block(3, 64, SEG), block(3, 64, SEG),
        block(3, KEYS, SEG), half(3, KEYS, SEG), half(3, KEYS, SEG),
        half(3, KEYS, SEG), half(3, KEYS, SEG),
        half(SEG, WIDTH), half(SEG, WIDTH),
        block(4, 3, 32, 128), block(3, 3, 32, 128),
        block(2, 4, 4, 24, 128), block(2, 3, 4, 24, 128), block(2, 4, 24, 128), block(2, 3, 24, 128),
        block(4, 4, 48, 128), block(3, 4, 48, 128), block(4, 48, 128), block(3, 48, 128),
        block(16, 12, 128), block(3, 64, SEG),
        block(4, 3, 128, 128), block(4, 3, 64, 128),
        pltpu.SemaphoreType.DMA((SENDS,)), pltpu.SemaphoreType.DMA((SENDS,)),
        pltpu.SemaphoreType.DMA((10,)),
    ]
    whole = pl.BlockSpec(memory_space=pltpu.HBM)
    scalars = pl.BlockSpec(memory_space=pltpu.SMEM)
    rows = jax.ShapeDtypeStruct((ROWS, WIDTH), F32)
    got = pl.pallas_call(
        kernel,
        out_shape=(
            jax.ShapeDtypeStruct((4, 3, 128, 128), F32),
            jax.ShapeDtypeStruct((4, 3, 64, 128), F32),
            jax.ShapeDtypeStruct((16, 12, 128), F32),
        ),
        in_specs=[whole] * 5 + [scalars] * 2,
        out_specs=(whole,) * 3,
        scratch_shapes=scratch,
        compiler_params=pltpu.CompilerParams(
            collective_id=0, has_side_effects=True, vmem_limit_bytes=60 * 1024 * 1024
        ),
        cost_estimate=pl.CostEstimate(
            flops=4_000_000_000, bytes_accessed=4_000_000, transcendentals=1_000_000
        ),
        name="dilated_backward",
    )(queries[0], keys[0], values[0], out_grad[0], out_weight, valid_tiles, head_offsets)
    d_query, d_key, d_value, d_weight = pl.pallas_call(
        put_together,
        out_shape=(rows, rows, rows, jax.ShapeDtypeStruct((3, WIDTH), F32)),
        in_specs=[whole] * 3 + [scalars],
        out_specs=(whole,) * 4,
        scratch_shapes=[
            block(4, 3, 128, 128), block(4, 3, 64, 128), block(16, 12, 128),
            block(ROWS, WIDTH), block(ROWS, WIDTH), block(ROWS, WIDTH), block(3, WIDTH),
            pltpu.SemaphoreType.DMA((7,)), pltpu.SemaphoreType.DMA((4,)),
        ],
        compiler_params=pltpu.CompilerParams(vmem_limit_bytes=60 * 1024 * 1024),
        cost_estimate=pl.CostEstimate(flops=1_000_000, bytes_accessed=2_500_000, transcendentals=0),
        name="put_together",
    )(*got, head_offsets)
    return d_query[None], d_key[None], d_value[None], d_weight


def solution(mesh):
    from jax.sharding import PartitionSpec as P

    tiles = P("dp", "seq", None)
    weight = P(("dp", "seq"), None)
    return jax.shard_map(
        on_device,
        mesh=mesh,
        in_specs=(tiles, tiles, tiles, tiles, weight, P("dp"), P()),
        out_specs=(tiles, tiles, tiles, weight),
        check_vma=False,
    )
```

```python
import jax
import jax.numpy as jnp
from jax import lax
from jax.experimental import pallas as pl
from jax.experimental.pallas import tpu as pltpu

F32 = jnp.float32
BF16 = jnp.bfloat16
MASKED = -1e30
MESH = pl.DeviceIdType.MESH

X = 4
ROWS = 128
SEATS = 4
SEG = ROWS * SEATS
SPACING = 64
FAR = 128
WIDTH = 768
HEADS_HERE = 3
KEYS = SEG + FAR
G_CHUNKS = 4
G_EARLY = 2
FAR_FIRST = (8, 7, 9, 6, 10, 5, 11, 4, 12, 3, 13, 2, 14, 1, 15)
SENDS = 32


def dot(left, right):
    return lax.dot_general(left, right, (((1,), (0,)), ((), ())), preferred_element_type=F32)


def dot_nt(left, right):
    return lax.dot_general(left, right, (((1,), (1,)), ((), ())), preferred_element_type=F32)


def flip(block):
    return pltpu.roll(block, 64, 1)


def low_lanes(block):
    return lax.broadcasted_iota(jnp.int32, block.shape, 1) < 64


def split(block):
    high = block.astype(BF16).astype(F32)
    return high, block - high


def pair(block, upper):
    high, low = split(block)
    if upper:
        return jnp.where(low_lanes(block), flip(high), low)
    return jnp.where(low_lanes(block), high, flip(low))


def twice(block, upper):
    if upper:
        return jnp.where(low_lanes(block), flip(block), block)
    return jnp.where(low_lanes(block), block, flip(block))


def unfold(packed):
    return jnp.concatenate([packed, flip(packed)], axis=0)


def fold_halves(block):
    return block + flip(block)


def lanes_of(tile):
    return slice(tile * 128, (tile + 1) * 128)


def full_tile(seat):
    return 3 * (seat // 2) + 2 * (seat % 2)


def middle_tile(seat):
    return 3 * (seat // 2) + 1


def head_of(seat, h):
    return 6 * (seat // 2) + (2 + seat % 2 if h == 2 else 4 * (seat % 2) + h)


def kernel(
    q_in, k_in, v_in, g_in, w_in, valid_ref, offset_ref,
    full_got, half_got, last_got,
    q_own, k_own, v_own, w_own, half_in, half_seg, full_in, full_seg, g_seg,
    note, note_got, w_full, w_mid, w_hi, w_lo, far,
    q4, k4, v4, kt, vt, do4, do_t, attn_t, prob, prob_hi, prob_lo, ds_hi, ds_lo, g_hi, g_lo,
    far_part, far_got,
    wg_full, wg_full_1, wg_full_sum, wg_full_2, wg_mid, wg_mid_1, wg_mid_sum, wg_mid_2,
    last, dq_t, full_send, half_send,
    send_sem, recv_sem, local_sem,
):
    x = lax.axis_index("dp")
    s = lax.axis_index("seq")
    y = lax.div(s, 16)
    m = lax.rem(s, 16)
    z = lax.div(m, 2)
    c = lax.rem(s, 2)
    hz = lax.rem(z, 2)
    zz = lax.div(z, 2)
    t = lax.rem(s, 4)
    seg = lax.div(s, 4)

    def seat_of(d):
        core = c if d % 2 == 0 else 1 - c
        half = hz if d < 2 else 1 - hz
        return half * 2 + core

    def seg_peer(d):
        return (x, seg * 4 + seat_of(d))

    def ring_place(j):
        return lax.rem(m + j, 16)

    def ring_peer(j):
        return (x, y * 16 + ring_place(j))

    def y_place(j):
        return lax.rem(y + j, 4)

    def y_peer(j):
        return (x, y_place(j) * 16 + m)

    def x_place(j):
        return lax.rem(x + j, 4)

    def x_peer(j):
        return (x_place(j), s)

    class Group:
        count = 0

        def __init__(self, like, copies=()):
            self.like, self.index = like, Group.count
            Group.count += 1
            self.add(copies)

        def describe(self, src, dst, device):
            return pltpu.make_async_remote_copy(
                src_ref=src, dst_ref=dst, send_sem=send_sem.at[self.index],
                recv_sem=recv_sem.at[self.index], device_id=device, device_id_type=MESH,
            )

        def add(self, copies):
            for src, dst, device in copies:
                self.describe(src, dst, device).start()

        def arrive(self):
            self.describe(self.like, self.like, seg_peer(1)).wait_recv()

        def sent(self):
            self.describe(self.like, self.like, seg_peer(1)).wait_send()

    barrier = pltpu.get_barrier_semaphore()
    for device in (
        [ring_peer(j) for j in range(1, 16)]
        + [y_peer(j) for j in (1, 2, 3)]
        + [x_peer(j) for j in (1, 2, 3)]
    ):
        pl.semaphore_signal(barrier, inc=1, device_id=device, device_id_type=MESH)

    loads = []
    for src, dst in (
        (g_in, g_seg.at[t]), (k_in, k_own), (v_in, v_own), (w_in, w_own), (q_in, q_own),
    ):
        copy = pltpu.make_async_copy(src, dst, local_sem.at[len(loads)])
        copy.start()
        loads.append(copy)

    owns = (q_own, k_own, v_own)

    def deal(n):
        for tt in range(SEATS):
            full_in[tt, n] = owns[n][:, lanes_of(full_tile(tt))]
            top = owns[n][0:64, lanes_of(middle_tile(tt))]
            bottom = owns[n][64:128, lanes_of(middle_tile(tt))]
            if tt % 2 == 0:
                half_in[tt, n] = jnp.where(low_lanes(top), top, flip(bottom))
            else:
                half_in[tt, n] = jnp.where(low_lanes(top), flip(top), bottom)

    g_rows = ROWS // G_CHUNKS

    def g_part(seat, n):
        return g_seg.at[seat, pl.ds(n * g_rows, g_rows)]

    loads[0].wait()
    pl.semaphore_wait(barrier, 21)
    def send_across(n):
        return Group(g_part(0, n), [(g_part(t, n), g_part(t, n), seg_peer(2))])

    g_across = [send_across(n) for n in range(G_EARLY)]

    loads[1].wait()
    deal(1)
    loads[2].wait()
    deal(2)

    def long_rows(tt, h, n):
        offset = offset_ref[head_of(tt, h)]
        if h == 2:
            row = half_in[tt, n, pl.ds(offset, 1), :]
            return jnp.concatenate([row, flip(row)], axis=0)
        return jnp.concatenate(
            [full_in[tt, n, pl.ds(r * 64 + offset, 1), :] for r in range(2)], axis=0
        )

    loads[3].wait()
    for tt in range(SEATS):
        note[tt, 0:3, :] = w_own[:, lanes_of(full_tile(tt))]
        note[tt, 3:6, :] = w_own[:, lanes_of(middle_tile(tt))]
        for h in range(HEADS_HERE):
            key_rows, value_rows = long_rows(tt, h, 1), long_rows(tt, h, 2)
            low = low_lanes(key_rows)
            if h == 1:
                rows = jnp.where(low, flip(key_rows), value_rows)
            else:
                rows = jnp.where(low, key_rows, flip(value_rows))
            note[tt, 6 + 2 * h:8 + 2 * h, :] = rows

    notes = Group(
        note_got.at[pl.ds(0, 15)],
        [(note.at[lax.rem(ring_place(j), 4)], note_got.at[m], ring_peer(j)) for j in FAR_FIRST],
    )
    g_across += [send_across(n) for n in range(G_EARLY, G_CHUNKS)]
    note_got[m] = note[t]
    loads[4].wait()
    deal(0)
    full_in_moves = Group(
        full_seg.at[pl.ds(0, 3), pl.ds(0, 2)],
        [
            (full_in.at[seat_of(d), pl.ds(0, 2)], full_seg.at[t, pl.ds(0, 2)], seg_peer(d))
            for d in (2, 3, 1)
        ],
    )
    value_in_moves = Group(
        full_seg.at[pl.ds(0, 3), 2],
        [(full_in.at[seat_of(d), 2], full_seg.at[t, 2], seg_peer(d)) for d in (2, 3, 1)],
    )
    g_beside = Group(g_seg.at[0], [(g_seg.at[t], g_seg.at[t], seg_peer(1))])
    half_in_moves = Group(
        half_seg.at[pl.ds(0, 3)],
        [(half_in.at[seat_of(d)], half_seg.at[t], seg_peer(d)) for d in (2, 3, 1)],
    )
    half_seg[t] = half_in[t]
    full_seg[t] = full_in[t]

    notes.arrive()
    for mm in range(16):
        w_full[x, y, 3 * mm:3 * mm + 3, :] = note_got[mm, 0:3, :]
        w_mid[x, y, 3 * mm:3 * mm + 3, :] = note_got[mm, 3:6, :]
        for h in range(HEADS_HERE):
            far[y, h, 2 * mm:2 * mm + 2, :] = note_got[mm, 6 + 2 * h:8 + 2 * h, :]
    w_first = Group(
        w_full.at[pl.ds(0, 2), pl.ds(0, 3)],
        [(w_full.at[x, y], w_full.at[x, y], y_peer(j)) for j in (2, 1, 3)]
        + [(w_mid.at[x, y], w_mid.at[x, y], x_peer(j)) for j in (2, 1, 3)],
    )
    far_moves = Group(
        far.at[pl.ds(0, 3)], [(far.at[y], far.at[y], y_peer(j)) for j in (2, 1, 3)]
    )
    w_first.arrive()
    w_full_moves = Group(
        w_full.at[pl.ds(0, 3)], [(w_full.at[x], w_full.at[x], x_peer(j)) for j in (2, 1, 3)]
    )
    w_mid_moves = Group(
        w_mid.at[pl.ds(0, 3)], [(w_mid.at[:, y], w_mid.at[:, y], y_peer(j)) for j in (2, 1, 3)]
    )
    far_moves.arrive()

    def as_keys(h, rows, block, upper, four, transposed):
        high, low = split(block)
        four[h, rows, 0:128] = twice(high, upper).astype(BF16)
        four[h, rows, 128:256] = twice(low, upper).astype(BF16)
        transposed[h, :, rows] = pair(block, upper).T.astype(BF16)

    for h in range(HEADS_HERE):
        block = far[:, h].reshape(FAR, 128)
        as_keys(h, slice(SEG, KEYS), block, False, k4, kt)
        as_keys(h, slice(SEG, KEYS), block, True, v4, vt)

    valid = valid_ref[0]
    tile_row = lax.broadcasted_iota(jnp.int32, (ROWS, WIDTH), 0)

    def take_grad(seat):
        rows = pl.ds(pl.multiple_of(seat * ROWS, ROWS), ROWS)
        grad = jnp.where(seg * SEG + seat * ROWS + tile_row < valid, g_seg[seat], 0.0)
        high = grad.astype(BF16)
        g_hi[rows, :] = high
        g_lo[rows, :] = (grad - high.astype(F32)).astype(BF16)

    take_grad(t)
    g_beside.arrive()
    take_grad(seat_of(1))
    g_forwarded = Group(g_seg.at[0])
    for n in range(G_CHUNKS):
        g_across[n].arrive()
        part = g_part(seat_of(2), n)
        g_forwarded.add([(part, part, seg_peer(1))])
    take_grad(seat_of(2))

    w_full_moves.arrive()
    w_mid_moves.arrive()
    for tile, ref in ((0, w_full), (1, w_mid)):
        columns = ref[...].reshape(WIDTH, 128)
        if tile == 1:
            columns = jnp.where(c == 1, flip(columns), columns)
        high = columns.astype(BF16)
        w_hi[:, lanes_of(tile)] = high
        w_lo[:, lanes_of(tile)] = (columns - high.astype(F32)).astype(BF16)

    g_forwarded.arrive()
    take_grad(seat_of(3))
    for tt in range(SEATS):
        rows = slice(tt * 128, (tt + 1) * 128)
        high, low = g_hi[rows, :], g_lo[rows, :]
        out = dot(high, w_hi[...]) + dot(low, w_hi[...]) + dot(high, w_lo[...])
        full, middle = out[:, 0:128], out[:, 128:256]
        for h, block, upper in ((0, full, False), (1, full, True), (2, middle, False)):
            both = pair(block, upper).astype(BF16)
            do4[h, rows, 0:128] = both
            do4[h, rows, 128:256] = both
        turned = full.T
        do_t[0, :, rows] = turned[0:64]
        do_t[1, :, rows] = turned[64:128]
        do_t[2, :, rows] = middle.T[0:64]

    def as_queries(h, rows, block, upper):
        both = pair(block * 0.125, upper).astype(BF16)
        q4[h, rows, 0:128] = both
        q4[h, rows, 128:256] = both

    key_row = lax.broadcasted_iota(jnp.int32, (128, 256), 0)
    query_lane = lax.broadcasted_iota(jnp.int32, (128, 256), 1)

    def weights(h):
        head = 6 * hz + jnp.where(h == 2, 2 + c, 4 * c + h)
        offset = offset_ref[head]
        for qb in range(2):
            lanes = slice(qb * 256, (qb + 1) * 256)
            queries = q4[h, lanes, :]
            top = None
            for kb in range(5):
                rows = slice(kb * 128, (kb + 1) * 128)
                scores = dot_nt(k4[h, rows, :], queries)
                if kb < 4:
                    keep = (seg * SEG + kb * 128 + key_row < valid) | (
                        kb * 128 + key_row == qb * 256 + query_lane
                    )
                else:
                    keep = (key_row * SPACING + offset < valid) & (
                        lax.rem(query_lane, SPACING) == offset
                    )
                scores = jnp.where(keep, scores, MASKED)
                prob[h, rows, lanes] = scores
                here = jnp.max(scores, axis=0, keepdims=True)
                top = here if top is None else jnp.maximum(top, here)
            total = None
            for kb in range(5):
                rows = slice(kb * 128, (kb + 1) * 128)
                weight = jnp.exp(prob[h, rows, lanes] - top)
                prob[h, rows, lanes] = weight
                here = jnp.sum(weight, axis=0, keepdims=True)
                total = here if total is None else total + here
            scale = 1.0 / total
            for kb in range(5):
                rows = slice(kb * 128, (kb + 1) * 128)
                p = prob[h, rows, lanes] * scale
                prob[h, rows, lanes] = p
                high = p.astype(BF16)
                prob_hi[h, rows, lanes] = high
                prob_lo[h, rows, lanes] = (p - high.astype(F32)).astype(BF16)

    def attention(h):
        for qb in range(2):
            lanes = slice(qb * 256, (qb + 1) * 256)
            out = dot(vt[h], prob_hi[h, :, lanes]) + dot(vt[h], prob_lo[h, :, lanes])
            attn_t[h, :, lanes] = out[0:64] + out[64:128]

    def value_grad(h):
        grads = do4[h, :, 0:128]
        return fold_halves(dot(prob_hi[h], grads) + dot(prob_lo[h], grads))

    def key_grad(h):
        queries = q4[h, :, 0:128]
        return fold_halves(dot(ds_hi[h], queries) + dot(ds_lo[h], queries))

    def score_grad(h):
        for qb in range(2):
            lanes = slice(qb * 256, (qb + 1) * 256)
            delta = jnp.sum(attn_t[h, :, lanes] * do_t[h, :, lanes], axis=0, keepdims=True)
            for kb in range(5):
                rows = slice(kb * 128, (kb + 1) * 128)
                d_prob = dot_nt(v4[h, rows, :], do4[h, lanes, :])
                ds = prob[h, rows, lanes] * (d_prob - delta)
                high = ds.astype(BF16)
                ds_hi[h, rows, lanes] = high
                ds_lo[h, rows, lanes] = (ds - high.astype(F32)).astype(BF16)

    def query_grad(h):
        turned = dot(kt[h], ds_hi[h]) + dot(kt[h], ds_lo[h])
        dq_t[h] = (turned[0:64] + turned[64:128]) * 0.125

    def weight_grad(attn):
        high = attn.astype(BF16)
        low = (attn - high.astype(F32)).astype(BF16)
        return dot(high, g_hi[...]) + dot(low, g_hi[...]) + dot(high, g_lo[...])

    def far_grad(h, d_key, d_value):
        d_key, d_value = d_key[SEG:KEYS], d_value[SEG:KEYS]
        block = jnp.where(low_lanes(d_key), d_key, d_value)
        far_part[:, h] = block.reshape(4, 32, 128)

    for group in [notes, w_first, far_moves, g_beside] + g_across:
        group.sent()
    full_in_moves.arrive()
    for tt in range(SEATS):
        rows = slice(tt * 128, (tt + 1) * 128)
        for h in range(2):
            as_queries(h, rows, full_seg[tt, 0], h == 1)
            as_keys(h, rows, full_seg[tt, 1], h == 1, k4, kt)
    weights(0)
    weights(1)
    value_in_moves.arrive()
    for tt in range(SEATS):
        rows = slice(tt * 128, (tt + 1) * 128)
        for h in range(2):
            as_keys(h, rows, full_seg[tt, 2], h == 1, v4, vt)
    attention(0)
    attention(1)
    turned = weight_grad(attn_t[0:2].reshape(128, SEG))
    for xx in range(X):
        block = turned[:, xx * 192:(xx + 1) * 192].T
        for yy in range(4):
            for n in range(2):
                wg_full[n, xx, yy] = block[yy * 48 + n * 24:yy * 48 + n * 24 + 24]
    wg_first = Group(
        wg_full_1,
        [(wg_full.at[0, x_place(j)], wg_full_1.at[0, j - 1], x_peer(j)) for j in (2, 1, 3)]
        + [(wg_full.at[1, :, y_place(j)], wg_full_1.at[1, j - 1], y_peer(j)) for j in (2, 1, 3)],
    )

    full_out = Group(full_got.at[pl.ds(0, 3)])
    own_out = []

    def keep_own(src, dst):
        copy = pltpu.make_async_copy(src, dst, local_sem.at[5 + len(own_out)])
        copy.start()
        own_out.append(copy)

    def send_full(n):
        full_out.add(
            (full_send.at[seat_of(d), n], full_got.at[t, n], seg_peer(d)) for d in (2, 3, 1)
        )
        keep_own(full_send.at[t, n], full_got.at[t, n])

    def both_heads(low, high, n):
        block = jnp.where(low_lanes(low), low, high)
        for tt in range(SEATS):
            full_send[tt, n] = block[tt * 128:(tt + 1) * 128]
        send_full(n)

    values_0, values_1 = value_grad(0), value_grad(1)
    both_heads(values_0, values_1, 2)
    score_grad(0)
    score_grad(1)
    keys_0, keys_1 = key_grad(0), key_grad(1)
    both_heads(keys_0, keys_1, 1)
    far_grad(0, keys_0, values_0)
    far_grad(1, keys_1, values_1)
    far_out = Group(
        far_got,
        [
            (far_part.at[y_place(j), pl.ds(0, 2)], far_got.at[j - 1, pl.ds(0, 2)], y_peer(j))
            for j in (2, 1, 3)
        ],
    )
    query_grad(0)
    query_grad(1)
    for tt in range(SEATS):
        full_send[tt, 0] = dq_t[0:2, :, tt * 128:(tt + 1) * 128].reshape(128, 128).T
    send_full(0)

    half_in_moves.arrive()
    for tt in range(SEATS):
        rows = slice(tt * 128, (tt + 1) * 128)
        as_queries(2, rows, unfold(half_seg[tt, 0]), False)
        as_keys(2, rows, unfold(half_seg[tt, 1]), False, k4, kt)
        as_keys(2, rows, unfold(half_seg[tt, 2]), False, v4, vt)
    weights(2)
    attention(2)
    turned = weight_grad(attn_t[2])
    turned = jnp.concatenate([turned, turned], axis=0)
    for xx in range(X):
        block = turned[:, xx * 192:(xx + 1) * 192].T
        for yy in range(4):
            top, bottom = block[yy * 48:yy * 48 + 24], block[yy * 48 + 24:yy * 48 + 48]
            wg_mid[xx, yy] = jnp.where(low_lanes(top), top, bottom)
    mid_first = Group(
        wg_mid_1, [(wg_mid.at[x_place(j)], wg_mid_1.at[j - 1], x_peer(j)) for j in (2, 1, 3)]
    )
    wg_first.arrive()
    wg_full_sum[0] = wg_full[0, x] + wg_full_1[0, 0] + wg_full_1[0, 1] + wg_full_1[0, 2]
    wg_full_sum[1] = wg_full[1, :, y] + wg_full_1[1, 0] + wg_full_1[1, 1] + wg_full_1[1, 2]
    wg_second = Group(
        wg_full_2,
        [(wg_full_sum.at[0, y_place(j)], wg_full_2.at[0, j - 1], y_peer(j)) for j in (2, 1, 3)]
        + [(wg_full_sum.at[1, x_place(j)], wg_full_2.at[1, j - 1], x_peer(j)) for j in (2, 1, 3)],
    )
    d_value = value_grad(2)
    score_grad(2)
    d_key = key_grad(2)
    far_grad(2, d_key, d_value)
    far_out.add(
        (far_part.at[y_place(j), pl.ds(2, 1)], far_got.at[j - 1, pl.ds(2, 1)], y_peer(j))
        for j in (2, 1, 3)
    )
    query_grad(2)
    for tt in range(SEATS):
        block = dq_t[2, :, tt * 128:(tt + 1) * 128]
        block = jnp.concatenate([block, block], axis=0).T
        low = low_lanes(block[0:64])
        half_send[tt, 0] = jnp.where(low, block[0:64], block[64:128])
        for n, part in ((1, d_key), (2, d_value)):
            top, bottom = part[tt * 128:tt * 128 + 64], part[tt * 128 + 64:tt * 128 + 128]
            half_send[tt, n] = jnp.where(low, top, bottom)
    half_out = Group(
        half_got.at[pl.ds(0, 3)],
        [(half_send.at[seat_of(d)], half_got.at[t], seg_peer(d)) for d in (2, 3, 1)],
    )
    keep_own(half_send.at[t], half_got.at[t])

    mid_first.arrive()
    wg_mid_sum[...] = wg_mid[x] + wg_mid_1[0] + wg_mid_1[1] + wg_mid_1[2]
    mid_second = Group(
        wg_mid_2, [(wg_mid_sum.at[y_place(j)], wg_mid_2.at[j - 1], y_peer(j)) for j in (2, 1, 3)]
    )
    wg_second.arrive()
    rows_0 = wg_full_sum[0, y] + wg_full_2[0, 0] + wg_full_2[0, 1] + wg_full_2[0, 2]
    rows_1 = wg_full_sum[1, x] + wg_full_2[1, 0] + wg_full_2[1, 1] + wg_full_2[1, 2]
    for mm in range(16):
        rows = rows_0 if mm < 8 else rows_1
        last[mm, 0:3, :] = rows[3 * (mm % 8):3 * (mm % 8) + 3]
    far_out.arrive()
    for h in range(HEADS_HERE):
        rows = far_part[y, h] + far_got[0, h] + far_got[1, h] + far_got[2, h]
        for mm in range(16):
            last[mm, 6 + 2 * h:8 + 2 * h, :] = rows[2 * mm:2 * mm + 2]
    mid_second.arrive()
    packed = wg_mid_sum[y] + wg_mid_2[0] + wg_mid_2[1] + wg_mid_2[2]
    for mm in range(16):
        rows = packed if mm < 8 else flip(packed)
        last[mm, 3:6, :] = rows[3 * (mm % 8):3 * (mm % 8) + 3]
    last_moves = Group(
        last_got.at[pl.ds(0, 15)],
        [(last.at[ring_place(j)], last_got.at[m], ring_peer(j)) for j in FAR_FIRST],
    )
    keep_own(last.at[m], last_got.at[m])

    for group in (
        w_full_moves, w_mid_moves, g_forwarded, full_in_moves, value_in_moves, half_in_moves,
        wg_first, mid_first, wg_second, far_out, mid_second,
    ):
        group.sent()
    for copy in own_out:
        copy.wait()
    for group in (full_out, half_out, last_moves):
        group.arrive()
        group.sent()


def put_together(
    full_in, half_in, last_in, offset_ref, dq_out, dk_out, dv_out, wg_out,
    full_got, half_got, last_got, dq_own, dk_own, dv_own, wg_own, in_sem, out_sem,
):
    loads = []
    for n in range(3):
        for src, dst in ((full_in, full_got), (half_in, half_got)):
            loads.append(
                pltpu.make_async_copy(src.at[:, n], dst.at[:, n], in_sem.at[len(loads)])
            )
    loads.append(pltpu.make_async_copy(last_in, last_got, in_sem.at[6]))
    for copy in loads:
        copy.start()
    stores = [
        pltpu.make_async_copy(src, dst, out_sem.at[n])
        for n, (src, dst) in enumerate(
            ((dq_own, dq_out), (dk_own, dk_out), (dv_own, dv_out), (wg_own, wg_out))
        )
    ]
    row64 = lax.broadcasted_iota(jnp.int32, (64, 128), 0)
    low64 = lax.broadcasted_iota(jnp.int32, (64, 128), 1) < 64
    outs = (dq_own, dk_own, dv_own)
    notes = []

    def with_extra(n, r, tt, h, upper, block):
        if n == 0:
            return block
        row = notes[tt][6 + 2 * h + r:7 + 2 * h + r]
        if (n == 2) != upper:
            row = flip(row)
        keep = (row64 == offset_ref[head_of(tt, h)]) & (low64 != upper)
        return block + jnp.where(keep, jnp.broadcast_to(row, (64, 128)), 0.0)

    for n in range(3):
        loads[2 * n].wait()
        loads[2 * n + 1].wait()
        if n == 1:
            loads[6].wait()
            notes += [
                last_got[tt] + last_got[4 + tt] + last_got[8 + tt] + last_got[12 + tt]
                for tt in range(SEATS)
            ]
        for half in range(2):
            even, odd = half_got[2 * half, n], half_got[2 * half + 1, n]
            for r in range(2):
                if r == 0:
                    block = jnp.where(low64, even, flip(odd))
                else:
                    block = jnp.where(low64, flip(even), odd)
                block = with_extra(n, r, 2 * half, 2, False, block)
                block = with_extra(n, r, 2 * half + 1, 2, True, block)
                outs[n][r * 64:(r + 1) * 64, lanes_of(3 * half + 1)] = block
        for tt in range(SEATS):
            for r in range(2):
                block = full_got[tt, n, r * 64:(r + 1) * 64, :]
                block = with_extra(n, r, tt, 0, False, block)
                block = with_extra(n, r, tt, 1, True, block)
                outs[n][r * 64:(r + 1) * 64, lanes_of(full_tile(tt))] = block
        stores[n].start()

    scale = 8192.0 ** -0.5
    for tt in range(SEATS):
        wg_own[:, lanes_of(full_tile(tt))] = notes[tt][0:3] * scale
    for half in range(2):
        even, odd = notes[2 * half][3:6], notes[2 * half + 1][3:6]
        wg_own[:, lanes_of(3 * half + 1)] = jnp.where(low_lanes(even), even, flip(odd)) * scale
    stores[3].start()
    for copy in stores:
        copy.wait()


def on_device(queries, keys, values, out_grad, out_weight, valid_tiles, head_offsets):
    def block(*shape):
        return pltpu.VMEM(shape, F32)

    def half(*shape):
        return pltpu.VMEM(shape, BF16)

    scratch = [
        block(ROWS, WIDTH), block(ROWS, WIDTH), block(ROWS, WIDTH), block(3, WIDTH),
        block(4, 3, 64, 128), block(4, 3, 64, 128), block(4, 3, 128, 128), block(4, 3, 128, 128),
        block(4, ROWS, WIDTH),
        block(4, 12, 128), block(16, 12, 128),
        block(4, 4, 48, 128), block(4, 4, 48, 128), half(WIDTH, 256), half(WIDTH, 256),
        block(4, 3, 32, 128),
        half(3, SEG, 256), half(3, KEYS, 256), half(3, KEYS, 256),
        half(3, 128, KEYS), half(3, 128, KEYS),
        half(3, SEG, 256), block(3, 64, SEG), block(3, 64, SEG),
        block(3, KEYS, SEG), half(3, KEYS, SEG), half(3, KEYS, SEG),
        half(3, KEYS, SEG), half(3, KEYS, SEG),
        half(SEG, WIDTH), half(SEG, WIDTH),
        block(4, 3, 32, 128), block(3, 3, 32, 128),
        block(2, 4, 4, 24, 128), block(2, 3, 4, 24, 128), block(2, 4, 24, 128), block(2, 3, 24, 128),
        block(4, 4, 24, 128), block(3, 4, 24, 128), block(4, 24, 128), block(3, 24, 128),
        block(16, 12, 128), block(3, 64, SEG),
        block(4, 3, 128, 128), block(4, 3, 64, 128),
        pltpu.SemaphoreType.DMA((SENDS,)), pltpu.SemaphoreType.DMA((SENDS,)),
        pltpu.SemaphoreType.DMA((10,)),
    ]
    whole = pl.BlockSpec(memory_space=pltpu.HBM)
    scalars = pl.BlockSpec(memory_space=pltpu.SMEM)
    rows = jax.ShapeDtypeStruct((ROWS, WIDTH), F32)
    got = pl.pallas_call(
        kernel,
        out_shape=(
            jax.ShapeDtypeStruct((4, 3, 128, 128), F32),
            jax.ShapeDtypeStruct((4, 3, 64, 128), F32),
            jax.ShapeDtypeStruct((16, 12, 128), F32),
        ),
        in_specs=[whole] * 5 + [scalars] * 2,
        out_specs=(whole,) * 3,
        scratch_shapes=scratch,
        compiler_params=pltpu.CompilerParams(
            collective_id=0, has_side_effects=True, vmem_limit_bytes=60 * 1024 * 1024
        ),
        cost_estimate=pl.CostEstimate(
            flops=4_000_000_000, bytes_accessed=4_000_000, transcendentals=1_000_000
        ),
        name="dilated_backward",
    )(queries[0], keys[0], values[0], out_grad[0], out_weight, valid_tiles, head_offsets)
    d_query, d_key, d_value, d_weight = pl.pallas_call(
        put_together,
        out_shape=(rows, rows, rows, jax.ShapeDtypeStruct((3, WIDTH), F32)),
        in_specs=[whole] * 3 + [scalars],
        out_specs=(whole,) * 4,
        scratch_shapes=[
            block(4, 3, 128, 128), block(4, 3, 64, 128), block(16, 12, 128),
            block(ROWS, WIDTH), block(ROWS, WIDTH), block(ROWS, WIDTH), block(3, WIDTH),
            pltpu.SemaphoreType.DMA((7,)), pltpu.SemaphoreType.DMA((4,)),
        ],
        compiler_params=pltpu.CompilerParams(vmem_limit_bytes=60 * 1024 * 1024),
        cost_estimate=pl.CostEstimate(flops=1_000_000, bytes_accessed=2_500_000, transcendentals=0),
        name="put_together",
    )(*got, head_offsets)
    return d_query[None], d_key[None], d_value[None], d_weight


def solution(mesh):
    from jax.sharding import PartitionSpec as P

    tiles = P("dp", "seq", None)
    weight = P(("dp", "seq"), None)
    return jax.shard_map(
        on_device,
        mesh=mesh,
        in_specs=(tiles, tiles, tiles, tiles, weight, P("dp"), P()),
        out_specs=(tiles, tiles, tiles, weight),
        check_vma=False,
    )
```

```python
import jax
import jax.numpy as jnp
from jax import lax
from jax.experimental import pallas as pl
from jax.experimental.pallas import tpu as pltpu

F32 = jnp.float32
BF16 = jnp.bfloat16
MASKED = -1e30
MESH = pl.DeviceIdType.MESH

X = 4
ROWS = 128
SEATS = 4
SEG = ROWS * SEATS
SPACING = 64
FAR = 128
WIDTH = 768
HEADS_HERE = 3
KEYS = SEG + FAR
G_CHUNKS = 4
G_EARLY = 2
FAR_FIRST = (8, 7, 9, 6, 10, 5, 11, 4, 12, 3, 13, 2, 14, 1, 15)
SENDS = 32


def dot(left, right):
    return lax.dot_general(left, right, (((1,), (0,)), ((), ())), preferred_element_type=F32)


def dot_nt(left, right):
    return lax.dot_general(left, right, (((1,), (1,)), ((), ())), preferred_element_type=F32)


def flip(block):
    return pltpu.roll(block, 64, 1)


def low_lanes(block):
    return lax.broadcasted_iota(jnp.int32, block.shape, 1) < 64


def split(block):
    high = block.astype(BF16).astype(F32)
    return high, block - high


def pair(block, upper):
    high, low = split(block)
    if upper:
        return jnp.where(low_lanes(block), flip(high), low)
    return jnp.where(low_lanes(block), high, flip(low))


def twice(block, upper):
    if upper:
        return jnp.where(low_lanes(block), flip(block), block)
    return jnp.where(low_lanes(block), block, flip(block))


def unfold(packed):
    return jnp.concatenate([packed, flip(packed)], axis=0)


def fold_halves(block):
    return block + flip(block)


def lanes_of(tile):
    return slice(tile * 128, (tile + 1) * 128)


def full_tile(seat):
    return 3 * (seat // 2) + 2 * (seat % 2)


def middle_tile(seat):
    return 3 * (seat // 2) + 1


def head_of(seat, h):
    return 6 * (seat // 2) + (2 + seat % 2 if h == 2 else 4 * (seat % 2) + h)


def kernel(
    q_in, k_in, v_in, g_in, w_in, valid_ref, offset_ref,
    full_got, half_got, last_got, far_note_got,
    q_own, k_own, v_own, w_own, half_in, half_seg, full_in, full_seg, g_seg,
    note, note_got, w_full, w_mid, w_hi, w_lo, far,
    q4, k4, v4, kt, vt, do4, do_t, attn_t, prob, prob_hi, prob_lo, ds_hi, ds_lo, g_hi, g_lo,
    far_part, far_got,
    wg_full, wg_full_1, wg_full_sum, wg_full_2, wg_mid, wg_mid_1, wg_mid_sum, wg_mid_2,
    last, far_note, dq_t, full_send, half_send,
    send_sem, recv_sem, local_sem,
):
    x = lax.axis_index("dp")
    s = lax.axis_index("seq")
    y = lax.div(s, 16)
    m = lax.rem(s, 16)
    z = lax.div(m, 2)
    c = lax.rem(s, 2)
    hz = lax.rem(z, 2)
    zz = lax.div(z, 2)
    t = lax.rem(s, 4)
    seg = lax.div(s, 4)

    def seat_of(d):
        core = c if d % 2 == 0 else 1 - c
        half = hz if d < 2 else 1 - hz
        return half * 2 + core

    def seg_peer(d):
        return (x, seg * 4 + seat_of(d))

    def ring_place(j):
        return lax.rem(m + j, 16)

    def ring_peer(j):
        return (x, y * 16 + ring_place(j))

    def y_place(j):
        return lax.rem(y + j, 4)

    def y_peer(j):
        return (x, y_place(j) * 16 + m)

    def x_place(j):
        return lax.rem(x + j, 4)

    def x_peer(j):
        return (x_place(j), s)

    class Group:
        count = 0

        def __init__(self, like, copies=()):
            self.like, self.index = like, Group.count
            Group.count += 1
            self.add(copies)

        def describe(self, src, dst, device):
            return pltpu.make_async_remote_copy(
                src_ref=src, dst_ref=dst, send_sem=send_sem.at[self.index],
                recv_sem=recv_sem.at[self.index], device_id=device, device_id_type=MESH,
            )

        def add(self, copies):
            for src, dst, device in copies:
                self.describe(src, dst, device).start()

        def arrive(self):
            self.describe(self.like, self.like, seg_peer(1)).wait_recv()

        def sent(self):
            self.describe(self.like, self.like, seg_peer(1)).wait_send()

    loads = []
    for src, dst in (
        (g_in, g_seg.at[t]), (k_in, k_own), (v_in, v_own), (w_in, w_own), (q_in, q_own),
    ):
        copy = pltpu.make_async_copy(src, dst, local_sem.at[len(loads)])
        copy.start()
        loads.append(copy)

    barrier = pltpu.get_barrier_semaphore()
    for device in (
        [ring_peer(j) for j in range(1, 16)]
        + [y_peer(j) for j in (1, 2, 3)]
        + [x_peer(j) for j in (1, 2, 3)]
    ):
        pl.semaphore_signal(barrier, inc=1, device_id=device, device_id_type=MESH)

    owns = (q_own, k_own, v_own)

    def deal(n):
        for tt in range(SEATS):
            full_in[tt, n] = owns[n][:, lanes_of(full_tile(tt))]
            top = owns[n][0:64, lanes_of(middle_tile(tt))]
            bottom = owns[n][64:128, lanes_of(middle_tile(tt))]
            if tt % 2 == 0:
                half_in[tt, n] = jnp.where(low_lanes(top), top, flip(bottom))
            else:
                half_in[tt, n] = jnp.where(low_lanes(top), flip(top), bottom)

    g_rows = ROWS // G_CHUNKS

    def g_part(seat, n):
        return g_seg.at[seat, pl.ds(n * g_rows, g_rows)]

    loads[0].wait()
    pl.semaphore_wait(barrier, 21)
    def send_across(n):
        return Group(g_part(0, n), [(g_part(t, n), g_part(t, n), seg_peer(2))])

    g_across = [send_across(n) for n in range(G_EARLY)]

    loads[1].wait()
    deal(1)
    loads[2].wait()
    deal(2)

    def long_rows(tt, h, n):
        offset = offset_ref[head_of(tt, h)]
        if h == 2:
            row = half_in[tt, n, pl.ds(offset, 1), :]
            return jnp.concatenate([row, flip(row)], axis=0)
        return jnp.concatenate(
            [full_in[tt, n, pl.ds(r * 64 + offset, 1), :] for r in range(2)], axis=0
        )

    loads[3].wait()
    for tt in range(SEATS):
        note[tt, 0:3, :] = w_own[:, lanes_of(full_tile(tt))]
        note[tt, 3:6, :] = w_own[:, lanes_of(middle_tile(tt))]
        for h in range(HEADS_HERE):
            key_rows, value_rows = long_rows(tt, h, 1), long_rows(tt, h, 2)
            low = low_lanes(key_rows)
            if h == 1:
                rows = jnp.where(low, flip(key_rows), value_rows)
            else:
                rows = jnp.where(low, key_rows, flip(value_rows))
            note[tt, 6 + 2 * h:8 + 2 * h, :] = rows

    notes = Group(
        note_got.at[pl.ds(0, 15)],
        [(note.at[lax.rem(ring_place(j), 4)], note_got.at[m], ring_peer(j)) for j in FAR_FIRST],
    )
    g_across += [send_across(n) for n in range(G_EARLY, G_CHUNKS)]
    note_got[m] = note[t]
    loads[4].wait()
    deal(0)
    full_in_moves = Group(
        full_seg.at[pl.ds(0, 3), pl.ds(0, 2)],
        [
            (full_in.at[seat_of(d), pl.ds(0, 2)], full_seg.at[t, pl.ds(0, 2)], seg_peer(d))
            for d in (2, 3, 1)
        ],
    )
    value_in_moves = Group(
        full_seg.at[pl.ds(0, 3), 2],
        [(full_in.at[seat_of(d), 2], full_seg.at[t, 2], seg_peer(d)) for d in (2, 3, 1)],
    )
    g_beside = Group(g_seg.at[0], [(g_seg.at[t], g_seg.at[t], seg_peer(1))])
    half_in_moves = Group(
        half_seg.at[pl.ds(0, 3), pl.ds(0, 2)],
        [
            (half_in.at[seat_of(d), pl.ds(0, 2)], half_seg.at[t, pl.ds(0, 2)], seg_peer(d))
            for d in (2, 3, 1)
        ],
    )
    half_value_moves = Group(
        half_seg.at[pl.ds(0, 3), 2],
        [(half_in.at[seat_of(d), 2], half_seg.at[t, 2], seg_peer(d)) for d in (2, 3, 1)],
    )
    half_seg[t] = half_in[t]
    full_seg[t] = full_in[t]

    notes.arrive()
    for mm in range(16):
        w_full[x, y, 3 * mm:3 * mm + 3, :] = note_got[mm, 0:3, :]
        w_mid[x, y, 3 * mm:3 * mm + 3, :] = note_got[mm, 3:6, :]
        for h in range(HEADS_HERE):
            far[y, h, 2 * mm:2 * mm + 2, :] = note_got[mm, 6 + 2 * h:8 + 2 * h, :]
    w_first = Group(
        w_full.at[pl.ds(0, 2), pl.ds(0, 3)],
        [(w_full.at[x, y], w_full.at[x, y], y_peer(j)) for j in (2, 1, 3)]
        + [(w_mid.at[x, y], w_mid.at[x, y], x_peer(j)) for j in (2, 1, 3)],
    )
    far_moves = Group(
        far.at[pl.ds(0, 3)], [(far.at[y], far.at[y], y_peer(j)) for j in (2, 1, 3)]
    )
    w_first.arrive()
    w_full_moves = Group(
        w_full.at[pl.ds(0, 3)], [(w_full.at[x], w_full.at[x], x_peer(j)) for j in (2, 1, 3)]
    )
    w_mid_moves = Group(
        w_mid.at[pl.ds(0, 3)], [(w_mid.at[:, y], w_mid.at[:, y], y_peer(j)) for j in (2, 1, 3)]
    )
    far_moves.arrive()

    def as_keys(h, rows, block, upper, four, transposed):
        high, low = split(block)
        four[h, rows, 0:128] = twice(high, upper).astype(BF16)
        four[h, rows, 128:256] = twice(low, upper).astype(BF16)
        transposed[h, :, rows] = pair(block, upper).T.astype(BF16)

    for h in range(HEADS_HERE):
        block = far[:, h].reshape(FAR, 128)
        as_keys(h, slice(SEG, KEYS), block, False, k4, kt)
        as_keys(h, slice(SEG, KEYS), block, True, v4, vt)

    valid = valid_ref[0]
    tile_row = lax.broadcasted_iota(jnp.int32, (ROWS, WIDTH), 0)

    def take_grad(seat):
        rows = pl.ds(pl.multiple_of(seat * ROWS, ROWS), ROWS)
        grad = jnp.where(seg * SEG + seat * ROWS + tile_row < valid, g_seg[seat], 0.0)
        high = grad.astype(BF16)
        g_hi[rows, :] = high
        g_lo[rows, :] = (grad - high.astype(F32)).astype(BF16)

    take_grad(t)
    g_beside.arrive()
    take_grad(seat_of(1))
    g_forwarded = Group(g_seg.at[0])
    for n in range(G_CHUNKS):
        g_across[n].arrive()
        part = g_part(seat_of(2), n)
        g_forwarded.add([(part, part, seg_peer(1))])
    take_grad(seat_of(2))

    w_full_moves.arrive()
    w_mid_moves.arrive()
    for tile, ref in ((0, w_full), (1, w_mid)):
        columns = ref[...].reshape(WIDTH, 128)
        if tile == 1:
            columns = jnp.where(c == 1, flip(columns), columns)
        high = columns.astype(BF16)
        w_hi[:, lanes_of(tile)] = high
        w_lo[:, lanes_of(tile)] = (columns - high.astype(F32)).astype(BF16)

    g_forwarded.arrive()
    take_grad(seat_of(3))
    for tt in range(SEATS):
        rows = slice(tt * 128, (tt + 1) * 128)
        high, low = g_hi[rows, :], g_lo[rows, :]
        out = dot(high, w_hi[...]) + dot(low, w_hi[...]) + dot(high, w_lo[...])
        full, middle = out[:, 0:128], out[:, 128:256]
        for h, block, upper in ((0, full, False), (1, full, True), (2, middle, False)):
            both = pair(block, upper).astype(BF16)
            do4[h, rows, 0:128] = both
            do4[h, rows, 128:256] = both
        turned = full.T
        do_t[0, :, rows] = turned[0:64]
        do_t[1, :, rows] = turned[64:128]
        do_t[2, :, rows] = middle.T[0:64]

    def as_queries(h, rows, block, upper):
        both = pair(block * 0.125, upper).astype(BF16)
        q4[h, rows, 0:128] = both
        q4[h, rows, 128:256] = both

    key_row = lax.broadcasted_iota(jnp.int32, (128, 256), 0)
    query_lane = lax.broadcasted_iota(jnp.int32, (128, 256), 1)

    def weights(h):
        head = 6 * hz + jnp.where(h == 2, 2 + c, 4 * c + h)
        offset = offset_ref[head]
        for qb in range(2):
            lanes = slice(qb * 256, (qb + 1) * 256)
            queries = q4[h, lanes, :]
            top = None
            for kb in range(5):
                rows = slice(kb * 128, (kb + 1) * 128)
                scores = dot_nt(k4[h, rows, :], queries)
                if kb < 4:
                    keep = (seg * SEG + kb * 128 + key_row < valid) | (
                        kb * 128 + key_row == qb * 256 + query_lane
                    )
                else:
                    keep = (key_row * SPACING + offset < valid) & (
                        lax.rem(query_lane, SPACING) == offset
                    )
                scores = jnp.where(keep, scores, MASKED)
                prob[h, rows, lanes] = scores
                here = jnp.max(scores, axis=0, keepdims=True)
                top = here if top is None else jnp.maximum(top, here)
            total = None
            for kb in range(5):
                rows = slice(kb * 128, (kb + 1) * 128)
                weight = jnp.exp(prob[h, rows, lanes] - top)
                prob[h, rows, lanes] = weight
                here = jnp.sum(weight, axis=0, keepdims=True)
                total = here if total is None else total + here
            scale = 1.0 / total
            for kb in range(5):
                rows = slice(kb * 128, (kb + 1) * 128)
                p = prob[h, rows, lanes] * scale
                prob[h, rows, lanes] = p
                high = p.astype(BF16)
                prob_hi[h, rows, lanes] = high
                prob_lo[h, rows, lanes] = (p - high.astype(F32)).astype(BF16)

    def attention(h):
        for qb in range(2):
            lanes = slice(qb * 256, (qb + 1) * 256)
            out = dot(vt[h], prob_hi[h, :, lanes]) + dot(vt[h], prob_lo[h, :, lanes])
            attn_t[h, :, lanes] = out[0:64] + out[64:128]

    def value_grad(h):
        grads = do4[h, :, 0:128]
        return fold_halves(dot(prob_hi[h], grads) + dot(prob_lo[h], grads))

    def key_grad(h):
        queries = q4[h, :, 0:128]
        return fold_halves(dot(ds_hi[h], queries) + dot(ds_lo[h], queries))

    def score_grad(h):
        for qb in range(2):
            lanes = slice(qb * 256, (qb + 1) * 256)
            delta = jnp.sum(attn_t[h, :, lanes] * do_t[h, :, lanes], axis=0, keepdims=True)
            for kb in range(5):
                rows = slice(kb * 128, (kb + 1) * 128)
                d_prob = dot_nt(v4[h, rows, :], do4[h, lanes, :])
                ds = prob[h, rows, lanes] * (d_prob - delta)
                high = ds.astype(BF16)
                ds_hi[h, rows, lanes] = high
                ds_lo[h, rows, lanes] = (ds - high.astype(F32)).astype(BF16)

    def query_grad(h):
        turned = dot(kt[h], ds_hi[h]) + dot(kt[h], ds_lo[h])
        dq_t[h] = (turned[0:64] + turned[64:128]) * 0.125

    def weight_grad(attn):
        high = attn.astype(BF16)
        low = (attn - high.astype(F32)).astype(BF16)
        return dot(high, g_hi[...]) + dot(low, g_hi[...]) + dot(high, g_lo[...])

    def far_grad(h, d_key, d_value):
        d_key, d_value = d_key[SEG:KEYS], d_value[SEG:KEYS]
        block = jnp.where(low_lanes(d_key), d_key, d_value)
        far_part[:, h] = block.reshape(4, 32, 128)

    def sum_first(parts, got):
        return Group(
            got,
            [(parts.at[0, x_place(j)], got.at[0, j - 1], x_peer(j)) for j in (2, 1, 3)]
            + [(parts.at[1, :, y_place(j)], got.at[1, j - 1], y_peer(j)) for j in (2, 1, 3)],
        )

    def sum_second(parts, got, sums, got_next):
        sums[0] = parts[0, x] + got[0, 0] + got[0, 1] + got[0, 2]
        sums[1] = parts[1, :, y] + got[1, 0] + got[1, 1] + got[1, 2]
        return Group(
            got_next,
            [(sums.at[0, y_place(j)], got_next.at[0, j - 1], y_peer(j)) for j in (2, 1, 3)]
            + [(sums.at[1, x_place(j)], got_next.at[1, j - 1], x_peer(j)) for j in (2, 1, 3)],
        )

    def sum_last(sums, got_next):
        return (
            sums[0, y] + got_next[0, 0] + got_next[0, 1] + got_next[0, 2],
            sums[1, x] + got_next[1, 0] + got_next[1, 1] + got_next[1, 2],
        )

    for group in [notes, w_first, far_moves, g_beside] + g_across:
        group.sent()
    full_in_moves.arrive()
    for tt in range(SEATS):
        rows = slice(tt * 128, (tt + 1) * 128)
        for h in range(2):
            as_queries(h, rows, full_seg[tt, 0], h == 1)
            as_keys(h, rows, full_seg[tt, 1], h == 1, k4, kt)
    weights(0)
    weights(1)
    value_in_moves.arrive()
    for tt in range(SEATS):
        rows = slice(tt * 128, (tt + 1) * 128)
        for h in range(2):
            as_keys(h, rows, full_seg[tt, 2], h == 1, v4, vt)
    attention(0)
    attention(1)
    turned = weight_grad(attn_t[0:2].reshape(128, SEG))
    for xx in range(X):
        block = turned[:, xx * 192:(xx + 1) * 192].T
        for yy in range(4):
            for n in range(2):
                wg_full[n, xx, yy] = block[yy * 48 + n * 24:yy * 48 + n * 24 + 24]
    wg_first = sum_first(wg_full, wg_full_1)

    full_out = Group(full_got.at[pl.ds(0, 3)])
    own_out = []

    def keep_own(src, dst):
        copy = pltpu.make_async_copy(src, dst, local_sem.at[5 + len(own_out)])
        copy.start()
        own_out.append(copy)

    def send_full(n):
        full_out.add(
            (full_send.at[seat_of(d), n], full_got.at[t, n], seg_peer(d)) for d in (2, 3, 1)
        )
        keep_own(full_send.at[t, n], full_got.at[t, n])

    def both_heads(low, high, n):
        block = jnp.where(low_lanes(low), low, high)
        for tt in range(SEATS):
            full_send[tt, n] = block[tt * 128:(tt + 1) * 128]
        send_full(n)

    values_0, values_1 = value_grad(0), value_grad(1)
    both_heads(values_0, values_1, 2)
    score_grad(0)
    score_grad(1)
    keys_0, keys_1 = key_grad(0), key_grad(1)
    both_heads(keys_0, keys_1, 1)
    far_grad(0, keys_0, values_0)
    far_grad(1, keys_1, values_1)
    far_out = Group(
        far_got,
        [
            (far_part.at[y_place(j), pl.ds(0, 2)], far_got.at[j - 1, pl.ds(0, 2)], y_peer(j))
            for j in (2, 1, 3)
        ],
    )

    half_in_moves.arrive()
    for tt in range(SEATS):
        rows = slice(tt * 128, (tt + 1) * 128)
        as_queries(2, rows, unfold(half_seg[tt, 0]), False)
        as_keys(2, rows, unfold(half_seg[tt, 1]), False, k4, kt)
    weights(2)
    half_value_moves.arrive()
    for tt in range(SEATS):
        rows = slice(tt * 128, (tt + 1) * 128)
        as_keys(2, rows, unfold(half_seg[tt, 2]), False, v4, vt)
    attention(2)
    turned = weight_grad(attn_t[2])
    turned = jnp.concatenate([turned, turned], axis=0)
    for xx in range(X):
        block = turned[:, xx * 192:(xx + 1) * 192].T
        for yy in range(4):
            top, bottom = block[yy * 48:yy * 48 + 24], block[yy * 48 + 24:yy * 48 + 48]
            packed = jnp.where(low_lanes(top), top, bottom)
            wg_mid[0, xx, yy] = packed[0:12]
            wg_mid[1, xx, yy] = packed[12:24]

    mid_first = sum_first(wg_mid, wg_mid_1)
    query_grad(0)
    query_grad(1)
    for tt in range(SEATS):
        full_send[tt, 0] = dq_t[0:2, :, tt * 128:(tt + 1) * 128].reshape(128, 128).T
    send_full(0)
    wg_first.arrive()
    wg_second = sum_second(wg_full, wg_full_1, wg_full_sum, wg_full_2)
    d_value = value_grad(2)
    score_grad(2)
    d_key = key_grad(2)
    far_grad(2, d_key, d_value)
    far_out.add(
        (far_part.at[y_place(j), pl.ds(2, 1)], far_got.at[j - 1, pl.ds(2, 1)], y_peer(j))
        for j in (2, 1, 3)
    )
    mid_first.arrive()
    mid_second = sum_second(wg_mid, wg_mid_1, wg_mid_sum, wg_mid_2)
    query_grad(2)
    for tt in range(SEATS):
        block = dq_t[2, :, tt * 128:(tt + 1) * 128]
        block = jnp.concatenate([block, block], axis=0).T
        low = low_lanes(block[0:64])
        half_send[tt, 0] = jnp.where(low, block[0:64], block[64:128])
        for n, part in ((1, d_key), (2, d_value)):
            top, bottom = part[tt * 128:tt * 128 + 64], part[tt * 128 + 64:tt * 128 + 128]
            half_send[tt, n] = jnp.where(low, top, bottom)

    def to_owners(notes, got):
        return Group(
            got.at[pl.ds(0, 15)],
            [(notes.at[ring_place(j)], got.at[m], ring_peer(j)) for j in FAR_FIRST],
        )

    wg_second.arrive()
    parts = sum_last(wg_full_sum, wg_full_2)
    for mm in range(16):
        last[mm, 0:3, :] = parts[mm // 8][3 * (mm % 8):3 * (mm % 8) + 3]
    far_out.arrive()
    for h in range(HEADS_HERE):
        rows = far_part[y, h] + far_got[0, h] + far_got[1, h] + far_got[2, h]
        for mm in range(16):
            far_note[mm, 2 * h:2 * h + 2, :] = rows[2 * mm:2 * mm + 2]
    far_last = to_owners(far_note, far_note_got)
    mid_second.arrive()
    parts = sum_last(wg_mid_sum, wg_mid_2)
    for mm in range(16):
        rows = parts[mm // 4 % 2]
        last[mm, 3:6, :] = (rows if mm < 8 else flip(rows))[3 * (mm % 4):3 * (mm % 4) + 3]
    last_moves = to_owners(last, last_got)
    half_out = Group(
        half_got.at[pl.ds(0, 3)],
        [(half_send.at[seat_of(d)], half_got.at[t], seg_peer(d)) for d in (2, 3, 1)],
    )
    keep_own(half_send.at[t], half_got.at[t])
    keep_own(last.at[m], last_got.at[m])
    keep_own(far_note.at[m], far_note_got.at[m])

    for group in (
        w_full_moves, w_mid_moves, g_forwarded, full_in_moves, value_in_moves, half_in_moves,
        half_value_moves, wg_first, mid_first, wg_second, far_out, mid_second, full_out,
    ):
        group.sent()
    full_out.arrive()
    for copy in own_out:
        copy.wait()
    for group in (far_last, last_moves, half_out):
        group.sent()
        group.arrive()


def put_together(
    full_got, half_got, last_got, far_got, offset_ref, dq_out, dk_out, dv_out, wg_out,
    dq_own, dk_own, dv_own, wg_own, out_sem,
):
    stores = [
        pltpu.make_async_copy(src, dst, out_sem.at[n])
        for n, (src, dst) in enumerate(
            ((dq_own, dq_out), (dk_own, dk_out), (dv_own, dv_out), (wg_own, wg_out))
        )
    ]
    row64 = lax.broadcasted_iota(jnp.int32, (64, 128), 0)
    low64 = lax.broadcasted_iota(jnp.int32, (64, 128), 1) < 64
    outs = (dq_own, dk_own, dv_own)
    far_rows, wg_rows = [
        [got[tt] + got[4 + tt] + got[8 + tt] + got[12 + tt] for tt in range(SEATS)]
        for got in (far_got, last_got)
    ]

    def with_extra(n, r, tt, h, upper, block):
        if n == 0:
            return block
        row = far_rows[tt][2 * h + r:2 * h + r + 1]
        if (n == 2) != upper:
            row = flip(row)
        keep = (row64 == offset_ref[head_of(tt, h)]) & (low64 != upper)
        return block + jnp.where(keep, jnp.broadcast_to(row, (64, 128)), 0.0)

    for n in range(3):
        for half in range(2):
            even, odd = half_got[2 * half, n], half_got[2 * half + 1, n]
            for r in range(2):
                if r == 0:
                    block = jnp.where(low64, even, flip(odd))
                else:
                    block = jnp.where(low64, flip(even), odd)
                block = with_extra(n, r, 2 * half, 2, False, block)
                block = with_extra(n, r, 2 * half + 1, 2, True, block)
                outs[n][r * 64:(r + 1) * 64, lanes_of(3 * half + 1)] = block
        for tt in range(SEATS):
            for r in range(2):
                block = full_got[tt, n, r * 64:(r + 1) * 64, :]
                block = with_extra(n, r, tt, 0, False, block)
                block = with_extra(n, r, tt, 1, True, block)
                outs[n][r * 64:(r + 1) * 64, lanes_of(full_tile(tt))] = block
        stores[n].start()

    scale = 8192.0 ** -0.5
    for tt in range(SEATS):
        wg_own[:, lanes_of(full_tile(tt))] = wg_rows[tt][0:3] * scale
    for half in range(2):
        even, odd = wg_rows[2 * half][3:6], wg_rows[2 * half + 1][3:6]
        wg_own[:, lanes_of(3 * half + 1)] = jnp.where(low_lanes(even), even, flip(odd)) * scale
    stores[3].start()
    for copy in stores:
        copy.wait()


def on_device(queries, keys, values, out_grad, out_weight, valid_tiles, head_offsets):
    def block(*shape):
        return pltpu.VMEM(shape, F32)

    def half(*shape):
        return pltpu.VMEM(shape, BF16)

    scratch = [
        block(ROWS, WIDTH), block(ROWS, WIDTH), block(ROWS, WIDTH), block(3, WIDTH),
        block(4, 3, 64, 128), block(4, 3, 64, 128), block(4, 3, 128, 128), block(4, 3, 128, 128),
        block(4, ROWS, WIDTH),
        block(4, 12, 128), block(16, 12, 128),
        block(4, 4, 48, 128), block(4, 4, 48, 128), half(WIDTH, 256), half(WIDTH, 256),
        block(4, 3, 32, 128),
        half(3, SEG, 256), half(3, KEYS, 256), half(3, KEYS, 256),
        half(3, 128, KEYS), half(3, 128, KEYS),
        half(3, SEG, 256), block(3, 64, SEG), block(3, 64, SEG),
        block(3, KEYS, SEG), half(3, KEYS, SEG), half(3, KEYS, SEG),
        half(3, KEYS, SEG), half(3, KEYS, SEG),
        half(SEG, WIDTH), half(SEG, WIDTH),
        block(4, 3, 32, 128), block(3, 3, 32, 128),
        block(2, 4, 4, 24, 128), block(2, 3, 4, 24, 128), block(2, 4, 24, 128), block(2, 3, 24, 128),
        block(2, 4, 4, 12, 128), block(2, 3, 4, 12, 128), block(2, 4, 12, 128), block(2, 3, 12, 128),
        block(16, 6, 128), block(16, 6, 128), block(3, 64, SEG),
        block(4, 3, 128, 128), block(4, 3, 64, 128),
        pltpu.SemaphoreType.DMA((SENDS,)), pltpu.SemaphoreType.DMA((SENDS,)),
        pltpu.SemaphoreType.DMA((11,)),
    ]
    whole = pl.BlockSpec(memory_space=pltpu.HBM)
    scalars = pl.BlockSpec(memory_space=pltpu.SMEM)
    rows = jax.ShapeDtypeStruct((ROWS, WIDTH), F32)
    blocks = [
        pltpu.with_memory_space_constraint(array, pltpu.HBM)
        for array in (queries[0], keys[0], values[0], out_grad[0], out_weight)
    ]
    head_offsets = pltpu.with_memory_space_constraint(head_offsets, pltpu.HBM)
    got = pl.pallas_call(
        kernel,
        out_shape=(
            jax.ShapeDtypeStruct((4, 3, 128, 128), F32),
            jax.ShapeDtypeStruct((4, 3, 64, 128), F32),
            jax.ShapeDtypeStruct((16, 6, 128), F32),
            jax.ShapeDtypeStruct((16, 6, 128), F32),
        ),
        in_specs=[whole] * 5 + [scalars] * 2,
        out_specs=(whole,) * 4,
        scratch_shapes=scratch,
        compiler_params=pltpu.CompilerParams(
            collective_id=0, has_side_effects=True, vmem_limit_bytes=48 * 1024 * 1024
        ),
        cost_estimate=pl.CostEstimate(
            flops=4_000_000_000, bytes_accessed=4_000_000, transcendentals=1_000_000
        ),
        name="dilated_backward",
    )(*blocks, valid_tiles, head_offsets)
    d_query, d_key, d_value, d_weight = pl.pallas_call(
        put_together,
        out_shape=(rows, rows, rows, jax.ShapeDtypeStruct((3, WIDTH), F32)),
        in_specs=[pl.BlockSpec(memory_space=pltpu.VMEM)] * 4 + [scalars],
        out_specs=(whole,) * 4,
        scratch_shapes=[
            block(ROWS, WIDTH), block(ROWS, WIDTH), block(ROWS, WIDTH), block(3, WIDTH),
            pltpu.SemaphoreType.DMA((4,)),
        ],
        compiler_params=pltpu.CompilerParams(vmem_limit_bytes=16 * 1024 * 1024),
        cost_estimate=pl.CostEstimate(flops=1_000_000, bytes_accessed=2_500_000, transcendentals=0),
        name="put_together",
    )(*got, head_offsets)
    return d_query[None], d_key[None], d_value[None], d_weight


def solution(mesh):
    from jax.sharding import PartitionSpec as P

    tiles = P("dp", "seq", None)
    weight = P(("dp", "seq"), None)
    return jax.shard_map(
        on_device,
        mesh=mesh,
        in_specs=(tiles, tiles, tiles, tiles, weight, P("dp"), P()),
        out_specs=(tiles, tiles, tiles, weight),
        check_vma=False,
    )
```

```python
import jax
import jax.numpy as jnp
from jax import lax
from jax.experimental import pallas as pl
from jax.experimental.pallas import tpu as pltpu

F32 = jnp.float32
BF16 = jnp.bfloat16
MASKED = -1e30
MESH = pl.DeviceIdType.MESH

X = 4
ROWS = 128
SEATS = 4
SEG = ROWS * SEATS
SPACING = 64
FAR = 128
WIDTH = 768
HEADS_HERE = 3
KEYS = SEG + FAR
G_CHUNKS = 4
G_EARLY = 1
FAR_FIRST = (8, 7, 9, 6, 10, 5, 11, 4, 12, 3, 13, 2, 14, 1, 15)
SENDS = 32


def dot(left, right):
    return lax.dot_general(left, right, (((1,), (0,)), ((), ())), preferred_element_type=F32)


def dot_nt(left, right):
    return lax.dot_general(left, right, (((1,), (1,)), ((), ())), preferred_element_type=F32)


def flip(block):
    return pltpu.roll(block, 64, 1)


def low_lanes(block):
    return lax.broadcasted_iota(jnp.int32, block.shape, 1) < 64


def split(block):
    high = block.astype(BF16).astype(F32)
    return high, block - high


def pair(block, upper):
    high, low = split(block)
    if upper:
        return jnp.where(low_lanes(block), flip(high), low)
    return jnp.where(low_lanes(block), high, flip(low))


def twice(block, upper):
    if upper:
        return jnp.where(low_lanes(block), flip(block), block)
    return jnp.where(low_lanes(block), block, flip(block))


def unfold(packed):
    return jnp.concatenate([packed, flip(packed)], axis=0)


def fold_halves(block):
    return block + flip(block)


def lanes_of(tile):
    return slice(tile * 128, (tile + 1) * 128)


def full_tile(seat):
    return 3 * (seat // 2) + 2 * (seat % 2)


def middle_tile(seat):
    return 3 * (seat // 2) + 1


def head_of(seat, h):
    return 6 * (seat // 2) + (2 + seat % 2 if h == 2 else 4 * (seat % 2) + h)


def kernel(
    q_in, k_in, v_in, g_in, w_in, valid_ref, offset_ref,
    full_got, half_got, last_got, far_note_got,
    q_own, k_own, v_own, w_own, half_in, half_seg, full_in, full_seg, g_seg,
    note, note_got, w_full, w_mid, w_hi, w_lo, far,
    q4, k4, v4, kt, vt, do4, do_t, attn_t, prob, prob_hi, prob_lo, ds_hi, ds_lo, g_hi, g_lo,
    far_part, far_got,
    wg_full, wg_full_1, wg_full_sum, wg_full_2, wg_mid, wg_mid_1, wg_mid_sum, wg_mid_2,
    last, far_note, dq_t, full_send, half_send,
    send_sem, recv_sem, local_sem,
):
    x = lax.axis_index("dp")
    s = lax.axis_index("seq")
    y = lax.div(s, 16)
    m = lax.rem(s, 16)
    z = lax.div(m, 2)
    c = lax.rem(s, 2)
    hz = lax.rem(z, 2)
    zz = lax.div(z, 2)
    t = lax.rem(s, 4)
    seg = lax.div(s, 4)

    def seat_of(d):
        core = c if d % 2 == 0 else 1 - c
        half = hz if d < 2 else 1 - hz
        return half * 2 + core

    def seg_peer(d):
        return (x, seg * 4 + seat_of(d))

    def ring_place(j):
        return lax.rem(m + j, 16)

    def ring_peer(j):
        return (x, y * 16 + ring_place(j))

    def y_place(j):
        return lax.rem(y + j, 4)

    def y_peer(j):
        return (x, y_place(j) * 16 + m)

    def x_place(j):
        return lax.rem(x + j, 4)

    def x_peer(j):
        return (x_place(j), s)

    class Group:
        count = 0

        def __init__(self, like, copies=()):
            self.like, self.index = like, Group.count
            Group.count += 1
            self.add(copies)

        def describe(self, src, dst, device):
            return pltpu.make_async_remote_copy(
                src_ref=src, dst_ref=dst, send_sem=send_sem.at[self.index],
                recv_sem=recv_sem.at[self.index], device_id=device, device_id_type=MESH,
            )

        def add(self, copies):
            for src, dst, device in copies:
                self.describe(src, dst, device).start()

        def arrive(self):
            self.describe(self.like, self.like, seg_peer(1)).wait_recv()

        def sent(self):
            self.describe(self.like, self.like, seg_peer(1)).wait_send()

    loads = []
    for src, dst in (
        (g_in, g_seg.at[t]), (k_in, k_own), (v_in, v_own), (w_in, w_own), (q_in, q_own),
    ):
        copy = pltpu.make_async_copy(src, dst, local_sem.at[len(loads)])
        copy.start()
        loads.append(copy)

    barrier = pltpu.get_barrier_semaphore()
    for device in (
        [ring_peer(j) for j in range(1, 16)]
        + [y_peer(j) for j in (1, 2, 3)]
        + [x_peer(j) for j in (1, 2, 3)]
    ):
        pl.semaphore_signal(barrier, inc=1, device_id=device, device_id_type=MESH)

    owns = (q_own, k_own, v_own)

    def deal(n):
        for tt in range(SEATS):
            full_in[tt, n] = owns[n][:, lanes_of(full_tile(tt))]
            top = owns[n][0:64, lanes_of(middle_tile(tt))]
            bottom = owns[n][64:128, lanes_of(middle_tile(tt))]
            if tt % 2 == 0:
                half_in[tt, n] = jnp.where(low_lanes(top), top, flip(bottom))
            else:
                half_in[tt, n] = jnp.where(low_lanes(top), flip(top), bottom)

    g_rows = ROWS // G_CHUNKS

    def g_part(seat, n):
        return g_seg.at[seat, pl.ds(n * g_rows, g_rows)]

    loads[0].wait()
    pl.semaphore_wait(barrier, 21)
    def send_across(n):
        return Group(g_part(0, n), [(g_part(t, n), g_part(t, n), seg_peer(2))])

    g_across = [send_across(n) for n in range(G_EARLY)]

    loads[1].wait()
    deal(1)
    loads[2].wait()
    deal(2)

    def long_rows(tt, h, n):
        offset = offset_ref[head_of(tt, h)]
        if h == 2:
            row = half_in[tt, n, pl.ds(offset, 1), :]
            return jnp.concatenate([row, flip(row)], axis=0)
        return jnp.concatenate(
            [full_in[tt, n, pl.ds(r * 64 + offset, 1), :] for r in range(2)], axis=0
        )

    loads[3].wait()
    for tt in range(SEATS):
        note[tt, 0:3, :] = w_own[:, lanes_of(full_tile(tt))]
        note[tt, 3:6, :] = w_own[:, lanes_of(middle_tile(tt))]
        for h in range(HEADS_HERE):
            key_rows, value_rows = long_rows(tt, h, 1), long_rows(tt, h, 2)
            low = low_lanes(key_rows)
            if h == 1:
                rows = jnp.where(low, flip(key_rows), value_rows)
            else:
                rows = jnp.where(low, key_rows, flip(value_rows))
            note[tt, 6 + 2 * h:8 + 2 * h, :] = rows

    notes = Group(
        note_got.at[pl.ds(0, 15)],
        [(note.at[lax.rem(ring_place(j), 4)], note_got.at[m], ring_peer(j)) for j in FAR_FIRST],
    )
    g_across += [send_across(n) for n in range(G_EARLY, G_CHUNKS)]
    note_got[m] = note[t]
    loads[4].wait()
    deal(0)
    full_in_moves = Group(
        full_seg.at[pl.ds(0, 3), pl.ds(0, 2)],
        [
            (full_in.at[seat_of(d), pl.ds(0, 2)], full_seg.at[t, pl.ds(0, 2)], seg_peer(d))
            for d in (2, 3, 1)
        ],
    )
    value_in_moves = Group(
        full_seg.at[pl.ds(0, 3), 2],
        [(full_in.at[seat_of(d), 2], full_seg.at[t, 2], seg_peer(d)) for d in (2, 3, 1)],
    )
    g_beside = Group(g_seg.at[0], [(g_seg.at[t], g_seg.at[t], seg_peer(1))])
    half_in_moves = Group(
        half_seg.at[pl.ds(0, 3), pl.ds(0, 2)],
        [
            (half_in.at[seat_of(d), pl.ds(0, 2)], half_seg.at[t, pl.ds(0, 2)], seg_peer(d))
            for d in (2, 3, 1)
        ],
    )
    half_value_moves = Group(
        half_seg.at[pl.ds(0, 3), 2],
        [(half_in.at[seat_of(d), 2], half_seg.at[t, 2], seg_peer(d)) for d in (2, 3, 1)],
    )
    half_seg[t] = half_in[t]
    full_seg[t] = full_in[t]

    notes.arrive()
    for mm in range(16):
        w_full[x, y, 3 * mm:3 * mm + 3, :] = note_got[mm, 0:3, :]
        w_mid[x, y, 3 * mm:3 * mm + 3, :] = note_got[mm, 3:6, :]
        for h in range(HEADS_HERE):
            far[y, h, 2 * mm:2 * mm + 2, :] = note_got[mm, 6 + 2 * h:8 + 2 * h, :]
    w_first = Group(
        w_full.at[pl.ds(0, 2), pl.ds(0, 3)],
        [(w_full.at[x, y], w_full.at[x, y], y_peer(j)) for j in (2, 1, 3)]
        + [(w_mid.at[x, y], w_mid.at[x, y], x_peer(j)) for j in (2, 1, 3)],
    )
    far_moves = Group(
        far.at[pl.ds(0, 3)], [(far.at[y], far.at[y], y_peer(j)) for j in (2, 1, 3)]
    )
    w_first.arrive()
    w_full_moves = Group(
        w_full.at[pl.ds(0, 3)], [(w_full.at[x], w_full.at[x], x_peer(j)) for j in (2, 1, 3)]
    )
    w_mid_moves = Group(
        w_mid.at[pl.ds(0, 3)], [(w_mid.at[:, y], w_mid.at[:, y], y_peer(j)) for j in (2, 1, 3)]
    )
    far_moves.arrive()

    def as_keys(h, rows, block, upper, four, transposed):
        high, low = split(block)
        four[h, rows, 0:128] = twice(high, upper).astype(BF16)
        four[h, rows, 128:256] = twice(low, upper).astype(BF16)
        transposed[h, :, rows] = pair(block, upper).T.astype(BF16)

    for h in range(HEADS_HERE):
        block = far[:, h].reshape(FAR, 128)
        as_keys(h, slice(SEG, KEYS), block, False, k4, kt)
        as_keys(h, slice(SEG, KEYS), block, True, v4, vt)

    valid = valid_ref[0]
    tile_row = lax.broadcasted_iota(jnp.int32, (ROWS, WIDTH), 0)

    def take_grad(seat):
        rows = pl.ds(pl.multiple_of(seat * ROWS, ROWS), ROWS)
        grad = jnp.where(seg * SEG + seat * ROWS + tile_row < valid, g_seg[seat], 0.0)
        high = grad.astype(BF16)
        g_hi[rows, :] = high
        g_lo[rows, :] = (grad - high.astype(F32)).astype(BF16)

    take_grad(t)
    g_beside.arrive()
    take_grad(seat_of(1))
    g_forwarded = Group(g_seg.at[0])
    for n in range(G_CHUNKS):
        g_across[n].arrive()
        part = g_part(seat_of(2), n)
        g_forwarded.add([(part, part, seg_peer(1))])
    take_grad(seat_of(2))

    g_forwarded.arrive()
    take_grad(seat_of(3))
    def as_queries(h, rows, block, upper):
        both = pair(block * 0.125, upper).astype(BF16)
        q4[h, rows, 0:128] = both
        q4[h, rows, 128:256] = both

    key_row = lax.broadcasted_iota(jnp.int32, (128, 256), 0)
    query_lane = lax.broadcasted_iota(jnp.int32, (128, 256), 1)

    def weights(h):
        head = 6 * hz + jnp.where(h == 2, 2 + c, 4 * c + h)
        offset = offset_ref[head]
        for qb in range(2):
            lanes = slice(qb * 256, (qb + 1) * 256)
            queries = q4[h, lanes, :]
            top = None
            for kb in range(5):
                rows = slice(kb * 128, (kb + 1) * 128)
                scores = dot_nt(k4[h, rows, :], queries)
                if kb < 4:
                    keep = (seg * SEG + kb * 128 + key_row < valid) | (
                        kb * 128 + key_row == qb * 256 + query_lane
                    )
                else:
                    keep = (key_row * SPACING + offset < valid) & (
                        lax.rem(query_lane, SPACING) == offset
                    )
                scores = jnp.where(keep, scores, MASKED)
                prob[h, rows, lanes] = scores
                here = jnp.max(scores, axis=0, keepdims=True)
                top = here if top is None else jnp.maximum(top, here)
            total = None
            for kb in range(5):
                rows = slice(kb * 128, (kb + 1) * 128)
                weight = jnp.exp(prob[h, rows, lanes] - top)
                prob[h, rows, lanes] = weight
                here = jnp.sum(weight, axis=0, keepdims=True)
                total = here if total is None else total + here
            scale = 1.0 / total
            for kb in range(5):
                rows = slice(kb * 128, (kb + 1) * 128)
                p = prob[h, rows, lanes] * scale
                prob[h, rows, lanes] = p
                high = p.astype(BF16)
                prob_hi[h, rows, lanes] = high
                prob_lo[h, rows, lanes] = (p - high.astype(F32)).astype(BF16)

    def attention(h):
        for qb in range(2):
            lanes = slice(qb * 256, (qb + 1) * 256)
            out = dot(vt[h], prob_hi[h, :, lanes]) + dot(vt[h], prob_lo[h, :, lanes])
            attn_t[h, :, lanes] = out[0:64] + out[64:128]

    def value_grad(h):
        grads = do4[h, :, 0:128]
        return fold_halves(dot(prob_hi[h], grads) + dot(prob_lo[h], grads))

    def key_grad(h):
        queries = q4[h, :, 0:128]
        return fold_halves(dot(ds_hi[h], queries) + dot(ds_lo[h], queries))

    def score_grad(h):
        for qb in range(2):
            lanes = slice(qb * 256, (qb + 1) * 256)
            delta = jnp.sum(attn_t[h, :, lanes] * do_t[h, :, lanes], axis=0, keepdims=True)
            for kb in range(5):
                rows = slice(kb * 128, (kb + 1) * 128)
                d_prob = dot_nt(v4[h, rows, :], do4[h, lanes, :])
                ds = prob[h, rows, lanes] * (d_prob - delta)
                high = ds.astype(BF16)
                ds_hi[h, rows, lanes] = high
                ds_lo[h, rows, lanes] = (ds - high.astype(F32)).astype(BF16)

    def query_grad(h):
        turned = dot(kt[h], ds_hi[h]) + dot(kt[h], ds_lo[h])
        dq_t[h] = (turned[0:64] + turned[64:128]) * 0.125

    def weight_grad(attn):
        high = attn.astype(BF16)
        low = (attn - high.astype(F32)).astype(BF16)
        return dot(high, g_hi[...]) + dot(low, g_hi[...]) + dot(high, g_lo[...])

    def far_grad(h, d_key, d_value):
        d_key, d_value = d_key[SEG:KEYS], d_value[SEG:KEYS]
        block = jnp.where(low_lanes(d_key), d_key, d_value)
        far_part[:, h] = block.reshape(4, 32, 128)

    def sum_first(parts, got):
        return Group(
            got,
            [(parts.at[0, x_place(j)], got.at[0, j - 1], x_peer(j)) for j in (2, 1, 3)]
            + [(parts.at[1, :, y_place(j)], got.at[1, j - 1], y_peer(j)) for j in (2, 1, 3)],
        )

    def sum_second(parts, got, sums, got_next):
        sums[0] = parts[0, x] + got[0, 0] + got[0, 1] + got[0, 2]
        sums[1] = parts[1, :, y] + got[1, 0] + got[1, 1] + got[1, 2]
        return Group(
            got_next,
            [(sums.at[0, y_place(j)], got_next.at[0, j - 1], y_peer(j)) for j in (2, 1, 3)]
            + [(sums.at[1, x_place(j)], got_next.at[1, j - 1], x_peer(j)) for j in (2, 1, 3)],
        )

    def sum_last(sums, got_next):
        return (
            sums[0, y] + got_next[0, 0] + got_next[0, 1] + got_next[0, 2],
            sums[1, x] + got_next[1, 0] + got_next[1, 1] + got_next[1, 2],
        )

    for group in [notes, w_first, far_moves, g_beside] + g_across:
        group.sent()
    full_in_moves.arrive()
    for tt in range(SEATS):
        rows = slice(tt * 128, (tt + 1) * 128)
        for h in range(2):
            as_queries(h, rows, full_seg[tt, 0], h == 1)
            as_keys(h, rows, full_seg[tt, 1], h == 1, k4, kt)
    weights(0)
    weights(1)
    value_in_moves.arrive()
    for tt in range(SEATS):
        rows = slice(tt * 128, (tt + 1) * 128)
        for h in range(2):
            as_keys(h, rows, full_seg[tt, 2], h == 1, v4, vt)
    attention(0)
    attention(1)
    turned = weight_grad(attn_t[0:2].reshape(128, SEG))
    for xx in range(X):
        block = turned[:, xx * 192:(xx + 1) * 192].T
        for yy in range(4):
            for n in range(2):
                wg_full[n, xx, yy] = block[yy * 48 + n * 24:yy * 48 + n * 24 + 24]
    wg_first = sum_first(wg_full, wg_full_1)

    w_full_moves.arrive()
    w_mid_moves.arrive()
    for tile, ref in ((0, w_full), (1, w_mid)):
        columns = ref[...].reshape(WIDTH, 128)
        if tile == 1:
            columns = jnp.where(c == 1, flip(columns), columns)
        high = columns.astype(BF16)
        w_hi[:, lanes_of(tile)] = high
        w_lo[:, lanes_of(tile)] = (columns - high.astype(F32)).astype(BF16)

    for tt in range(SEATS):
        rows = slice(tt * 128, (tt + 1) * 128)
        high, low = g_hi[rows, :], g_lo[rows, :]
        out = dot(high, w_hi[...]) + dot(low, w_hi[...]) + dot(high, w_lo[...])
        full, middle = out[:, 0:128], out[:, 128:256]
        for h, block, upper in ((0, full, False), (1, full, True), (2, middle, False)):
            both = pair(block, upper).astype(BF16)
            do4[h, rows, 0:128] = both
            do4[h, rows, 128:256] = both
        turned = full.T
        do_t[0, :, rows] = turned[0:64]
        do_t[1, :, rows] = turned[64:128]
        do_t[2, :, rows] = middle.T[0:64]

    full_out = Group(full_got.at[pl.ds(0, 3)])
    own_out = []

    def keep_own(src, dst):
        copy = pltpu.make_async_copy(src, dst, local_sem.at[5 + len(own_out)])
        copy.start()
        own_out.append(copy)

    def send_full(n):
        full_out.add(
            (full_send.at[seat_of(d), n], full_got.at[t, n], seg_peer(d)) for d in (2, 3, 1)
        )
        keep_own(full_send.at[t, n], full_got.at[t, n])

    def both_heads(low, high, n):
        block = jnp.where(low_lanes(low), low, high)
        for tt in range(SEATS):
            full_send[tt, n] = block[tt * 128:(tt + 1) * 128]
        send_full(n)

    values_0, values_1 = value_grad(0), value_grad(1)
    both_heads(values_0, values_1, 2)

    half_in_moves.arrive()
    for tt in range(SEATS):
        rows = slice(tt * 128, (tt + 1) * 128)
        as_queries(2, rows, unfold(half_seg[tt, 0]), False)
        as_keys(2, rows, unfold(half_seg[tt, 1]), False, k4, kt)
    weights(2)
    half_value_moves.arrive()
    for tt in range(SEATS):
        rows = slice(tt * 128, (tt + 1) * 128)
        as_keys(2, rows, unfold(half_seg[tt, 2]), False, v4, vt)
    attention(2)
    turned = weight_grad(attn_t[2])
    turned = jnp.concatenate([turned, turned], axis=0)
    for xx in range(X):
        block = turned[:, xx * 192:(xx + 1) * 192].T
        for yy in range(4):
            top, bottom = block[yy * 48:yy * 48 + 24], block[yy * 48 + 24:yy * 48 + 48]
            packed = jnp.where(low_lanes(top), top, bottom)
            wg_mid[0, xx, yy] = packed[0:12]
            wg_mid[1, xx, yy] = packed[12:24]

    mid_first = sum_first(wg_mid, wg_mid_1)

    score_grad(0)
    score_grad(1)
    keys_0, keys_1 = key_grad(0), key_grad(1)
    both_heads(keys_0, keys_1, 1)
    wg_first.arrive()
    wg_second = sum_second(wg_full, wg_full_1, wg_full_sum, wg_full_2)
    far_grad(0, keys_0, values_0)
    far_grad(1, keys_1, values_1)
    far_out = Group(
        far_got,
        [
            (far_part.at[y_place(j), pl.ds(0, 2)], far_got.at[j - 1, pl.ds(0, 2)], y_peer(j))
            for j in (2, 1, 3)
        ],
    )
    query_grad(0)
    query_grad(1)
    for tt in range(SEATS):
        full_send[tt, 0] = dq_t[0:2, :, tt * 128:(tt + 1) * 128].reshape(128, 128).T
    send_full(0)
    d_value = value_grad(2)
    score_grad(2)
    d_key = key_grad(2)
    far_grad(2, d_key, d_value)
    far_out.add(
        (far_part.at[y_place(j), pl.ds(2, 1)], far_got.at[j - 1, pl.ds(2, 1)], y_peer(j))
        for j in (2, 1, 3)
    )
    for tt in range(SEATS):
        for n, part in ((1, d_key), (2, d_value)):
            top, bottom = part[tt * 128:tt * 128 + 64], part[tt * 128 + 64:tt * 128 + 128]
            half_send[tt, n] = jnp.where(low_lanes(top), top, bottom)
    half_out = Group(
        half_got.at[pl.ds(0, 3)],
        [
            (half_send.at[seat_of(d), pl.ds(1, 2)], half_got.at[t, pl.ds(1, 2)], seg_peer(d))
            for d in (2, 3, 1)
        ],
    )
    mid_first.arrive()
    mid_second = sum_second(wg_mid, wg_mid_1, wg_mid_sum, wg_mid_2)
    query_grad(2)
    for tt in range(SEATS):
        block = dq_t[2, :, tt * 128:(tt + 1) * 128]
        block = jnp.concatenate([block, block], axis=0).T
        half_send[tt, 0] = jnp.where(low_lanes(block[0:64]), block[0:64], block[64:128])

    def to_owners(notes, got):
        return Group(
            got.at[pl.ds(0, 15)],
            [(notes.at[ring_place(j)], got.at[m], ring_peer(j)) for j in FAR_FIRST],
        )

    wg_second.arrive()
    parts = sum_last(wg_full_sum, wg_full_2)
    for mm in range(16):
        last[mm, 0:3, :] = parts[mm // 8][3 * (mm % 8):3 * (mm % 8) + 3]
    far_out.arrive()
    for h in range(HEADS_HERE):
        rows = far_part[y, h] + far_got[0, h] + far_got[1, h] + far_got[2, h]
        for mm in range(16):
            far_note[mm, 2 * h:2 * h + 2, :] = rows[2 * mm:2 * mm + 2]
    far_last = to_owners(far_note, far_note_got)
    mid_second.arrive()
    parts = sum_last(wg_mid_sum, wg_mid_2)
    for mm in range(16):
        rows = parts[mm // 4 % 2]
        last[mm, 3:6, :] = (rows if mm < 8 else flip(rows))[3 * (mm % 4):3 * (mm % 4) + 3]
    last_moves = to_owners(last, last_got)
    half_out.add((half_send.at[seat_of(d), 0], half_got.at[t, 0], seg_peer(d)) for d in (2, 3, 1))
    keep_own(half_send.at[t], half_got.at[t])
    keep_own(last.at[m], last_got.at[m])
    keep_own(far_note.at[m], far_note_got.at[m])

    for group in (
        w_full_moves, w_mid_moves, g_forwarded, full_in_moves, value_in_moves, half_in_moves,
        half_value_moves, wg_first, mid_first, wg_second, far_out, mid_second, full_out,
    ):
        group.sent()
    full_out.arrive()
    for copy in own_out:
        copy.wait()
    for group in (far_last, last_moves, half_out):
        group.sent()
        group.arrive()


def put_together(
    full_got, half_got, last_got, far_got, offset_ref, dq_out, dk_out, dv_out, wg_out,
    dq_own, dk_own, dv_own, wg_own, out_sem,
):
    stores = [
        pltpu.make_async_copy(src, dst, out_sem.at[n])
        for n, (src, dst) in enumerate(
            ((dq_own, dq_out), (dk_own, dk_out), (dv_own, dv_out), (wg_own, wg_out))
        )
    ]
    row64 = lax.broadcasted_iota(jnp.int32, (64, 128), 0)
    low64 = lax.broadcasted_iota(jnp.int32, (64, 128), 1) < 64
    outs = (dq_own, dk_own, dv_own)
    far_rows, wg_rows = [
        [got[tt] + got[4 + tt] + got[8 + tt] + got[12 + tt] for tt in range(SEATS)]
        for got in (far_got, last_got)
    ]

    def with_extra(n, r, tt, h, upper, block):
        if n == 0:
            return block
        row = far_rows[tt][2 * h + r:2 * h + r + 1]
        if (n == 2) != upper:
            row = flip(row)
        keep = (row64 == offset_ref[head_of(tt, h)]) & (low64 != upper)
        return block + jnp.where(keep, jnp.broadcast_to(row, (64, 128)), 0.0)

    for n in range(3):
        for half in range(2):
            even, odd = half_got[2 * half, n], half_got[2 * half + 1, n]
            for r in range(2):
                if r == 0:
                    block = jnp.where(low64, even, flip(odd))
                else:
                    block = jnp.where(low64, flip(even), odd)
                block = with_extra(n, r, 2 * half, 2, False, block)
                block = with_extra(n, r, 2 * half + 1, 2, True, block)
                outs[n][r * 64:(r + 1) * 64, lanes_of(3 * half + 1)] = block
        for tt in range(SEATS):
            for r in range(2):
                block = full_got[tt, n, r * 64:(r + 1) * 64, :]
                block = with_extra(n, r, tt, 0, False, block)
                block = with_extra(n, r, tt, 1, True, block)
                outs[n][r * 64:(r + 1) * 64, lanes_of(full_tile(tt))] = block
        stores[n].start()

    scale = 8192.0 ** -0.5
    for tt in range(SEATS):
        wg_own[:, lanes_of(full_tile(tt))] = wg_rows[tt][0:3] * scale
    for half in range(2):
        even, odd = wg_rows[2 * half][3:6], wg_rows[2 * half + 1][3:6]
        wg_own[:, lanes_of(3 * half + 1)] = jnp.where(low_lanes(even), even, flip(odd)) * scale
    stores[3].start()
    for copy in stores:
        copy.wait()


def on_device(queries, keys, values, out_grad, out_weight, valid_tiles, head_offsets):
    def block(*shape):
        return pltpu.VMEM(shape, F32)

    def half(*shape):
        return pltpu.VMEM(shape, BF16)

    scratch = [
        block(ROWS, WIDTH), block(ROWS, WIDTH), block(ROWS, WIDTH), block(3, WIDTH),
        block(4, 3, 64, 128), block(4, 3, 64, 128), block(4, 3, 128, 128), block(4, 3, 128, 128),
        block(4, ROWS, WIDTH),
        block(4, 12, 128), block(16, 12, 128),
        block(4, 4, 48, 128), block(4, 4, 48, 128), half(WIDTH, 256), half(WIDTH, 256),
        block(4, 3, 32, 128),
        half(3, SEG, 256), half(3, KEYS, 256), half(3, KEYS, 256),
        half(3, 128, KEYS), half(3, 128, KEYS),
        half(3, SEG, 256), block(3, 64, SEG), block(3, 64, SEG),
        block(3, KEYS, SEG), half(3, KEYS, SEG), half(3, KEYS, SEG),
        half(3, KEYS, SEG), half(3, KEYS, SEG),
        half(SEG, WIDTH), half(SEG, WIDTH),
        block(4, 3, 32, 128), block(3, 3, 32, 128),
        block(2, 4, 4, 24, 128), block(2, 3, 4, 24, 128), block(2, 4, 24, 128), block(2, 3, 24, 128),
        block(2, 4, 4, 12, 128), block(2, 3, 4, 12, 128), block(2, 4, 12, 128), block(2, 3, 12, 128),
        block(16, 8, 128), block(16, 8, 128), block(3, 64, SEG),
        block(4, 3, 128, 128), block(4, 3, 64, 128),
        pltpu.SemaphoreType.DMA((SENDS,)), pltpu.SemaphoreType.DMA((SENDS,)),
        pltpu.SemaphoreType.DMA((11,)),
    ]
    whole = pl.BlockSpec(memory_space=pltpu.HBM)
    scalars = pl.BlockSpec(memory_space=pltpu.SMEM)
    rows = jax.ShapeDtypeStruct((ROWS, WIDTH), F32)
    blocks = [
        pltpu.with_memory_space_constraint(array, pltpu.HBM)
        for array in (queries[0], keys[0], values[0], out_grad[0], out_weight)
    ]
    head_offsets = pltpu.with_memory_space_constraint(head_offsets, pltpu.HBM)
    got = pl.pallas_call(
        kernel,
        out_shape=(
            jax.ShapeDtypeStruct((4, 3, 128, 128), F32),
            jax.ShapeDtypeStruct((4, 3, 64, 128), F32),
            jax.ShapeDtypeStruct((16, 8, 128), F32),
            jax.ShapeDtypeStruct((16, 8, 128), F32),
        ),
        in_specs=[whole] * 5 + [scalars] * 2,
        out_specs=(whole,) * 4,
        scratch_shapes=scratch,
        compiler_params=pltpu.CompilerParams(
            collective_id=0, has_side_effects=True, vmem_limit_bytes=48 * 1024 * 1024
        ),
        cost_estimate=pl.CostEstimate(
            flops=4_000_000_000, bytes_accessed=4_000_000, transcendentals=1_000_000
        ),
        name="dilated_backward",
    )(*blocks, valid_tiles, head_offsets)
    d_query, d_key, d_value, d_weight = pl.pallas_call(
        put_together,
        out_shape=(rows, rows, rows, jax.ShapeDtypeStruct((3, WIDTH), F32)),
        in_specs=[pl.BlockSpec(memory_space=pltpu.VMEM)] * 4 + [scalars],
        out_specs=(whole,) * 4,
        scratch_shapes=[
            block(ROWS, WIDTH), block(ROWS, WIDTH), block(ROWS, WIDTH), block(3, WIDTH),
            pltpu.SemaphoreType.DMA((4,)),
        ],
        compiler_params=pltpu.CompilerParams(vmem_limit_bytes=16 * 1024 * 1024),
        cost_estimate=pl.CostEstimate(flops=1_000_000, bytes_accessed=2_500_000, transcendentals=0),
        name="put_together",
    )(*got, head_offsets)
    return d_query[None], d_key[None], d_value[None], d_weight


def solution(mesh):
    from jax.sharding import PartitionSpec as P

    tiles = P("dp", "seq", None)
    weight = P(("dp", "seq"), None)
    return jax.shard_map(
        on_device,
        mesh=mesh,
        in_specs=(tiles, tiles, tiles, tiles, weight, P("dp"), P()),
        out_specs=(tiles, tiles, tiles, weight),
        check_vma=False,
    )
```

```python
import jax
import jax.numpy as jnp
from jax import lax
from jax.experimental import pallas as pl
from jax.experimental.pallas import tpu as pltpu

F32 = jnp.float32
BF16 = jnp.bfloat16
MASKED = -1e30
MESH = pl.DeviceIdType.MESH

X = 4
ROWS = 128
SEATS = 4
SEG = ROWS * SEATS
SPACING = 64
FAR = 128
WIDTH = 768
HEADS_HERE = 3
KEYS = SEG + FAR
G_CHUNKS = 4
G_EARLY = 1
FAR_FIRST = (8, 7, 9, 6, 10, 5, 11, 4, 12, 3, 13, 2, 14, 1, 15)
SENDS = 32


def dot(left, right):
    return lax.dot_general(left, right, (((1,), (0,)), ((), ())), preferred_element_type=F32)


def dot_nt(left, right):
    return lax.dot_general(left, right, (((1,), (1,)), ((), ())), preferred_element_type=F32)


def flip(block):
    return pltpu.roll(block, 64, 1)


def low_lanes(block):
    return lax.broadcasted_iota(jnp.int32, block.shape, 1) < 64


def split(block):
    high = block.astype(BF16).astype(F32)
    return high, block - high


def pair(block, upper):
    high, low = split(block)
    if upper:
        return jnp.where(low_lanes(block), flip(high), low)
    return jnp.where(low_lanes(block), high, flip(low))


def twice(block, upper):
    if upper:
        return jnp.where(low_lanes(block), flip(block), block)
    return jnp.where(low_lanes(block), block, flip(block))


def unfold(packed):
    return jnp.concatenate([packed, flip(packed)], axis=0)


def fold_halves(block):
    return block + flip(block)


def lanes_of(tile):
    return slice(tile * 128, (tile + 1) * 128)


def full_tile(seat):
    return 3 * (seat // 2) + 2 * (seat % 2)


def middle_tile(seat):
    return 3 * (seat // 2) + 1


def head_of(seat, h):
    return 6 * (seat // 2) + (2 + seat % 2 if h == 2 else 4 * (seat % 2) + h)


def kernel(
    q_in, k_in, v_in, g_in, w_in, valid_ref, offset_ref,
    full_got, half_got, last_got,
    q_own, k_own, v_own, w_own, half_in, half_seg, full_in, full_seg, g_seg,
    note, note_got, w_full, w_mid, w_hi, w_lo, far,
    q4, k4, v4, kt, vt, do4, do_t, attn_t, prob, prob_hi, prob_lo, ds_hi, ds_lo, g_hi, g_lo,
    far_part, far_got,
    wg_full, wg_full_1, wg_full_sum, wg_full_2, wg_mid, wg_mid_1, wg_mid_sum, wg_mid_2,
    last, dq_t, full_send, half_send,
    send_sem, recv_sem, local_sem,
):
    x = lax.axis_index("dp")
    s = lax.axis_index("seq")
    y = lax.div(s, 16)
    m = lax.rem(s, 16)
    z = lax.div(m, 2)
    c = lax.rem(s, 2)
    hz = lax.rem(z, 2)
    zz = lax.div(z, 2)
    t = lax.rem(s, 4)
    seg = lax.div(s, 4)

    def seat_of(d):
        core = c if d % 2 == 0 else 1 - c
        half = hz if d < 2 else 1 - hz
        return half * 2 + core

    def seg_peer(d):
        return (x, seg * 4 + seat_of(d))

    def ring_place(j):
        return lax.rem(m + j, 16)

    def ring_peer(j):
        return (x, y * 16 + ring_place(j))

    def y_place(j):
        return lax.rem(y + j, 4)

    def y_peer(j):
        return (x, y_place(j) * 16 + m)

    def x_place(j):
        return lax.rem(x + j, 4)

    def x_peer(j):
        return (x_place(j), s)

    class Group:
        count = 0

        def __init__(self, like, copies=()):
            self.like, self.index = like, Group.count
            Group.count += 1
            self.add(copies)

        def describe(self, src, dst, device):
            return pltpu.make_async_remote_copy(
                src_ref=src, dst_ref=dst, send_sem=send_sem.at[self.index],
                recv_sem=recv_sem.at[self.index], device_id=device, device_id_type=MESH,
            )

        def add(self, copies):
            for src, dst, device in copies:
                self.describe(src, dst, device).start()

        def arrive(self):
            self.describe(self.like, self.like, seg_peer(1)).wait_recv()

        def sent(self):
            self.describe(self.like, self.like, seg_peer(1)).wait_send()

    loads = []
    for src, dst in (
        (g_in, g_seg.at[t]), (k_in, k_own), (v_in, v_own), (w_in, w_own), (q_in, q_own),
    ):
        copy = pltpu.make_async_copy(src, dst, local_sem.at[len(loads)])
        copy.start()
        loads.append(copy)

    barrier = pltpu.get_barrier_semaphore()
    for device in (
        [ring_peer(j) for j in range(1, 16)]
        + [y_peer(j) for j in (1, 2, 3)]
        + [x_peer(j) for j in (1, 2, 3)]
    ):
        pl.semaphore_signal(barrier, inc=1, device_id=device, device_id_type=MESH)

    owns = (q_own, k_own, v_own)

    def deal(n):
        for tt in range(SEATS):
            full_in[tt, n] = owns[n][:, lanes_of(full_tile(tt))]
            top = owns[n][0:64, lanes_of(middle_tile(tt))]
            bottom = owns[n][64:128, lanes_of(middle_tile(tt))]
            if tt % 2 == 0:
                half_in[tt, n] = jnp.where(low_lanes(top), top, flip(bottom))
            else:
                half_in[tt, n] = jnp.where(low_lanes(top), flip(top), bottom)

    g_rows = ROWS // G_CHUNKS

    def g_part(seat, n):
        return g_seg.at[seat, pl.ds(n * g_rows, g_rows)]

    loads[0].wait()
    pl.semaphore_wait(barrier, 21)
    def send_across(n):
        return Group(g_part(0, n), [(g_part(t, n), g_part(t, n), seg_peer(2))])

    g_across = [send_across(n) for n in range(G_EARLY)]

    loads[1].wait()
    deal(1)
    loads[2].wait()
    deal(2)

    def long_rows(tt, h, n):
        offset = offset_ref[head_of(tt, h)]
        if h == 2:
            row = half_in[tt, n, pl.ds(offset, 1), :]
            return jnp.concatenate([row, flip(row)], axis=0)
        return jnp.concatenate(
            [full_in[tt, n, pl.ds(r * 64 + offset, 1), :] for r in range(2)], axis=0
        )

    loads[3].wait()
    for tt in range(SEATS):
        note[tt, 0:3, :] = w_own[:, lanes_of(full_tile(tt))]
        note[tt, 3:6, :] = w_own[:, lanes_of(middle_tile(tt))]
        for h in range(HEADS_HERE):
            key_rows, value_rows = long_rows(tt, h, 1), long_rows(tt, h, 2)
            low = low_lanes(key_rows)
            if h == 1:
                rows = jnp.where(low, flip(key_rows), value_rows)
            else:
                rows = jnp.where(low, key_rows, flip(value_rows))
            note[tt, 6 + 2 * h:8 + 2 * h, :] = rows

    notes = Group(
        note_got.at[pl.ds(0, 15)],
        [(note.at[lax.rem(ring_place(j), 4)], note_got.at[m], ring_peer(j)) for j in FAR_FIRST],
    )
    g_across += [send_across(n) for n in range(G_EARLY, G_CHUNKS)]
    note_got[m] = note[t]
    loads[4].wait()
    deal(0)
    full_in_moves = Group(
        full_seg.at[pl.ds(0, 3), pl.ds(0, 2)],
        [
            (full_in.at[seat_of(d), pl.ds(0, 2)], full_seg.at[t, pl.ds(0, 2)], seg_peer(d))
            for d in (2, 3, 1)
        ],
    )
    value_in_moves = Group(
        full_seg.at[pl.ds(0, 3), 2],
        [(full_in.at[seat_of(d), 2], full_seg.at[t, 2], seg_peer(d)) for d in (2, 3, 1)],
    )
    g_beside = Group(g_seg.at[0], [(g_seg.at[t], g_seg.at[t], seg_peer(1))])
    half_in_moves = Group(
        half_seg.at[pl.ds(0, 3), pl.ds(0, 2)],
        [
            (half_in.at[seat_of(d), pl.ds(0, 2)], half_seg.at[t, pl.ds(0, 2)], seg_peer(d))
            for d in (2, 3, 1)
        ],
    )
    half_value_moves = Group(
        half_seg.at[pl.ds(0, 3), 2],
        [(half_in.at[seat_of(d), 2], half_seg.at[t, 2], seg_peer(d)) for d in (2, 3, 1)],
    )
    half_seg[t] = half_in[t]
    full_seg[t] = full_in[t]

    notes.arrive()
    for mm in range(16):
        w_full[x, y, 3 * mm:3 * mm + 3, :] = note_got[mm, 0:3, :]
        w_mid[x, y, 3 * mm:3 * mm + 3, :] = note_got[mm, 3:6, :]
        for h in range(HEADS_HERE):
            far[y, h, 2 * mm:2 * mm + 2, :] = note_got[mm, 6 + 2 * h:8 + 2 * h, :]
    w_first = Group(
        w_full.at[pl.ds(0, 2), pl.ds(0, 3)],
        [(w_full.at[x, y], w_full.at[x, y], y_peer(j)) for j in (2, 1, 3)]
        + [(w_mid.at[x, y], w_mid.at[x, y], x_peer(j)) for j in (2, 1, 3)],
    )
    far_moves = Group(
        far.at[pl.ds(0, 3)], [(far.at[y], far.at[y], y_peer(j)) for j in (2, 1, 3)]
    )
    w_first.arrive()
    w_full_moves = Group(
        w_full.at[pl.ds(0, 3)], [(w_full.at[x], w_full.at[x], x_peer(j)) for j in (2, 1, 3)]
    )
    w_mid_moves = Group(
        w_mid.at[pl.ds(0, 3)], [(w_mid.at[:, y], w_mid.at[:, y], y_peer(j)) for j in (2, 1, 3)]
    )
    far_moves.arrive()

    def as_keys(h, rows, block, upper, four, transposed):
        high, low = split(block)
        four[h, rows, 0:128] = twice(high, upper).astype(BF16)
        four[h, rows, 128:256] = twice(low, upper).astype(BF16)
        transposed[h, :, rows] = pair(block, upper).T.astype(BF16)

    for h in range(HEADS_HERE):
        block = far[:, h].reshape(FAR, 128)
        as_keys(h, slice(SEG, KEYS), block, False, k4, kt)
        as_keys(h, slice(SEG, KEYS), block, True, v4, vt)

    valid = valid_ref[0]
    tile_row = lax.broadcasted_iota(jnp.int32, (ROWS, WIDTH), 0)

    def take_grad(seat):
        rows = pl.ds(pl.multiple_of(seat * ROWS, ROWS), ROWS)
        grad = jnp.where(seg * SEG + seat * ROWS + tile_row < valid, g_seg[seat], 0.0)
        high = grad.astype(BF16)
        g_hi[rows, :] = high
        g_lo[rows, :] = (grad - high.astype(F32)).astype(BF16)

    take_grad(t)
    g_beside.arrive()
    take_grad(seat_of(1))
    g_forwarded = Group(g_seg.at[0])
    for n in range(G_CHUNKS):
        g_across[n].arrive()
        part = g_part(seat_of(2), n)
        g_forwarded.add([(part, part, seg_peer(1))])
    take_grad(seat_of(2))

    g_forwarded.arrive()
    take_grad(seat_of(3))
    def as_queries(h, rows, block, upper):
        both = pair(block * 0.125, upper).astype(BF16)
        q4[h, rows, 0:128] = both
        q4[h, rows, 128:256] = both

    key_row = lax.broadcasted_iota(jnp.int32, (128, 256), 0)
    query_lane = lax.broadcasted_iota(jnp.int32, (128, 256), 1)

    def weights(h):
        head = 6 * hz + jnp.where(h == 2, 2 + c, 4 * c + h)
        offset = offset_ref[head]
        for qb in range(2):
            lanes = slice(qb * 256, (qb + 1) * 256)
            queries = q4[h, lanes, :]
            top = None
            for kb in range(5):
                rows = slice(kb * 128, (kb + 1) * 128)
                scores = dot_nt(k4[h, rows, :], queries)
                if kb < 4:
                    keep = (seg * SEG + kb * 128 + key_row < valid) | (
                        kb * 128 + key_row == qb * 256 + query_lane
                    )
                else:
                    keep = (key_row * SPACING + offset < valid) & (
                        lax.rem(query_lane, SPACING) == offset
                    )
                scores = jnp.where(keep, scores, MASKED)
                prob[h, rows, lanes] = scores
                here = jnp.max(scores, axis=0, keepdims=True)
                top = here if top is None else jnp.maximum(top, here)
            total = None
            for kb in range(5):
                rows = slice(kb * 128, (kb + 1) * 128)
                weight = jnp.exp(prob[h, rows, lanes] - top)
                prob[h, rows, lanes] = weight
                here = jnp.sum(weight, axis=0, keepdims=True)
                total = here if total is None else total + here
            scale = 1.0 / total
            for kb in range(5):
                rows = slice(kb * 128, (kb + 1) * 128)
                p = prob[h, rows, lanes] * scale
                prob[h, rows, lanes] = p
                high = p.astype(BF16)
                prob_hi[h, rows, lanes] = high
                prob_lo[h, rows, lanes] = (p - high.astype(F32)).astype(BF16)

    def attention(h):
        for qb in range(2):
            lanes = slice(qb * 256, (qb + 1) * 256)
            out = dot(vt[h], prob_hi[h, :, lanes]) + dot(vt[h], prob_lo[h, :, lanes])
            attn_t[h, :, lanes] = out[0:64] + out[64:128]

    def value_grad(h):
        grads = do4[h, :, 0:128]
        return fold_halves(dot(prob_hi[h], grads) + dot(prob_lo[h], grads))

    def key_grad(h):
        queries = q4[h, :, 0:128]
        return fold_halves(dot(ds_hi[h], queries) + dot(ds_lo[h], queries))

    def score_grad(h):
        for qb in range(2):
            lanes = slice(qb * 256, (qb + 1) * 256)
            delta = jnp.sum(attn_t[h, :, lanes] * do_t[h, :, lanes], axis=0, keepdims=True)
            for kb in range(5):
                rows = slice(kb * 128, (kb + 1) * 128)
                d_prob = dot_nt(v4[h, rows, :], do4[h, lanes, :])
                ds = prob[h, rows, lanes] * (d_prob - delta)
                high = ds.astype(BF16)
                ds_hi[h, rows, lanes] = high
                ds_lo[h, rows, lanes] = (ds - high.astype(F32)).astype(BF16)

    def query_grad(h):
        turned = dot(kt[h], ds_hi[h]) + dot(kt[h], ds_lo[h])
        dq_t[h] = (turned[0:64] + turned[64:128]) * 0.125

    def weight_grad(attn):
        high = attn.astype(BF16)
        low = (attn - high.astype(F32)).astype(BF16)
        return dot(high, g_hi[...]) + dot(low, g_hi[...]) + dot(high, g_lo[...])

    def far_grad(h, d_key, d_value):
        d_key, d_value = d_key[SEG:KEYS], d_value[SEG:KEYS]
        block = jnp.where(low_lanes(d_key), d_key, d_value)
        far_part[:, h] = block.reshape(4, 32, 128)

    def sum_first(parts, got):
        return Group(
            got,
            [(parts.at[0, x_place(j)], got.at[0, j - 1], x_peer(j)) for j in (2, 1, 3)]
            + [(parts.at[1, :, y_place(j)], got.at[1, j - 1], y_peer(j)) for j in (2, 1, 3)],
        )

    def sum_second(parts, got, sums, got_next):
        sums[0] = parts[0, x] + got[0, 0] + got[0, 1] + got[0, 2]
        sums[1] = parts[1, :, y] + got[1, 0] + got[1, 1] + got[1, 2]
        return Group(
            got_next,
            [(sums.at[0, y_place(j)], got_next.at[0, j - 1], y_peer(j)) for j in (2, 1, 3)]
            + [(sums.at[1, x_place(j)], got_next.at[1, j - 1], x_peer(j)) for j in (2, 1, 3)],
        )

    def sum_last(sums, got_next):
        return (
            sums[0, y] + got_next[0, 0] + got_next[0, 1] + got_next[0, 2],
            sums[1, x] + got_next[1, 0] + got_next[1, 1] + got_next[1, 2],
        )

    for group in [notes, w_first, far_moves, g_beside] + g_across:
        group.sent()
    full_in_moves.arrive()
    for tt in range(SEATS):
        rows = slice(tt * 128, (tt + 1) * 128)
        for h in range(2):
            as_queries(h, rows, full_seg[tt, 0], h == 1)
            as_keys(h, rows, full_seg[tt, 1], h == 1, k4, kt)
    weights(0)
    weights(1)
    value_in_moves.arrive()
    for tt in range(SEATS):
        rows = slice(tt * 128, (tt + 1) * 128)
        for h in range(2):
            as_keys(h, rows, full_seg[tt, 2], h == 1, v4, vt)
    attention(0)
    attention(1)
    turned = weight_grad(attn_t[0:2].reshape(128, SEG))
    for xx in range(X):
        block = turned[:, xx * 192:(xx + 1) * 192].T
        for yy in range(4):
            for n in range(2):
                wg_full[n, xx, yy] = block[yy * 48 + n * 24:yy * 48 + n * 24 + 24]
    wg_first = sum_first(wg_full, wg_full_1)

    w_full_moves.arrive()
    w_mid_moves.arrive()
    for tile, ref in ((0, w_full), (1, w_mid)):
        columns = ref[...].reshape(WIDTH, 128)
        if tile == 1:
            columns = jnp.where(c == 1, flip(columns), columns)
        high = columns.astype(BF16)
        w_hi[:, lanes_of(tile)] = high
        w_lo[:, lanes_of(tile)] = (columns - high.astype(F32)).astype(BF16)

    for tt in range(SEATS):
        rows = slice(tt * 128, (tt + 1) * 128)
        high, low = g_hi[rows, :], g_lo[rows, :]
        out = dot(high, w_hi[...]) + dot(low, w_hi[...]) + dot(high, w_lo[...])
        full, middle = out[:, 0:128], out[:, 128:256]
        for h, block, upper in ((0, full, False), (1, full, True), (2, middle, False)):
            both = pair(block, upper).astype(BF16)
            do4[h, rows, 0:128] = both
            do4[h, rows, 128:256] = both
        turned = full.T
        do_t[0, :, rows] = turned[0:64]
        do_t[1, :, rows] = turned[64:128]
        do_t[2, :, rows] = middle.T[0:64]

    full_out = Group(full_got.at[pl.ds(0, 3)])
    own_out = []

    def keep_own(src, dst):
        copy = pltpu.make_async_copy(src, dst, local_sem.at[5 + len(own_out)])
        copy.start()
        own_out.append(copy)

    def send_full(n):
        full_out.add(
            (full_send.at[seat_of(d), n], full_got.at[t, n], seg_peer(d)) for d in (2, 3, 1)
        )
        keep_own(full_send.at[t, n], full_got.at[t, n])

    def both_heads(low, high, n):
        block = jnp.where(low_lanes(low), low, high)
        for tt in range(SEATS):
            full_send[tt, n] = block[tt * 128:(tt + 1) * 128]
        send_full(n)

    values_0, values_1 = value_grad(0), value_grad(1)
    both_heads(values_0, values_1, 2)

    half_in_moves.arrive()
    for tt in range(SEATS):
        rows = slice(tt * 128, (tt + 1) * 128)
        as_queries(2, rows, unfold(half_seg[tt, 0]), False)
        as_keys(2, rows, unfold(half_seg[tt, 1]), False, k4, kt)
    weights(2)
    half_value_moves.arrive()
    for tt in range(SEATS):
        rows = slice(tt * 128, (tt + 1) * 128)
        as_keys(2, rows, unfold(half_seg[tt, 2]), False, v4, vt)
    attention(2)
    turned = weight_grad(attn_t[2])
    turned = jnp.concatenate([turned, turned], axis=0)
    for xx in range(X):
        block = turned[:, xx * 192:(xx + 1) * 192].T
        for yy in range(4):
            top, bottom = block[yy * 48:yy * 48 + 24], block[yy * 48 + 24:yy * 48 + 48]
            packed = jnp.where(low_lanes(top), top, bottom)
            wg_mid[0, xx, yy] = packed[0:12]
            wg_mid[1, xx, yy] = packed[12:24]

    mid_first = sum_first(wg_mid, wg_mid_1)

    score_grad(0)
    score_grad(1)
    keys_0, keys_1 = key_grad(0), key_grad(1)
    both_heads(keys_0, keys_1, 1)
    wg_first.arrive()
    wg_second = sum_second(wg_full, wg_full_1, wg_full_sum, wg_full_2)
    far_grad(0, keys_0, values_0)
    far_grad(1, keys_1, values_1)
    far_out = Group(
        far_got,
        [
            (far_part.at[y_place(j), pl.ds(0, 2)], far_got.at[j - 1, pl.ds(0, 2)], y_peer(j))
            for j in (2, 1, 3)
        ],
    )
    query_grad(0)
    query_grad(1)
    for tt in range(SEATS):
        full_send[tt, 0] = dq_t[0:2, :, tt * 128:(tt + 1) * 128].reshape(128, 128).T
    send_full(0)
    d_value = value_grad(2)
    score_grad(2)
    d_key = key_grad(2)
    far_grad(2, d_key, d_value)
    far_out.add(
        (far_part.at[y_place(j), pl.ds(2, 1)], far_got.at[j - 1, pl.ds(2, 1)], y_peer(j))
        for j in (2, 1, 3)
    )
    for tt in range(SEATS):
        for n, part in ((1, d_key), (2, d_value)):
            top, bottom = part[tt * 128:tt * 128 + 64], part[tt * 128 + 64:tt * 128 + 128]
            half_send[tt, n] = jnp.where(low_lanes(top), top, bottom)
    half_out = Group(
        half_got.at[pl.ds(0, 3)],
        [
            (half_send.at[seat_of(d), pl.ds(1, 2)], half_got.at[t, pl.ds(1, 2)], seg_peer(d))
            for d in (2, 3, 1)
        ],
    )
    mid_first.arrive()
    mid_second = sum_second(wg_mid, wg_mid_1, wg_mid_sum, wg_mid_2)
    query_grad(2)
    for tt in range(SEATS):
        block = dq_t[2, :, tt * 128:(tt + 1) * 128]
        block = jnp.concatenate([block, block], axis=0).T
        half_send[tt, 0] = jnp.where(low_lanes(block[0:64]), block[0:64], block[64:128])

    def to_owners(notes, got):
        return Group(
            got.at[pl.ds(0, 15)],
            [(notes.at[ring_place(j)], got.at[m], ring_peer(j)) for j in FAR_FIRST],
        )

    wg_second.arrive()
    parts = sum_last(wg_full_sum, wg_full_2)
    for mm in range(16):
        last[mm, 0:3, :] = parts[mm // 8][3 * (mm % 8):3 * (mm % 8) + 3]
    far_out.arrive()
    for h in range(HEADS_HERE):
        rows = far_part[y, h] + far_got[0, h] + far_got[1, h] + far_got[2, h]
        for mm in range(16):
            last[mm, 6 + 2 * h:8 + 2 * h, :] = rows[2 * mm:2 * mm + 2]
    mid_second.arrive()
    parts = sum_last(wg_mid_sum, wg_mid_2)
    for mm in range(16):
        rows = parts[mm // 4 % 2]
        last[mm, 3:6, :] = (rows if mm < 8 else flip(rows))[3 * (mm % 4):3 * (mm % 4) + 3]
    last_moves = to_owners(last, last_got)
    half_out.add((half_send.at[seat_of(d), 0], half_got.at[t, 0], seg_peer(d)) for d in (2, 3, 1))
    keep_own(half_send.at[t], half_got.at[t])
    keep_own(last.at[m], last_got.at[m])

    for group in (
        w_full_moves, w_mid_moves, g_forwarded, full_in_moves, value_in_moves, half_in_moves,
        half_value_moves, wg_first, mid_first, wg_second, far_out, mid_second, full_out,
    ):
        group.sent()
    full_out.arrive()
    for copy in own_out:
        copy.wait()
    for group in (last_moves, half_out):
        group.sent()
        group.arrive()


def put_together(
    full_got, half_got, last_got, offset_ref, dq_out, dk_out, dv_out, wg_out,
    dq_own, dk_own, dv_own, wg_own, out_sem,
):
    stores = [
        pltpu.make_async_copy(src, dst, out_sem.at[n])
        for n, (src, dst) in enumerate(
            ((dq_own, dq_out), (dk_own, dk_out), (dv_own, dv_out), (wg_own, wg_out))
        )
    ]
    row64 = lax.broadcasted_iota(jnp.int32, (64, 128), 0)
    low64 = lax.broadcasted_iota(jnp.int32, (64, 128), 1) < 64
    outs = (dq_own, dk_own, dv_own)
    notes = [
        last_got[tt] + last_got[4 + tt] + last_got[8 + tt] + last_got[12 + tt]
        for tt in range(SEATS)
    ]

    def with_extra(n, r, tt, h, upper, block):
        if n == 0:
            return block
        row = notes[tt][6 + 2 * h + r:7 + 2 * h + r]
        if (n == 2) != upper:
            row = flip(row)
        keep = (row64 == offset_ref[head_of(tt, h)]) & (low64 != upper)
        return block + jnp.where(keep, jnp.broadcast_to(row, (64, 128)), 0.0)

    for n in range(3):
        for half in range(2):
            even, odd = half_got[2 * half, n], half_got[2 * half + 1, n]
            for r in range(2):
                if r == 0:
                    block = jnp.where(low64, even, flip(odd))
                else:
                    block = jnp.where(low64, flip(even), odd)
                block = with_extra(n, r, 2 * half, 2, False, block)
                block = with_extra(n, r, 2 * half + 1, 2, True, block)
                outs[n][r * 64:(r + 1) * 64, lanes_of(3 * half + 1)] = block
        for tt in range(SEATS):
            for r in range(2):
                block = full_got[tt, n, r * 64:(r + 1) * 64, :]
                block = with_extra(n, r, tt, 0, False, block)
                block = with_extra(n, r, tt, 1, True, block)
                outs[n][r * 64:(r + 1) * 64, lanes_of(full_tile(tt))] = block
        stores[n].start()

    scale = 8192.0 ** -0.5
    for tt in range(SEATS):
        wg_own[:, lanes_of(full_tile(tt))] = notes[tt][0:3] * scale
    for half in range(2):
        even, odd = notes[2 * half][3:6], notes[2 * half + 1][3:6]
        wg_own[:, lanes_of(3 * half + 1)] = jnp.where(low_lanes(even), even, flip(odd)) * scale
    stores[3].start()
    for copy in stores:
        copy.wait()


def on_device(queries, keys, values, out_grad, out_weight, valid_tiles, head_offsets):
    def block(*shape):
        return pltpu.VMEM(shape, F32)

    def half(*shape):
        return pltpu.VMEM(shape, BF16)

    scratch = [
        block(ROWS, WIDTH), block(ROWS, WIDTH), block(ROWS, WIDTH), block(3, WIDTH),
        block(4, 3, 64, 128), block(4, 3, 64, 128), block(4, 3, 128, 128), block(4, 3, 128, 128),
        block(4, ROWS, WIDTH),
        block(4, 12, 128), block(16, 12, 128),
        block(4, 4, 48, 128), block(4, 4, 48, 128), half(WIDTH, 256), half(WIDTH, 256),
        block(4, 3, 32, 128),
        half(3, SEG, 256), half(3, KEYS, 256), half(3, KEYS, 256),
        half(3, 128, KEYS), half(3, 128, KEYS),
        half(3, SEG, 256), block(3, 64, SEG), block(3, 64, SEG),
        block(3, KEYS, SEG), half(3, KEYS, SEG), half(3, KEYS, SEG),
        half(3, KEYS, SEG), half(3, KEYS, SEG),
        half(SEG, WIDTH), half(SEG, WIDTH),
        block(4, 3, 32, 128), block(3, 3, 32, 128),
        block(2, 4, 4, 24, 128), block(2, 3, 4, 24, 128), block(2, 4, 24, 128), block(2, 3, 24, 128),
        block(2, 4, 4, 12, 128), block(2, 3, 4, 12, 128), block(2, 4, 12, 128), block(2, 3, 12, 128),
        block(16, 12, 128), block(3, 64, SEG),
        block(4, 3, 128, 128), block(4, 3, 64, 128),
        pltpu.SemaphoreType.DMA((SENDS,)), pltpu.SemaphoreType.DMA((SENDS,)),
        pltpu.SemaphoreType.DMA((11,)),
    ]
    whole = pl.BlockSpec(memory_space=pltpu.HBM)
    scalars = pl.BlockSpec(memory_space=pltpu.SMEM)
    rows = jax.ShapeDtypeStruct((ROWS, WIDTH), F32)
    blocks = [
        pltpu.with_memory_space_constraint(array, pltpu.HBM)
        for array in (queries[0], keys[0], values[0], out_grad[0], out_weight)
    ]
    head_offsets = pltpu.with_memory_space_constraint(head_offsets, pltpu.HBM)
    got = pl.pallas_call(
        kernel,
        out_shape=(
            jax.ShapeDtypeStruct((4, 3, 128, 128), F32),
            jax.ShapeDtypeStruct((4, 3, 64, 128), F32),
            jax.ShapeDtypeStruct((16, 12, 128), F32),
        ),
        in_specs=[whole] * 5 + [scalars] * 2,
        out_specs=(whole,) * 3,
        scratch_shapes=scratch,
        compiler_params=pltpu.CompilerParams(
            collective_id=0, has_side_effects=True, vmem_limit_bytes=48 * 1024 * 1024
        ),
        cost_estimate=pl.CostEstimate(
            flops=4_000_000_000, bytes_accessed=4_000_000, transcendentals=1_000_000
        ),
        name="dilated_backward",
    )(*blocks, valid_tiles, head_offsets)
    d_query, d_key, d_value, d_weight = pl.pallas_call(
        put_together,
        out_shape=(rows, rows, rows, jax.ShapeDtypeStruct((3, WIDTH), F32)),
        in_specs=[pl.BlockSpec(memory_space=pltpu.VMEM)] * 3 + [scalars],
        out_specs=(whole,) * 4,
        scratch_shapes=[
            block(ROWS, WIDTH), block(ROWS, WIDTH), block(ROWS, WIDTH), block(3, WIDTH),
            pltpu.SemaphoreType.DMA((4,)),
        ],
        compiler_params=pltpu.CompilerParams(vmem_limit_bytes=16 * 1024 * 1024),
        cost_estimate=pl.CostEstimate(flops=1_000_000, bytes_accessed=2_500_000, transcendentals=0),
        name="put_together",
    )(*got, head_offsets)
    return d_query[None], d_key[None], d_value[None], d_weight


def solution(mesh):
    from jax.sharding import PartitionSpec as P

    tiles = P("dp", "seq", None)
    weight = P(("dp", "seq"), None)
    return jax.shard_map(
        on_device,
        mesh=mesh,
        in_specs=(tiles, tiles, tiles, tiles, weight, P("dp"), P()),
        out_specs=(tiles, tiles, tiles, weight),
        check_vma=False,
    )
```

```python
import jax
import jax.numpy as jnp
from jax import lax
from jax.experimental import pallas as pl
from jax.experimental.pallas import tpu as pltpu

F32 = jnp.float32
BF16 = jnp.bfloat16
MASKED = -1e30
MESH = pl.DeviceIdType.MESH

X = 4
ROWS = 128
SEATS = 4
SEG = ROWS * SEATS
SPACING = 64
FAR = 128
WIDTH = 768
HEADS_HERE = 3
KEYS = SEG + FAR
G_CHUNKS = 2
G_EARLY = 0
FAR_FIRST = (8, 7, 9, 6, 10, 5, 11, 4, 12, 3, 13, 2, 14, 1, 15)
SENDS = 32


def dot(left, right):
    return lax.dot_general(left, right, (((1,), (0,)), ((), ())), preferred_element_type=F32)


def dot_nt(left, right):
    return lax.dot_general(left, right, (((1,), (1,)), ((), ())), preferred_element_type=F32)


def flip(block):
    return pltpu.roll(block, 64, 1)


def low_lanes(block):
    return lax.broadcasted_iota(jnp.int32, block.shape, 1) < 64


def split(block):
    high = block.astype(BF16).astype(F32)
    return high, block - high


def pair(block, upper):
    high, low = split(block)
    if upper:
        return jnp.where(low_lanes(block), flip(high), low)
    return jnp.where(low_lanes(block), high, flip(low))


def twice(block, upper):
    if upper:
        return jnp.where(low_lanes(block), flip(block), block)
    return jnp.where(low_lanes(block), block, flip(block))


def unfold(packed):
    return jnp.concatenate([packed, flip(packed)], axis=0)


def fold_halves(block):
    return block + flip(block)


def lanes_of(tile):
    return slice(tile * 128, (tile + 1) * 128)


def full_tile(seat):
    return 3 * (seat // 2) + 2 * (seat % 2)


def middle_tile(seat):
    return 3 * (seat // 2) + 1


def head_of(seat, h):
    return 6 * (seat // 2) + (2 + seat % 2 if h == 2 else 4 * (seat % 2) + h)


def kernel(
    q_in, k_in, v_in, g_in, w_in, valid_ref, offset_ref,
    full_got, half_got, last_got,
    q_own, k_own, v_own, w_own, half_in, half_seg, full_in, full_seg, g_seg,
    note, note_got, w_full, w_mid, w_hi, w_lo, far,
    q4, k4, v4, kt, vt, do4, do_t, attn_t, prob, prob_hi, prob_lo, ds_hi, ds_lo, g_hi, g_lo,
    far_part, far_got,
    wg_full, wg_full_1, wg_full_sum, wg_full_2, wg_mid, wg_mid_1, wg_mid_sum, wg_mid_2,
    last, dq_t, full_send, half_send,
    send_sem, recv_sem, local_sem,
):
    x = lax.axis_index("dp")
    s = lax.axis_index("seq")
    y = lax.div(s, 16)
    m = lax.rem(s, 16)
    z = lax.div(m, 2)
    c = lax.rem(s, 2)
    hz = lax.rem(z, 2)
    zz = lax.div(z, 2)
    t = lax.rem(s, 4)
    seg = lax.div(s, 4)

    def seat_of(d):
        core = c if d % 2 == 0 else 1 - c
        half = hz if d < 2 else 1 - hz
        return half * 2 + core

    def seg_peer(d):
        return (x, seg * 4 + seat_of(d))

    def ring_place(j):
        return lax.rem(m + j, 16)

    def ring_peer(j):
        return (x, y * 16 + ring_place(j))

    def y_place(j):
        return lax.rem(y + j, 4)

    def y_peer(j):
        return (x, y_place(j) * 16 + m)

    def x_place(j):
        return lax.rem(x + j, 4)

    def x_peer(j):
        return (x_place(j), s)

    class Group:
        count = 0

        def __init__(self, like, copies=()):
            self.like, self.index = like, Group.count
            Group.count += 1
            self.add(copies)

        def describe(self, src, dst, device):
            return pltpu.make_async_remote_copy(
                src_ref=src, dst_ref=dst, send_sem=send_sem.at[self.index],
                recv_sem=recv_sem.at[self.index], device_id=device, device_id_type=MESH,
            )

        def add(self, copies):
            for src, dst, device in copies:
                self.describe(src, dst, device).start()

        def arrive(self):
            self.describe(self.like, self.like, seg_peer(1)).wait_recv()

        def sent(self):
            self.describe(self.like, self.like, seg_peer(1)).wait_send()

    loads = []
    for src, dst in (
        (g_in, g_seg.at[t]), (k_in, k_own), (v_in, v_own), (w_in, w_own), (q_in, q_own),
    ):
        copy = pltpu.make_async_copy(src, dst, local_sem.at[len(loads)])
        copy.start()
        loads.append(copy)

    barrier = pltpu.get_barrier_semaphore()
    for device in (
        [ring_peer(j) for j in range(1, 16)]
        + [y_peer(j) for j in (1, 2, 3)]
        + [x_peer(j) for j in (1, 2, 3)]
    ):
        pl.semaphore_signal(barrier, inc=1, device_id=device, device_id_type=MESH)

    owns = (q_own, k_own, v_own)

    def deal(n):
        for tt in range(SEATS):
            full_in[tt, n] = owns[n][:, lanes_of(full_tile(tt))]
            top = owns[n][0:64, lanes_of(middle_tile(tt))]
            bottom = owns[n][64:128, lanes_of(middle_tile(tt))]
            if tt % 2 == 0:
                half_in[tt, n] = jnp.where(low_lanes(top), top, flip(bottom))
            else:
                half_in[tt, n] = jnp.where(low_lanes(top), flip(top), bottom)

    g_rows = ROWS // G_CHUNKS

    def g_part(seat, n):
        return g_seg.at[seat, pl.ds(n * g_rows, g_rows)]

    loads[0].wait()
    pl.semaphore_wait(barrier, 21)
    def send_across(n):
        return Group(g_part(0, n), [(g_part(t, n), g_part(t, n), seg_peer(2))])

    g_across = [send_across(n) for n in range(G_EARLY)]

    loads[1].wait()
    deal(1)
    loads[2].wait()
    deal(2)

    def long_rows(tt, h, n):
        offset = offset_ref[head_of(tt, h)]
        if h == 2:
            row = half_in[tt, n, pl.ds(offset, 1), :]
            return jnp.concatenate([row, flip(row)], axis=0)
        return jnp.concatenate(
            [full_in[tt, n, pl.ds(r * 64 + offset, 1), :] for r in range(2)], axis=0
        )

    loads[3].wait()
    for tt in range(SEATS):
        note[tt, 0:3, :] = w_own[:, lanes_of(full_tile(tt))]
        note[tt, 3:6, :] = w_own[:, lanes_of(middle_tile(tt))]
        for h in range(HEADS_HERE):
            key_rows, value_rows = long_rows(tt, h, 1), long_rows(tt, h, 2)
            low = low_lanes(key_rows)
            if h == 1:
                rows = jnp.where(low, flip(key_rows), value_rows)
            else:
                rows = jnp.where(low, key_rows, flip(value_rows))
            note[tt, 6 + 2 * h:8 + 2 * h, :] = rows

    notes = Group(
        note_got.at[pl.ds(0, 15)],
        [(note.at[lax.rem(ring_place(j), 4)], note_got.at[m], ring_peer(j)) for j in FAR_FIRST],
    )
    g_across += [send_across(n) for n in range(G_EARLY, G_CHUNKS)]
    note_got[m] = note[t]
    loads[4].wait()
    deal(0)
    full_in_moves = Group(
        full_seg.at[pl.ds(0, 3), pl.ds(0, 2)],
        [
            (full_in.at[seat_of(d), pl.ds(0, 2)], full_seg.at[t, pl.ds(0, 2)], seg_peer(d))
            for d in (2, 3, 1)
        ],
    )
    value_in_moves = Group(
        full_seg.at[pl.ds(0, 3), 2],
        [(full_in.at[seat_of(d), 2], full_seg.at[t, 2], seg_peer(d)) for d in (2, 3, 1)],
    )
    g_beside = Group(g_seg.at[0], [(g_seg.at[t], g_seg.at[t], seg_peer(1))])
    half_in_moves = Group(
        half_seg.at[pl.ds(0, 3), pl.ds(0, 2)],
        [
            (half_in.at[seat_of(d), pl.ds(0, 2)], half_seg.at[t, pl.ds(0, 2)], seg_peer(d))
            for d in (2, 3, 1)
        ],
    )
    half_value_moves = Group(
        half_seg.at[pl.ds(0, 3), 2],
        [(half_in.at[seat_of(d), 2], half_seg.at[t, 2], seg_peer(d)) for d in (2, 3, 1)],
    )
    half_seg[t] = half_in[t]
    full_seg[t] = full_in[t]

    notes.arrive()
    for mm in range(16):
        w_full[x, y, 3 * mm:3 * mm + 3, :] = note_got[mm, 0:3, :]
        w_mid[x, y, 3 * mm:3 * mm + 3, :] = note_got[mm, 3:6, :]
        for h in range(HEADS_HERE):
            far[y, h, 2 * mm:2 * mm + 2, :] = note_got[mm, 6 + 2 * h:8 + 2 * h, :]
    w_first = Group(
        w_full.at[pl.ds(0, 2), pl.ds(0, 3)],
        [(w_full.at[x, y], w_full.at[x, y], y_peer(j)) for j in (2, 1, 3)]
        + [(w_mid.at[x, y], w_mid.at[x, y], x_peer(j)) for j in (2, 1, 3)],
    )
    far_moves = Group(
        far.at[pl.ds(0, 3)], [(far.at[y], far.at[y], y_peer(j)) for j in (2, 1, 3)]
    )
    w_first.arrive()
    w_full_moves = Group(
        w_full.at[pl.ds(0, 3)], [(w_full.at[x], w_full.at[x], x_peer(j)) for j in (2, 1, 3)]
    )
    w_mid_moves = Group(
        w_mid.at[pl.ds(0, 3)], [(w_mid.at[:, y], w_mid.at[:, y], y_peer(j)) for j in (2, 1, 3)]
    )
    far_moves.arrive()

    def as_keys(h, rows, block, upper, four, transposed):
        high, low = split(block)
        four[h, rows, 0:128] = twice(high, upper).astype(BF16)
        four[h, rows, 128:256] = twice(low, upper).astype(BF16)
        transposed[h, :, rows] = pair(block, upper).T.astype(BF16)

    for h in range(HEADS_HERE):
        block = far[:, h].reshape(FAR, 128)
        as_keys(h, slice(SEG, KEYS), block, False, k4, kt)
        as_keys(h, slice(SEG, KEYS), block, True, v4, vt)

    valid = valid_ref[0]
    tile_row = lax.broadcasted_iota(jnp.int32, (ROWS, WIDTH), 0)

    def take_grad(seat):
        rows = pl.ds(pl.multiple_of(seat * ROWS, ROWS), ROWS)
        grad = jnp.where(seg * SEG + seat * ROWS + tile_row < valid, g_seg[seat], 0.0)
        high = grad.astype(BF16)
        g_hi[rows, :] = high
        g_lo[rows, :] = (grad - high.astype(F32)).astype(BF16)

    take_grad(t)
    g_beside.arrive()
    take_grad(seat_of(1))
    g_forwarded = Group(g_seg.at[0])
    for n in range(G_CHUNKS):
        g_across[n].arrive()
        part = g_part(seat_of(2), n)
        g_forwarded.add([(part, part, seg_peer(1))])
    take_grad(seat_of(2))

    g_forwarded.arrive()
    take_grad(seat_of(3))
    def as_queries(h, rows, block, upper):
        both = pair(block * 0.125, upper).astype(BF16)
        q4[h, rows, 0:128] = both
        q4[h, rows, 128:256] = both

    key_row = lax.broadcasted_iota(jnp.int32, (128, 256), 0)
    query_lane = lax.broadcasted_iota(jnp.int32, (128, 256), 1)

    def weights(h):
        head = 6 * hz + jnp.where(h == 2, 2 + c, 4 * c + h)
        offset = offset_ref[head]
        for qb in range(2):
            lanes = slice(qb * 256, (qb + 1) * 256)
            queries = q4[h, lanes, :]
            top = None
            for kb in range(5):
                rows = slice(kb * 128, (kb + 1) * 128)
                scores = dot_nt(k4[h, rows, :], queries)
                if kb < 4:
                    keep = (seg * SEG + kb * 128 + key_row < valid) | (
                        kb * 128 + key_row == qb * 256 + query_lane
                    )
                else:
                    keep = (key_row * SPACING + offset < valid) & (
                        lax.rem(query_lane, SPACING) == offset
                    )
                scores = jnp.where(keep, scores, MASKED)
                prob[h, rows, lanes] = scores
                here = jnp.max(scores, axis=0, keepdims=True)
                top = here if top is None else jnp.maximum(top, here)
            total = None
            for kb in range(5):
                rows = slice(kb * 128, (kb + 1) * 128)
                weight = jnp.exp(prob[h, rows, lanes] - top)
                prob[h, rows, lanes] = weight
                here = jnp.sum(weight, axis=0, keepdims=True)
                total = here if total is None else total + here
            scale = 1.0 / total
            for kb in range(5):
                rows = slice(kb * 128, (kb + 1) * 128)
                p = prob[h, rows, lanes] * scale
                prob[h, rows, lanes] = p
                high = p.astype(BF16)
                prob_hi[h, rows, lanes] = high
                prob_lo[h, rows, lanes] = (p - high.astype(F32)).astype(BF16)

    def attention(h):
        for qb in range(2):
            lanes = slice(qb * 256, (qb + 1) * 256)
            out = dot(vt[h], prob_hi[h, :, lanes]) + dot(vt[h], prob_lo[h, :, lanes])
            attn_t[h, :, lanes] = out[0:64] + out[64:128]

    def value_grad(h):
        grads = do4[h, :, 0:128]
        return fold_halves(dot(prob_hi[h], grads) + dot(prob_lo[h], grads))

    def key_grad(h):
        queries = q4[h, :, 0:128]
        return fold_halves(dot(ds_hi[h], queries) + dot(ds_lo[h], queries))

    def score_grad(h):
        for qb in range(2):
            lanes = slice(qb * 256, (qb + 1) * 256)
            delta = jnp.sum(attn_t[h, :, lanes] * do_t[h, :, lanes], axis=0, keepdims=True)
            for kb in range(5):
                rows = slice(kb * 128, (kb + 1) * 128)
                d_prob = dot_nt(v4[h, rows, :], do4[h, lanes, :])
                ds = prob[h, rows, lanes] * (d_prob - delta)
                high = ds.astype(BF16)
                ds_hi[h, rows, lanes] = high
                ds_lo[h, rows, lanes] = (ds - high.astype(F32)).astype(BF16)

    def query_grad(h):
        turned = dot(kt[h], ds_hi[h]) + dot(kt[h], ds_lo[h])
        dq_t[h] = (turned[0:64] + turned[64:128]) * 0.125

    def weight_grad(attn):
        high = attn.astype(BF16)
        low = (attn - high.astype(F32)).astype(BF16)
        return dot(high, g_hi[...]) + dot(low, g_hi[...]) + dot(high, g_lo[...])

    def far_grad(h, d_key, d_value):
        d_key, d_value = d_key[SEG:KEYS], d_value[SEG:KEYS]
        block = jnp.where(low_lanes(d_key), d_key, d_value)
        far_part[:, h] = block.reshape(4, 32, 128)

    def sum_first(parts, got):
        return Group(
            got,
            [(parts.at[0, x_place(j)], got.at[0, j - 1], x_peer(j)) for j in (2, 1, 3)]
            + [(parts.at[1, :, y_place(j)], got.at[1, j - 1], y_peer(j)) for j in (2, 1, 3)],
        )

    def sum_second(parts, got, sums, got_next):
        sums[0] = parts[0, x] + got[0, 0] + got[0, 1] + got[0, 2]
        sums[1] = parts[1, :, y] + got[1, 0] + got[1, 1] + got[1, 2]
        return Group(
            got_next,
            [(sums.at[0, y_place(j)], got_next.at[0, j - 1], y_peer(j)) for j in (2, 1, 3)]
            + [(sums.at[1, x_place(j)], got_next.at[1, j - 1], x_peer(j)) for j in (2, 1, 3)],
        )

    def sum_last(sums, got_next):
        return (
            sums[0, y] + got_next[0, 0] + got_next[0, 1] + got_next[0, 2],
            sums[1, x] + got_next[1, 0] + got_next[1, 1] + got_next[1, 2],
        )

    for group in [notes, w_first, far_moves, g_beside] + g_across:
        group.sent()
    full_in_moves.arrive()
    for tt in range(SEATS):
        rows = slice(tt * 128, (tt + 1) * 128)
        for h in range(2):
            as_queries(h, rows, full_seg[tt, 0], h == 1)
            as_keys(h, rows, full_seg[tt, 1], h == 1, k4, kt)
    weights(0)
    weights(1)
    value_in_moves.arrive()
    for tt in range(SEATS):
        rows = slice(tt * 128, (tt + 1) * 128)
        for h in range(2):
            as_keys(h, rows, full_seg[tt, 2], h == 1, v4, vt)
    attention(0)
    attention(1)
    turned = weight_grad(attn_t[0:2].reshape(128, SEG))
    for xx in range(X):
        block = turned[:, xx * 192:(xx + 1) * 192].T
        for yy in range(4):
            for n in range(2):
                wg_full[n, xx, yy] = block[yy * 48 + n * 24:yy * 48 + n * 24 + 24]
    wg_first = sum_first(wg_full, wg_full_1)

    w_full_moves.arrive()
    w_mid_moves.arrive()
    for tile, ref in ((0, w_full), (1, w_mid)):
        columns = ref[...].reshape(WIDTH, 128)
        if tile == 1:
            columns = jnp.where(c == 1, flip(columns), columns)
        high = columns.astype(BF16)
        w_hi[:, lanes_of(tile)] = high
        w_lo[:, lanes_of(tile)] = (columns - high.astype(F32)).astype(BF16)

    for tt in range(SEATS):
        rows = slice(tt * 128, (tt + 1) * 128)
        high, low = g_hi[rows, :], g_lo[rows, :]
        out = dot(high, w_hi[...]) + dot(low, w_hi[...]) + dot(high, w_lo[...])
        full, middle = out[:, 0:128], out[:, 128:256]
        for h, block, upper in ((0, full, False), (1, full, True), (2, middle, False)):
            both = pair(block, upper).astype(BF16)
            do4[h, rows, 0:128] = both
            do4[h, rows, 128:256] = both
        turned = full.T
        do_t[0, :, rows] = turned[0:64]
        do_t[1, :, rows] = turned[64:128]
        do_t[2, :, rows] = middle.T[0:64]

    full_out = Group(full_got.at[pl.ds(0, 3)])
    own_out = []

    def keep_own(src, dst):
        copy = pltpu.make_async_copy(src, dst, local_sem.at[5 + len(own_out)])
        copy.start()
        own_out.append(copy)

    def send_full(n):
        full_out.add(
            (full_send.at[seat_of(d), n], full_got.at[t, n], seg_peer(d)) for d in (2, 3, 1)
        )
        keep_own(full_send.at[t, n], full_got.at[t, n])

    def both_heads(low, high, n):
        block = jnp.where(low_lanes(low), low, high)
        for tt in range(SEATS):
            full_send[tt, n] = block[tt * 128:(tt + 1) * 128]
        send_full(n)

    values_0, values_1 = value_grad(0), value_grad(1)
    both_heads(values_0, values_1, 2)

    half_in_moves.arrive()
    for tt in range(SEATS):
        rows = slice(tt * 128, (tt + 1) * 128)
        as_queries(2, rows, unfold(half_seg[tt, 0]), False)
        as_keys(2, rows, unfold(half_seg[tt, 1]), False, k4, kt)
    weights(2)
    half_value_moves.arrive()
    for tt in range(SEATS):
        rows = slice(tt * 128, (tt + 1) * 128)
        as_keys(2, rows, unfold(half_seg[tt, 2]), False, v4, vt)
    attention(2)
    turned = weight_grad(attn_t[2])
    turned = jnp.concatenate([turned, turned], axis=0)
    for xx in range(X):
        block = turned[:, xx * 192:(xx + 1) * 192].T
        for yy in range(4):
            top, bottom = block[yy * 48:yy * 48 + 24], block[yy * 48 + 24:yy * 48 + 48]
            packed = jnp.where(low_lanes(top), top, bottom)
            wg_mid[0, xx, yy] = packed[0:12]
            wg_mid[1, xx, yy] = packed[12:24]

    mid_first = sum_first(wg_mid, wg_mid_1)

    score_grad(0)
    score_grad(1)
    keys_0, keys_1 = key_grad(0), key_grad(1)
    both_heads(keys_0, keys_1, 1)
    wg_first.arrive()
    wg_second = sum_second(wg_full, wg_full_1, wg_full_sum, wg_full_2)
    far_grad(0, keys_0, values_0)
    far_grad(1, keys_1, values_1)
    far_out = Group(
        far_got,
        [
            (far_part.at[y_place(j), pl.ds(0, 2)], far_got.at[j - 1, pl.ds(0, 2)], y_peer(j))
            for j in (2, 1, 3)
        ],
    )
    query_grad(0)
    query_grad(1)
    for tt in range(SEATS):
        full_send[tt, 0] = dq_t[0:2, :, tt * 128:(tt + 1) * 128].reshape(128, 128).T
    send_full(0)
    d_value = value_grad(2)
    score_grad(2)
    d_key = key_grad(2)
    far_grad(2, d_key, d_value)
    far_out.add(
        (far_part.at[y_place(j), pl.ds(2, 1)], far_got.at[j - 1, pl.ds(2, 1)], y_peer(j))
        for j in (2, 1, 3)
    )
    for tt in range(SEATS):
        for n, part in ((1, d_key), (2, d_value)):
            top, bottom = part[tt * 128:tt * 128 + 64], part[tt * 128 + 64:tt * 128 + 128]
            half_send[tt, n] = jnp.where(low_lanes(top), top, bottom)
    half_out = Group(
        half_got.at[pl.ds(0, 3)],
        [
            (half_send.at[seat_of(d), pl.ds(1, 2)], half_got.at[t, pl.ds(1, 2)], seg_peer(d))
            for d in (2, 3, 1)
        ],
    )
    mid_first.arrive()
    mid_second = sum_second(wg_mid, wg_mid_1, wg_mid_sum, wg_mid_2)
    query_grad(2)
    for tt in range(SEATS):
        block = dq_t[2, :, tt * 128:(tt + 1) * 128]
        block = jnp.concatenate([block, block], axis=0).T
        half_send[tt, 0] = jnp.where(low_lanes(block[0:64]), block[0:64], block[64:128])

    def to_owners(notes, got):
        return Group(
            got.at[pl.ds(0, 15)],
            [(notes.at[ring_place(j)], got.at[m], ring_peer(j)) for j in FAR_FIRST],
        )

    wg_second.arrive()
    parts = sum_last(wg_full_sum, wg_full_2)
    for mm in range(16):
        last[mm, 0:3, :] = parts[mm // 8][3 * (mm % 8):3 * (mm % 8) + 3]
    far_out.arrive()
    for h in range(HEADS_HERE):
        rows = far_part[y, h] + far_got[0, h] + far_got[1, h] + far_got[2, h]
        for mm in range(16):
            last[mm, 6 + 2 * h:8 + 2 * h, :] = rows[2 * mm:2 * mm + 2]
    mid_second.arrive()
    parts = sum_last(wg_mid_sum, wg_mid_2)
    for mm in range(16):
        rows = parts[mm // 4 % 2]
        last[mm, 3:6, :] = (rows if mm < 8 else flip(rows))[3 * (mm % 4):3 * (mm % 4) + 3]
    last_moves = to_owners(last, last_got)
    half_out.add((half_send.at[seat_of(d), 0], half_got.at[t, 0], seg_peer(d)) for d in (2, 3, 1))
    keep_own(half_send.at[t], half_got.at[t])
    keep_own(last.at[m], last_got.at[m])

    for group in (
        w_full_moves, w_mid_moves, g_forwarded, full_in_moves, value_in_moves, half_in_moves,
        half_value_moves, wg_first, mid_first, wg_second, far_out, mid_second, full_out,
    ):
        group.sent()
    full_out.arrive()
    for copy in own_out:
        copy.wait()
    for group in (last_moves, half_out):
        group.sent()
        group.arrive()


def put_together(
    full_got, half_got, last_got, offset_ref, dq_out, dk_out, dv_out, wg_out,
    dq_own, dk_own, dv_own, wg_own, out_sem,
):
    stores = [
        pltpu.make_async_copy(src, dst, out_sem.at[n])
        for n, (src, dst) in enumerate(
            ((dq_own, dq_out), (dk_own, dk_out), (dv_own, dv_out), (wg_own, wg_out))
        )
    ]
    row64 = lax.broadcasted_iota(jnp.int32, (64, 128), 0)
    low64 = lax.broadcasted_iota(jnp.int32, (64, 128), 1) < 64
    outs = (dq_own, dk_own, dv_own)
    notes = [
        last_got[tt] + last_got[4 + tt] + last_got[8 + tt] + last_got[12 + tt]
        for tt in range(SEATS)
    ]

    def with_extra(n, r, tt, h, upper, block):
        if n == 0:
            return block
        row = notes[tt][6 + 2 * h + r:7 + 2 * h + r]
        if (n == 2) != upper:
            row = flip(row)
        keep = (row64 == offset_ref[head_of(tt, h)]) & (low64 != upper)
        return block + jnp.where(keep, jnp.broadcast_to(row, (64, 128)), 0.0)

    for n in range(3):
        for half in range(2):
            even, odd = half_got[2 * half, n], half_got[2 * half + 1, n]
            for r in range(2):
                if r == 0:
                    block = jnp.where(low64, even, flip(odd))
                else:
                    block = jnp.where(low64, flip(even), odd)
                block = with_extra(n, r, 2 * half, 2, False, block)
                block = with_extra(n, r, 2 * half + 1, 2, True, block)
                outs[n][r * 64:(r + 1) * 64, lanes_of(3 * half + 1)] = block
        for tt in range(SEATS):
            for r in range(2):
                block = full_got[tt, n, r * 64:(r + 1) * 64, :]
                block = with_extra(n, r, tt, 0, False, block)
                block = with_extra(n, r, tt, 1, True, block)
                outs[n][r * 64:(r + 1) * 64, lanes_of(full_tile(tt))] = block
        stores[n].start()

    scale = 8192.0 ** -0.5
    for tt in range(SEATS):
        wg_own[:, lanes_of(full_tile(tt))] = notes[tt][0:3] * scale
    for half in range(2):
        even, odd = notes[2 * half][3:6], notes[2 * half + 1][3:6]
        wg_own[:, lanes_of(3 * half + 1)] = jnp.where(low_lanes(even), even, flip(odd)) * scale
    stores[3].start()
    for copy in stores:
        copy.wait()


def on_device(queries, keys, values, out_grad, out_weight, valid_tiles, head_offsets):
    def block(*shape):
        return pltpu.VMEM(shape, F32)

    def half(*shape):
        return pltpu.VMEM(shape, BF16)

    scratch = [
        block(ROWS, WIDTH), block(ROWS, WIDTH), block(ROWS, WIDTH), block(3, WIDTH),
        block(4, 3, 64, 128), block(4, 3, 64, 128), block(4, 3, 128, 128), block(4, 3, 128, 128),
        block(4, ROWS, WIDTH),
        block(4, 12, 128), block(16, 12, 128),
        block(4, 4, 48, 128), block(4, 4, 48, 128), half(WIDTH, 256), half(WIDTH, 256),
        block(4, 3, 32, 128),
        half(3, SEG, 256), half(3, KEYS, 256), half(3, KEYS, 256),
        half(3, 128, KEYS), half(3, 128, KEYS),
        half(3, SEG, 256), block(3, 64, SEG), block(3, 64, SEG),
        block(3, KEYS, SEG), half(3, KEYS, SEG), half(3, KEYS, SEG),
        half(3, KEYS, SEG), half(3, KEYS, SEG),
        half(SEG, WIDTH), half(SEG, WIDTH),
        block(4, 3, 32, 128), block(3, 3, 32, 128),
        block(2, 4, 4, 24, 128), block(2, 3, 4, 24, 128), block(2, 4, 24, 128), block(2, 3, 24, 128),
        block(2, 4, 4, 12, 128), block(2, 3, 4, 12, 128), block(2, 4, 12, 128), block(2, 3, 12, 128),
        block(16, 12, 128), block(3, 64, SEG),
        block(4, 3, 128, 128), block(4, 3, 64, 128),
        pltpu.SemaphoreType.DMA((SENDS,)), pltpu.SemaphoreType.DMA((SENDS,)),
        pltpu.SemaphoreType.DMA((11,)),
    ]
    whole = pl.BlockSpec(memory_space=pltpu.HBM)
    scalars = pl.BlockSpec(memory_space=pltpu.SMEM)
    rows = jax.ShapeDtypeStruct((ROWS, WIDTH), F32)
    blocks = [
        pltpu.with_memory_space_constraint(array, pltpu.HBM)
        for array in (queries[0], keys[0], values[0], out_grad[0], out_weight)
    ]
    head_offsets = pltpu.with_memory_space_constraint(head_offsets, pltpu.HBM)
    got = pl.pallas_call(
        kernel,
        out_shape=(
            jax.ShapeDtypeStruct((4, 3, 128, 128), F32),
            jax.ShapeDtypeStruct((4, 3, 64, 128), F32),
            jax.ShapeDtypeStruct((16, 12, 128), F32),
        ),
        in_specs=[whole] * 5 + [scalars] * 2,
        out_specs=(whole,) * 3,
        scratch_shapes=scratch,
        compiler_params=pltpu.CompilerParams(
            collective_id=0, has_side_effects=True, vmem_limit_bytes=48 * 1024 * 1024
        ),
        cost_estimate=pl.CostEstimate(
            flops=4_000_000_000, bytes_accessed=4_000_000, transcendentals=1_000_000
        ),
        name="dilated_backward",
    )(*blocks, valid_tiles, head_offsets)
    d_query, d_key, d_value, d_weight = pl.pallas_call(
        put_together,
        out_shape=(rows, rows, rows, jax.ShapeDtypeStruct((3, WIDTH), F32)),
        in_specs=[pl.BlockSpec(memory_space=pltpu.VMEM)] * 3 + [scalars],
        out_specs=(whole,) * 4,
        scratch_shapes=[
            block(ROWS, WIDTH), block(ROWS, WIDTH), block(ROWS, WIDTH), block(3, WIDTH),
            pltpu.SemaphoreType.DMA((4,)),
        ],
        compiler_params=pltpu.CompilerParams(vmem_limit_bytes=16 * 1024 * 1024),
        cost_estimate=pl.CostEstimate(flops=1_000_000, bytes_accessed=2_500_000, transcendentals=0),
        name="put_together",
    )(*got, head_offsets)
    return d_query[None], d_key[None], d_value[None], d_weight


def solution(mesh):
    from jax.sharding import PartitionSpec as P

    tiles = P("dp", "seq", None)
    weight = P(("dp", "seq"), None)
    return jax.shard_map(
        on_device,
        mesh=mesh,
        in_specs=(tiles, tiles, tiles, tiles, weight, P("dp"), P()),
        out_specs=(tiles, tiles, tiles, weight),
        check_vma=False,
    )
```
